128 devices in a mesh: node: 32 (over x, y_lo, z), local: 4 (over y_hi, core).
Axes of the slice: x: 4, y: 4 (y_hi: 2, y_lo: 2; y = y_hi * 2 + y_lo), z: 4, core: 2. Of those that a mesh axis runs over, the one named last changes fastest.
Arguments:
- images: bfloat16 [512, 14, 14, 1024], P(('node', 'local')), may hold values from -6 to 6
- labels: int32 [512], P(('node', 'local')), may hold values from 0 to 999
- params: float32 [32, 2141184], P('node', 'local'), as said below
- momentum: float32 [32, 2141184], P('node', 'local'), as said below
- step: int32 [1], replicated, may hold values from 0 to 999
Outputs:
- new_params: float32 [32, 2141184], P('node', 'local')
- new_momentum: float32 [32, 2141184], P('node', 'local')
The draws below stay inside these ranges and needn't reach their ends.
Inputs may be any that keep to these rules, and one draw needn't show every extreme that they name: `params`: weights drawn with standard deviation fan_in ** -0.5, gains between 0.5 and 1.5, biases of deviation 0.2. `momentum`: entries of the order of a running average of gradients of this loss.
All inputs are finite; a program needn't handle non-finite values.
Results may differ from the reference program's by a relative error of at most 0.012.
Values may be sent and summed in bfloat16 or wider, within the bound.
No kernel may reach another device: no remote copies, remote signals or barrier semaphores. Data moves between devices by JAX's collectives and lax.ppermute only.
A program may use at most 128 MiB of HBM per device.

```python
import math
import jax
import jax.numpy as jnp
from jax import lax

C_IN = 1024
C_MID = 256
CLASSES = 1000
SIDE = 14
IMG = 4
NODES = 32
IMAGES = 512
P_SIZE = 2141184


def draw_params(key, part):
    keys = jax.random.split(jax.random.fold_in(key, 17), 10)
    shapes = [(C_IN * C_MID, C_IN), (9 * C_MID * C_MID, 9 * C_MID), (C_MID * C_IN, C_MID), (C_IN * CLASSES, C_IN)]
    pieces = []
    for position in range(4):
        length, fan = shapes[position]
        pieces.append(jax.random.normal(keys[position], (NODES, length), jnp.float32) * fan ** (-0.5))
    widths = [C_MID, C_MID, C_IN]
    for position in range(3):
        pieces.append(jax.random.uniform(keys[4 + 2 * position], (NODES, widths[position]), jnp.float32, 0.5, 1.5))
        pieces.append(jax.random.normal(keys[5 + 2 * position], (NODES, widths[position]), jnp.float32) * 0.2)
    return jnp.concatenate(pieces, axis=1).astype(jnp.float32)


def draw_momentum(key, part):
    keys = jax.random.split(jax.random.fold_in(key, 29), 10)
    node_images = IMAGES // NODES
    base = 1.2 / math.sqrt(node_images)
    lengths = [C_IN * C_MID, 9 * C_MID * C_MID, C_MID * C_IN, C_IN * CLASSES, C_MID, C_MID, C_MID, C_MID, C_IN, C_IN]
    scales = [0.5 * base / math.sqrt(C_IN), 0.5 * base / math.sqrt(C_IN), 0.5 * base / math.sqrt(C_IN), base / math.sqrt(CLASSES), base / math.sqrt(C_MID), base / math.sqrt(C_MID), base / math.sqrt(C_MID), base / math.sqrt(C_MID), base / math.sqrt(C_IN), base / math.sqrt(C_IN)]
    pieces = []
    for position in range(10):
        values = jnp.clip(jax.random.normal(keys[position], (NODES, lengths[position]), jnp.float32), -6.0, 6.0)
        pieces.append(values * scales[position])
    return jnp.concatenate(pieces, axis=1).astype(jnp.float32)


def set_ends(values, stream_key, smallest, largest):
    extent = values.shape
    index_at = [jax.random.randint(jax.random.fold_in(stream_key, axis), (), 0, extent[axis]) for axis in range(len(extent))]
    values = values.at[tuple(index_at)].set(smallest)
    longest = extent.index(max(extent))
    index_at[longest] = (index_at[longest] + 1) % extent[longest]
    return values.at[tuple(index_at)].set(largest)


def level_of(key, extent, shards, low, high):
    factor_of, own = 1.0, jax.random.fold_in(key, 6)
    for dim, parts in shards:
        heights = jnp.exp(jax.random.uniform(jax.random.fold_in(own, dim), (parts,), jnp.float32, low / len(shards), high / len(shards)))
        factor_of = factor_of * jnp.repeat(heights, extent[dim] // parts).reshape([-1 if axis == dim else 1 for axis in range(len(extent))])
    return factor_of


def gaussian(key, extent, scale, bound, cuts=(), kind=jnp.bfloat16):
    values = jax.random.normal(key, extent, jnp.float32) * scale
    if len(cuts) > 0:
        values = level_of(key, extent, cuts, -0.22, 0.18) * values
    return jnp.clip(values, min=-bound, max=bound).astype(kind)


def setup_inputs(seed: int = 0) -> dict:
    splits = jax.random.split(jax.random.key(seed), 6)
    return {
        "images": gaussian(splits[0], (IMAGES, SIDE, SIDE, C_IN), 1.0, 6.0, ((0, 128),)),
        "labels": set_ends(jax.random.randint(splits[1], (IMAGES,), 0, CLASSES), jax.random.fold_in(splits[1], 1), 0, CLASSES - 1).astype(jnp.int32),
        "params": draw_params(jax.random.fold_in(splits[5], 71), 0),
        "momentum": draw_momentum(jax.random.fold_in(splits[5], 71), 0),
        "step": jax.random.randint(splits[4], (1,), 0, 1000).astype(jnp.int32),
    }


EPS = 1e-05
MOMENTUM_RATE = 0.9
LEARN_RATE = 0.1

def unpack(flat_weights):
    lengths = [C_IN * C_MID, 9 * C_MID * C_MID, C_MID * C_IN, C_IN * CLASSES, C_MID, C_MID, C_MID, C_MID, C_IN, C_IN]
    pieces = []
    offset = 0
    for length in lengths:
        pieces.append(flat_weights[offset:offset + length])
        offset = offset + length
    w_reduce = pieces[0].reshape(C_IN, C_MID)
    w_spatial = pieces[1].reshape(3, 3, C_MID, C_MID)
    w_expand = pieces[2].reshape(C_MID, C_IN)
    w_classify = pieces[3].reshape(C_IN, CLASSES)
    return (w_reduce, w_spatial, w_expand, w_classify, pieces[4:])

def normalize(values, gain, bias_term):
    average = lax.optimization_barrier(jnp.mean(values, 0))
    centred = values - average
    spread = lax.optimization_barrier(jnp.mean(centred * centred, 0))
    return centred * lax.rsqrt(spread + EPS) * gain.astype(jnp.float32) + bias_term.astype(jnp.float32)

def local_loss(flat_weights, images, labels):
    w_reduce, w_spatial, w_expand, w_classify, norms = unpack(flat_weights)
    count = images.shape[0]
    side = images.shape[1]
    rows_in = images.reshape(count * side * side, C_IN)
    first = jnp.maximum(normalize(jnp.dot(rows_in, w_reduce, preferred_element_type=jnp.float32), norms[0], norms[1]), 0.0).astype(jnp.bfloat16)
    spatial = lax.conv_general_dilated(first.reshape(count, side, side, C_MID), w_spatial, (1, 1), 'SAME', dimension_numbers=('NHWC', 'HWIO', 'NHWC'), preferred_element_type=jnp.float32)
    second = jnp.maximum(normalize(spatial.reshape(count * side * side, C_MID), norms[2], norms[3]), 0.0).astype(jnp.bfloat16)
    third = normalize(jnp.dot(second, w_expand, preferred_element_type=jnp.float32), norms[4], norms[5])
    output_rows = jnp.maximum(third + rows_in.astype(jnp.float32), 0.0)
    pooled = lax.optimization_barrier(jnp.mean(output_rows.reshape(count, side * side, C_IN), 1)).astype(jnp.bfloat16)
    logits = jnp.dot(pooled, w_classify, preferred_element_type=jnp.float32)
    classes = jnp.arange(CLASSES).astype(jnp.int32)
    picked = lax.optimization_barrier(jnp.sum(jnp.where(labels[:, None] == classes[None, :], logits, 0.0), 1))
    return jnp.sum(jnp.log(lax.optimization_barrier(jnp.sum(jnp.exp(logits), 1))) - picked) / count

def device_grads(whole, images, labels):
    total_loss, pullback = jax.vjp(lambda weights: local_loss(weights, images, labels), whole)
    grads, = pullback(jnp.ones((), jnp.float32))
    return grads

def reference(images, labels, params, momentum, step):
    locals_count = IMAGES // (IMG * NODES)
    grouped = images.reshape(NODES, locals_count, IMG, SIDE, SIDE, C_IN)
    grouped_labels = labels.reshape(NODES, locals_count, IMG)

    def one_owner(owner):
        whole = params[owner].astype(jnp.bfloat16)
        summed = jnp.zeros((P_SIZE,), jnp.float32)
        for member in range(locals_count):
            summed = summed + device_grads(whole, grouped[owner, member], grouped_labels[owner, member]).astype(jnp.float32)
        return summed / locals_count
    grad = lax.map(one_owner, jnp.arange(NODES).astype(jnp.int32))
    moved_m = MOMENTUM_RATE * momentum + grad
    moved_p = params - LEARN_RATE * moved_m
    degrees = NODES.bit_length() - 1
    distance = jnp.left_shift(jnp.int32(1), step[0] % degrees)
    new_params = 0.5 * (moved_p + jnp.roll(moved_p, distance, axis=0))
    new_momentum = 0.5 * (moved_m + jnp.roll(moved_m, distance, axis=0))
    return (new_params, new_momentum)
```

```python
import functools

import jax
import jax.numpy as jnp
from jax import lax
from jax.experimental import pallas as pl
from jax.experimental.pallas import tpu as pltpu
from jax.sharding import PartitionSpec as P

F32 = jnp.float32
BF = jnp.bfloat16

CLASSES = 1000
EPS = 1e-05
MOMENTUM_RATE = 0.9
LEARN_RATE = 0.1

LROWS = 4182
GROWS = 4192
OFF = 96
PIX = 784.0

ROWS = 896
LINE = 64
VALID = 56
STEPS = 7

WINDOWS = []
for _j in range(16):
    _first = (CLASSES * _j) // 128
    _last = (CLASSES * _j + CLASSES - 1) // 128
    WINDOWS.append((_first, _last + 1, CLASSES * _j - 128 * _first))

VMEM_LIMIT = 48 * 1024 * 1024

ANY = pl.BlockSpec(memory_space=pl.ANY)
VM = pl.BlockSpec(memory_space=pltpu.VMEM)
SM = pl.BlockSpec(memory_space=pltpu.SMEM)


def shape(dims, dtype):
    return jax.ShapeDtypeStruct(dims, dtype)


def call(kernel, name, in_specs, out_shape, scratch, flops, moved, out_specs=None):
    extra = {} if out_specs is None else {"out_specs": out_specs}
    return pl.pallas_call(
        kernel,
        name=name,
        in_specs=in_specs,
        out_shape=out_shape,
        scratch_shapes=scratch,
        compiler_params=pltpu.CompilerParams(vmem_limit_bytes=VMEM_LIMIT),
        cost_estimate=pl.CostEstimate(flops=flops, bytes_accessed=moved, transcendentals=0),
        **extra,
    )


def at(step, size=128):
    return pl.ds(pl.multiple_of(step * size, size), size)


def dot(a, b):
    return jnp.dot(a, b, preferred_element_type=F32)


def dot_nt(a, b):
    return lax.dot_general(a, b, (((1,), (1,)), ((), ())), preferred_element_type=F32)


def fold(values):
    rows, lanes = values.shape
    return jnp.sum(values.reshape(rows // 8, 8, lanes), axis=0)


def total(folded):
    return jnp.sum(folded, axis=0, keepdims=True)


def row_mask(lanes):
    rows = lax.broadcasted_iota(jnp.int32, (128, lanes), 0)
    return jnp.where(lax.rem(rows, LINE) < VALID, 1.0, 0.0).astype(F32)


def slope(values):
    return jnp.where(values > 0.0, 1.0, jnp.where(values == 0.0, 0.5, 0.0))


def vector(norms, row, count):
    return jnp.concatenate([norms[row + i : row + i + 1, :] for i in range(count)], axis=1)


def choose(own, wanted, candidates, place, sem):
    for distance in range(4):

        @pl.when(lax.bitwise_xor(own, wanted) == distance)
        def _(source=candidates[distance]):
            pltpu.make_async_copy(source, place, sem).start()


def landed(candidates, place, sem):
    pltpu.make_async_copy(candidates[0], place, sem).wait()


def load_flat(flat, buf, sem):
    copy = pltpu.make_async_copy(flat.reshape(LROWS, 128), buf.at[pl.ds(OFF, LROWS)], sem)
    copy.start()
    buf[0:OFF, :] = jnp.zeros((OFF, 128), F32)
    end = OFF + LROWS
    buf[end : buf.shape[0], :] = jnp.zeros((buf.shape[0] - end, 128), F32)
    copy.wait()


def class_tiles(buf, out, start):
    for r in range(125):
        out[16 * r : 16 * r + 16, :] = buf[pl.ds(start + r, 16, stride=125), :].astype(BF)


def prepare_a(role, flat, out, buf, sem):
    load_flat(flat, buf, sem)
    own = role[0]

    @pl.when(own == 0)
    def _():
        for t in range(2):
            out[1024 * t : 1024 * t + 1024, :] = buf[pl.ds(OFF + t, 1024, stride=2), :].astype(BF)

    @pl.when(own == 1)
    def _():
        out[0:1280, :] = buf[pl.ds(10, 1280, stride=2), :].astype(BF)
        out[1280:2048, :] = buf[pl.ds(11, 768, stride=2), :].astype(BF)

    @pl.when(own == 2)
    def _():
        class_tiles(buf, out, 436)
        out[2000:2048, :] = jnp.zeros((48, 128), BF)

    @pl.when(own == 3)
    def _():
        class_tiles(buf, out, 254)
        out[2000:2048, :] = jnp.zeros((48, 128), BF)


def prepare_b(role, flat, spill, out, small, buf, sem):
    load_flat(flat, buf, sem)
    own = role[0]

    @pl.when(own == 0)
    def _():
        for t in range(2):
            out[1280 * t : 1280 * t + 1280, :] = buf[
                pl.ds(OFF + 2048 + t, 1280, stride=2), :
            ].astype(BF)

    @pl.when(own == 1)
    def _():
        out[0:512, :] = buf[pl.ds(11 + 2 * 768, 512, stride=2), :].astype(BF)
        for j in range(8):
            out[512 + 256 * j : 768 + 256 * j, :] = buf[
                pl.ds(OFF + 2474 + j, 256, stride=8), :
            ].astype(BF)

    @pl.when(own == 2)
    def _():
        for j in range(8):
            small[48 * j : 48 * j + 48, :] = buf[pl.ds(52 + j, 48, stride=8), :].astype(BF)
        buf[OFF + LROWS : OFF + LROWS + 160, :] = spill[...]
        class_tiles(buf, out, 436 + 16 * 125)
        out[2000:2560, :] = jnp.zeros((560, 128), BF)

    @pl.when(own == 3)
    def _():
        small[0:32, :] = buf[OFF + 4158 : OFF + 4190, :].astype(BF)
        small[32:384, :] = jnp.zeros((352, 128), BF)
        class_tiles(buf, out, 254 + 16 * 125)
        out[2000:2560, :] = jnp.zeros((560, 128), BF)

    @pl.when(own < 2)
    def _():
        small[...] = jnp.zeros((384, 128), BF)


def prepare_gossip(flat_p, flat_m, out_p, out_m, buf_p, buf_m, sems):
    copies = [
        pltpu.make_async_copy(flat_p.reshape(LROWS, 128), buf_p.at[pl.ds(0, LROWS)], sems.at[0]),
        pltpu.make_async_copy(flat_m.reshape(LROWS, 128), buf_m.at[pl.ds(0, LROWS)], sems.at[1]),
    ]
    for copy in copies:
        copy.start()
    for copy in copies:
        copy.wait()
    for buf in (buf_p, buf_m):
        buf[LROWS:GROWS, :] = jnp.zeros((GROWS - LROWS, 128), F32)

    def piece(where):
        decayed = MOMENTUM_RATE * buf_m[where, :]
        out_p[where, :] = (buf_p[where, :] - LEARN_RATE * decayed).astype(BF)
        out_m[where, :] = decayed.astype(BF)

    def step(i, carry):
        piece(at(i, 512))
        return carry

    lax.fori_loop(0, 8, step, 0)
    piece(pl.ds(4096, 96))


def turned(source, out):
    for c in range(STEPS):
        out[:, 128 * c : 128 * c + 128] = source[128 * c : 128 * c + 128, :].T


def spread(out, step, values, mask):
    where = pl.ds(pl.multiple_of(step * 128 + LINE, LINE), 128)
    out[where, 0:256] = (pltpu.roll(values, 4, 0) * mask).astype(BF)
    out[where, 256:512] = values.astype(BF)
    out[where, 512:768] = (pltpu.roll(values, 124, 0) * mask).astype(BF)


def edges(out):
    zeros = jnp.zeros((LINE, out.shape[1]), out.dtype)
    out[0:LINE, :] = zeros
    out[LINE + ROWS : 2 * LINE + ROWS, :] = zeros


def spread_of(values, mask):
    def step(c, carry):
        centred = (values[at(c), :] - carry[1]) * mask
        return (carry[0] + fold(centred * centred), carry[1])

    return step


def first_layer(role, rows, a0, a1, a2, a3, norms, xh, inv_out, padded, weight, sem):
    cands = (a0, a1, a2, a3)
    choose(role[0], 0, cands, weight, sem)
    edges(padded)
    mask = row_mask(256)
    small = norms[...].astype(F32)
    gain, bias = vector(small, 0, 2), vector(small, 2, 2)
    landed(cands, weight, sem)

    def one(c, acc):
        w = jnp.concatenate([weight[0:1024, :], weight[1024:2048, :]], axis=1)
        h = dot(rows[at(c), :], w)
        xh[at(c), :] = h
        return acc + fold(h)

    mean = total(lax.fori_loop(0, STEPS, one, jnp.zeros((8, 256), F32))) / PIX
    square, _ = lax.fori_loop(0, STEPS, spread_of(xh, mask), (jnp.zeros((8, 256), F32), mean))
    inv = lax.rsqrt(total(square) / PIX + EPS)
    inv_out[...] = jnp.broadcast_to(inv, (8, 256))

    def two(c, carry):
        hat = (xh[at(c), :] - mean) * inv * mask
        xh[at(c), :] = hat
        spread(padded, c, jnp.maximum(hat * gain + bias, 0.0) * mask, mask)
        return carry

    lax.fori_loop(0, STEPS, two, 0)


def middle(
    role, labels, rows, padded, norms, last, xa0, xa1, xa2, xa3, xb0, xb1, xb2, xb3,
    de, dsec, xh2, inv_out, wsp, pd, dnorm,
    s_b0, s_a1, s_b1, s_a2, s_b2, s_a3, s_b3, we, h3, dh3, sec, sect, turn, turn2, sems,
):
    own = role[0]
    xa, xb = (xa0, xa1, xa2, xa3), (xb0, xb1, xb2, xb3)
    plan = [
        (0, xb, s_b0), (1, xa, s_a1), (1, xb, s_b1),
        (2, xa, s_a2), (2, xb, s_b2), (3, xa, s_a3), (3, xb, s_b3),
    ]
    for i, (wanted, cands, place) in enumerate(plan):
        choose(own, wanted, cands, place, sems.at[i])
    mask = row_mask(256)
    mask3 = row_mask(1024)
    small = norms[...].astype(F32)
    gain2, bias2 = vector(small, 4, 2), vector(small, 6, 2)
    gain3, bias3 = vector(small, 8, 8), vector(small, 16, 8)

    for i in range(3):
        landed(plan[i][1], plan[i][2], sems.at[i])
    wsp[0:1024, 0:128] = s_b0[0:1024, :]
    wsp[0:1024, 128:256] = s_b0[1280:2304, :]
    wsp[1024:1280, 0:128] = s_b0[1024:1280, :] + s_a1[0:256, :]
    wsp[1024:1280, 128:256] = s_b0[2304:2560, :] + s_a1[1280:1536, :]
    wsp[1280:2304, 0:128] = s_a1[256:1280, :]
    wsp[1280:1792, 128:256] = s_a1[1536:2048, :]
    wsp[1792:2304, 128:256] = s_b1[0:512, :]
    for j in range(8):
        we[0:208, 128 * j : 128 * j + 128] = s_b1[512 + 256 * j : 720 + 256 * j, :]
        we[208:256, 128 * j : 128 * j + 128] = (
            s_b1[720 + 256 * j : 768 + 256 * j, :] + last[48 * j : 48 * j + 48, :]
        )

    def conv(c, acc):
        h = jnp.zeros((128, 256), F32)
        for dy in range(3):
            where = pl.ds(pl.multiple_of(c * 128 + dy * LINE, LINE), 128)
            h = h + dot(padded[where, :], wsp[768 * dy : 768 * dy + 768, :])
        xh2[at(c), :] = h
        return acc + fold(h)

    mean = total(lax.fori_loop(0, STEPS, conv, jnp.zeros((8, 256), F32))) / PIX
    square, _ = lax.fori_loop(0, STEPS, spread_of(xh2, mask), (jnp.zeros((8, 256), F32), mean))
    inv = lax.rsqrt(total(square) / PIX + EPS)
    inv_out[...] = jnp.broadcast_to(inv, (8, 256))

    def expand(c, acc):
        hat = (xh2[at(c), :] - mean) * inv * mask
        xh2[at(c), :] = hat
        second = (jnp.maximum(hat * gain2 + bias2, 0.0) * mask).astype(BF)
        sec[at(c), :] = second
        h = dot(second, we[...])
        h3[at(c), :] = h
        return acc + fold(h)

    mean3 = total(lax.fori_loop(0, STEPS, expand, jnp.zeros((8, 1024), F32))) / PIX
    square3, _ = lax.fori_loop(0, STEPS, spread_of(h3, mask3), (jnp.zeros((8, 1024), F32), mean3))
    inv3 = lax.rsqrt(total(square3) / PIX + EPS)

    def pool(c, carry):
        acc, count, weighed = carry
        hat = (h3[at(c), :] - mean3) * inv3
        h3[at(c), :] = hat
        out = hat * gain3 + bias3 + rows[at(c), :].astype(F32)
        on = slope(out) * mask3
        return (
            acc + fold(jnp.maximum(out, 0.0) * mask3),
            count + fold(on),
            weighed + fold(on * hat),
        )

    zero8 = jnp.zeros((8, 1024), F32)
    acc, count, weighed = lax.fori_loop(0, STEPS, pool, (zero8, zero8, zero8))
    acc = (acc + pltpu.roll(acc, 4, 0)) / 196.0
    four = lax.broadcasted_iota(jnp.int32, (8, 1024), 0) < 4
    pooled = jnp.where(four, acc, 0.0).astype(BF).astype(F32)

    turn[...] = jnp.concatenate([pooled, jnp.zeros((120, 1024), F32)], axis=0).T
    for j in range(16):
        turn2[128 * j : 128 * j + 64, :] = turn[pl.ds(j, 64, stride=16), :]
        turn2[128 * j + 64 : 128 * j + 128, :] = jnp.zeros((64, 128), F32)
    for i in range(3, 7):
        landed(plan[i][1], plan[i][2], sems.at[i])

    def window(first, end):
        tiles = []
        for r in range(first, end):
            parts = [s[16 * r : 16 * r + 16, :] for s in (s_a2, s_b2, s_a3, s_b3)]
            tiles.append(jnp.concatenate(parts, axis=0))
        return jnp.concatenate(tiles, axis=1)

    logits = jnp.zeros((16, 1024), F32)
    for j, (first, end, shift) in enumerate(WINDOWS):
        part = turn2[128 * j : 128 * j + 128, :].T[0:16, 0:64].astype(BF)
        wide = dot(part, window(first, end))
        width = 128 * (end - first)
        if shift:
            wide = pltpu.roll(wide, width - shift, 1)
        logits = logits + wide[:, 0:1024]
    lane = lax.broadcasted_iota(jnp.int32, (16, 1024), 1)
    image = lax.broadcasted_iota(jnp.int32, (16, 1024), 0)
    real = lane < CLASSES
    logits = jnp.where(real, logits, -1e30)
    top = jnp.max(logits, axis=1, keepdims=True)
    ex = jnp.where(real, jnp.exp(logits - top), 0.0)
    prob = ex / jnp.sum(ex, axis=1, keepdims=True)
    hot = jnp.zeros((16, 1024), jnp.bool_)
    for i in range(4):
        hot = hot | ((image == i) & (lane == labels[i]))
    dl = jnp.where(image < 4, (prob - jnp.where(hot, 1.0, 0.0)) * 0.25, 0.0)
    pd[...] = jnp.concatenate([pooled, dl[0:8, :]], axis=0).astype(BF)
    dl = jnp.concatenate([dl, jnp.zeros((112, 1024), F32)], axis=0)
    dl = jnp.concatenate([dl, jnp.zeros((128, 128), F32)], axis=1)
    for j, (first, end, shift) in enumerate(WINDOWS):
        width = 128 * (end - first)
        moved = dl[:, 0:width]
        if shift:
            moved = pltpu.roll(moved, shift, 1)
        turn[pl.ds(j, 64, stride=16), :] = dot_nt(window(first, end), moved.astype(BF))
    dpool = turn[...].T[0:8, :] / 196.0
    dpool = jnp.where(four, dpool, pltpu.roll(dpool, 4, 0))

    dbias3 = total(count * dpool)
    dgain3 = total(weighed * dpool)
    for j in range(8):
        dnorm[j : j + 1, :] = dgain3[:, 128 * j : 128 * j + 128]
        dnorm[8 + j : 9 + j, :] = dbias3[:, 128 * j : 128 * j + 128]
    scale = gain3 * inv3
    level = scale * dbias3 / PIX
    tilt = scale * dgain3 / PIX
    steep = scale * dpool

    def back(c, carry):
        hat = h3[at(c), :]
        on = slope(hat * gain3 + bias3 + rows[at(c), :].astype(F32))
        step = (on.reshape(16, 8, 1024) * steep[None]).reshape(128, 1024)
        dh3[at(c), :] = (step - level - hat * tilt).astype(BF)
        return carry

    lax.fori_loop(0, STEPS, back, 0)
    turned(sec, sect)
    for n in range(4):
        for m in range(2):
            piece = dot(sect[128 * m : 128 * m + 128, :], dh3[:, 256 * n : 256 * n + 256])
            for t in range(2):
                start = 256 * (2 * n + t) + 128 * m
                de[start : start + 128, :] = piece[:, 128 * t : 128 * t + 128].astype(BF)

    def down(c, carry):
        dsec[at(c), :] = dot_nt(dh3[at(c), :], we[...])
        return carry

    lax.fori_loop(0, STEPS, down, 0)


def bn_back(dy, xh, gain, bias, inv, mask):
    def sums(c, carry):
        hat = xh[at(c), :]
        d = dy[at(c), :] * slope(hat * gain + bias) * mask
        dy[at(c), :] = d
        return (carry[0] + fold(d), carry[1] + fold(d * hat))

    zero = jnp.zeros((8, 256), F32)
    a, b = lax.fori_loop(0, STEPS, sums, (zero, zero))
    return total(a), total(b)


def back_spatial(role, dsec, xh2, inv2, norms, padt, ds, dext, dnorm, work):
    own = role[0]
    small = norms[...].astype(F32)
    gain, bias = vector(small, 4, 2), vector(small, 6, 2)
    inv = inv2[0:1, :]
    mask = row_mask(256)

    def take(c, carry):
        work[at(c), :] = dsec[at(c), :]
        return carry

    lax.fori_loop(0, STEPS, take, 0)
    dbias, dgain = bn_back(work, xh2, gain, bias, inv, mask)
    for t in range(2):
        dnorm[t : t + 1, :] = dgain[:, 128 * t : 128 * t + 128]
        dnorm[2 + t : 3 + t, :] = dbias[:, 128 * t : 128 * t + 128]
    dnorm[4:8, :] = jnp.zeros((4, 128), F32)
    dext[0:128, :] = jnp.zeros((128, 256), BF)
    dext[1024:1152, :] = jnp.zeros((128, 256), BF)
    scale = gain * inv
    level, tilt = dbias / PIX, dgain / PIX

    def one(c, carry):
        d = scale * (work[at(c), :] - level - xh2[at(c), :] * tilt) * mask
        dext[pl.ds(pl.multiple_of(c * 128 + 128, 128), 128), :] = d.astype(BF)
        return carry

    lax.fori_loop(0, STEPS, one, 0)
    other = 1 - own
    for dy in range(3):
        right = dext[128 - LINE * dy : 1152 - LINE * dy, :]
        for m in range(6):
            piece = dot(padt[128 * m : 128 * m + 128, :], right).astype(BF)
            start = 768 * dy + 128 * m
            for t in range(2):
                half = piece[:, 128 * t : 128 * t + 128]
                if start < 1280:
                    ds[own, 1280 * t + start : 1280 * t + start + 128, :] = half
                if start >= 1024:
                    low = 1280 * t + start - 1024
                    ds[other, low : low + 128, :] = half


def back_reduce(dext, xh1, inv1, norms, rowst, wsp, dwr, dnorm, spreads, work, dh1):
    small = norms[...].astype(F32)
    gain, bias = vector(small, 0, 2), vector(small, 2, 2)
    inv = inv1[0:1, :]
    mask = row_mask(256)
    edges(spreads)

    def widen(c, carry):
        where = pl.ds(pl.multiple_of(c * 128 + 128, 128), 128)
        spread(spreads, c, dext[where, :].astype(F32), mask)
        return carry

    lax.fori_loop(0, STEPS, widen, 0)

    def conv(c, carry):
        d = jnp.zeros((128, 256), F32)
        for dy in range(3):
            where = pl.ds(pl.multiple_of(c * 128 + (2 - dy) * LINE, LINE), 128)
            for dx in range(3):
                tap = 256 * (3 * dy + dx)
                lanes = 256 * (2 - dx)
                d = d + dot_nt(spreads[where, lanes : lanes + 256], wsp[tap : tap + 256, :])
        work[at(c), :] = d
        return carry

    lax.fori_loop(0, STEPS, conv, 0)
    dbias, dgain = bn_back(work, xh1, gain, bias, inv, mask)
    for t in range(2):
        dnorm[t : t + 1, :] = dgain[:, 128 * t : 128 * t + 128]
        dnorm[2 + t : 3 + t, :] = dbias[:, 128 * t : 128 * t + 128]
    dnorm[4:8, :] = jnp.zeros((4, 128), F32)
    scale = gain * inv
    level, tilt = dbias / PIX, dgain / PIX

    def one(c, carry):
        d = scale * (work[at(c), :] - level - xh1[at(c), :] * tilt) * mask
        dh1[at(c), :] = d.astype(BF)
        return carry

    lax.fori_loop(0, STEPS, one, 0)
    for m in range(8):
        piece = dot(rowst[128 * m : 128 * m + 128, :], dh1[...]).astype(BF)
        for t in range(2):
            start = 1024 * t + 128 * m
            dwr[start : start + 128, :] = piece[:, 128 * t : 128 * t + 128]


def finish(
    role, flat_p, flat_m, peer_p, peer_m, r_own, r_peer, s_own, s_peer, e_own, e_peer,
    t_own, t_peer, n_own, n_peer, pd_own, pd_peer,
    out_p, out_m, grad, buf_p, buf_m, turn, sems,
):
    own = role[0]
    copies = [
        pltpu.make_async_copy(flat_p.reshape(LROWS, 128), buf_p.at[pl.ds(0, LROWS)], sems.at[0]),
        pltpu.make_async_copy(flat_m.reshape(LROWS, 128), buf_m.at[pl.ds(0, LROWS)], sems.at[1]),
    ]
    for copy in copies:
        copy.start()

    def both(a, b, start, size):
        return a[start : start + size, :].astype(F32) + b[start : start + size, :].astype(F32)

    @pl.when(own == 0)
    def _():
        for t in range(2):
            grad[pl.ds(OFF + t, 1024, stride=2), :] = both(r_own, r_peer, 1024 * t, 1024)
            grad[pl.ds(OFF + 2048 + t, 1280, stride=2), :] = both(s_own, s_peer, 1280 * t, 1280)

    @pl.when(own == 1)
    def _():
        for t in range(2):
            grad[pl.ds(10 + t, 1280, stride=2), :] = both(s_own, s_peer, 1280 * t, 1280)
        for j in range(8):
            grad[pl.ds(OFF + 2474 + j, 256, stride=8), :] = both(e_own, e_peer, 256 * j, 256)

    def classify(group, start):
        both_pd = [pd_own[...].astype(F32), pd_peer[...].astype(F32)]
        pooled = [part[i : i + 8, :] for part in both_pd for i in range(0, 64, 16)]
        pooled = jnp.concatenate(pooled + [jnp.zeros((64, 1024), F32)], axis=0)
        turn[0:1024, :] = pooled.T
        turn[1024:1152, :] = jnp.zeros((128, 128), F32)
        dl = [part[i + 8 : i + 16, :] for part in both_pd for i in range(0, 64, 16)]
        dl = jnp.concatenate(dl + [jnp.zeros((64, 1024), F32)], axis=0)
        dl = jnp.concatenate([dl, jnp.zeros((128, 128), F32)], axis=1)
        carried = None
        for j, (first, end, shift) in enumerate(WINDOWS):
            width = 128 * (end - first)
            moved = dl[:, 0:width]
            if shift:
                moved = pltpu.roll(moved, shift, 1)
            left = turn[pl.ds(16 * group + j, 40, stride=16), :].astype(BF)
            piece = dot(left, moved.astype(BF))
            for r in range(first, end):
                tile = piece[:, 128 * (r - first) : 128 * (r - first) + 128]
                if r == first and carried is not None:
                    tile = tile + carried
                    carried = None
                if r == end - 1 and j < 15 and WINDOWS[j + 1][0] == r:
                    carried = tile
                else:
                    grad[pl.ds(start + r, 40, stride=125), :] = tile

    @pl.when(own == 2)
    def _():
        classify(0, 436)
        for j in range(8):
            grad[pl.ds(52 + j, 48, stride=8), :] = both(t_own, t_peer, 48 * j, 48)

    @pl.when(own == 3)
    def _():
        classify(30, 4)
        grad[OFF + 4158 : OFF + 4182, :] = both(n_own, n_peer, 0, 32)[0:24, :]

    for copy in copies:
        copy.wait()

    def piece(where, shifted):
        g = grad[shifted, :] * 0.25
        decayed = MOMENTUM_RATE * buf_m[where, :]
        p = 0.5 * ((buf_p[where, :] - LEARN_RATE * decayed) + peer_p[where, :].astype(F32))
        m = 0.5 * (decayed + peer_m[where, :].astype(F32))
        buf_p[where, :] = p - (0.5 * LEARN_RATE) * g
        buf_m[where, :] = m + 0.5 * g

    def step(i, carry):
        piece(at(i, 256), pl.ds(pl.multiple_of(i * 256 + OFF, 32), 256))
        return carry

    lax.fori_loop(0, 16, step, 0)
    piece(pl.ds(4096, 96), pl.ds(4096 + OFF, 96))
    copies = [
        pltpu.make_async_copy(buf_p.at[pl.ds(0, LROWS)], out_p.reshape(LROWS, 128), sems.at[0]),
        pltpu.make_async_copy(buf_m.at[pl.ds(0, LROWS)], out_m.reshape(LROWS, 128), sems.at[1]),
    ]
    for copy in copies:
        copy.start()
    for copy in copies:
        copy.wait()


def along(value, pairs):
    return lax.ppermute(value, "local", pairs)


CORE = [(l, l ^ 1) for l in range(4)]
CHIP = [(l, l ^ 2) for l in range(4)]


def add(a, b):
    return (a.astype(F32) + b.astype(F32)).astype(BF)


def whole_step(images, labels, params, momentum, distance):
    nodes = lax.axis_size("node")
    index = lax.axis_index("local")
    role = index.astype(jnp.int32).reshape(1)
    odd = (index % 2) == 1
    dma = pltpu.SemaphoreType.DMA
    flat = (LROWS * 128) * 4

    def ahead(value, members):
        pairs = [
            (n * 4 + l, ((n + distance) % nodes) * 4 + l) for n in range(nodes) for l in members
        ]
        return lax.ppermute(value, ("node", "local"), pairs)

    xa = call(
        prepare_a, "prepare_a", [SM, ANY], shape((2048, 128), BF),
        [pltpu.VMEM((4704, 128), F32), dma], 0, flat,
    )(role, params)
    spill = along(params[:, : 160 * 128].reshape(160, 128), [(3, 2)])
    ya = along(xa, CHIP)
    xb, small = call(
        prepare_b, "prepare_b", [SM, ANY, VM],
        [shape((2560, 128), BF), shape((384, 128), BF)],
        [pltpu.VMEM((4704, 128), F32), dma], 0, flat,
    )(role, params, spill)
    small_y = along(small, CHIP)
    yb = along(xb, CHIP)
    za, zb = along(xa, CORE), along(xb, CORE)
    small_u = jnp.where(index >= 2, small, small_y)
    small_d = along(small_u, CORE)
    last = jnp.where(odd, small_d, small_u)
    norms = jnp.where(odd, small_u, small_d)[0:32]
    va, vb = along(ya, CORE), along(yb, CORE)

    send_p, send_m = call(
        prepare_gossip, "prepare_gossip", [ANY, ANY],
        [shape((GROWS, 128), BF)] * 2,
        [pltpu.VMEM((GROWS, 128), F32), pltpu.VMEM((GROWS, 128), F32), dma((2,))], 0, 3 * flat,
    )(params, momentum)
    peer_p, peer_m = ahead(send_p, range(4)), ahead(send_m, range(4))

    rows = jnp.transpose(images, (1, 2, 0, 3))
    rows = jnp.pad(rows, ((0, 0), (0, 2), (0, 0), (0, 0))).reshape(ROWS, 1024)
    rowst = call(
        turned, "turn_rows", [VM], shape((1024, ROWS), BF), [], 0, 4 * ROWS * 1024,
    )(rows)
    xh1, inv1, padded = call(
        first_layer, "first_layer", [SM, VM, ANY, ANY, ANY, ANY, VM],
        [shape((ROWS, 256), F32), shape((8, 256), F32), shape((1024, 768), BF)],
        [pltpu.VMEM((2048, 128), BF), dma], 2 * ROWS * 1024 * 256, 6 * 2**20,
    )(role, rows, xa, za, ya, va, norms)

    def turn_padded(source, out):
        for c in range(8):
            out[:, 128 * c : 128 * c + 128] = source[128 * c : 128 * c + 128, :].T

    padt = call(
        turn_padded, "turn_padded", [VM], shape((768, 1024), BF), [], 0, 4 * 768 * 1024,
    )(padded)
    half_a, half_b = pltpu.VMEM((2048, 128), BF), pltpu.VMEM((2560, 128), BF)
    de, dsec, xh2, inv2, wsp, pd, dnorm3 = call(
        middle, "middle", [SM, SM, VM, VM, VM, VM] + [ANY] * 8,
        [
            shape((2048, 128), BF), shape((ROWS, 256), F32), shape((ROWS, 256), F32),
            shape((8, 256), F32), shape((2304, 256), BF), shape((16, 1024), BF),
            shape((16, 128), F32),
        ],
        [
            half_b, half_a, half_b, half_a, half_b, half_a, half_b,
            pltpu.VMEM((256, 1024), BF), pltpu.VMEM((ROWS, 1024), F32),
            pltpu.VMEM((ROWS, 1024), BF), pltpu.VMEM((ROWS, 256), BF),
            pltpu.VMEM((256, ROWS), BF), pltpu.VMEM((1024, 128), F32),
            pltpu.VMEM((2048, 128), F32), dma((7,)),
        ],
        4 * 10**9, 12 * 2**20,
    )(role, labels, rows, padded, norms, last, xa, za, ya, va, xb, zb, yb, vb)
    e_core = add(de, along(de, [(0, 1), (2, 3)]))
    e_own = add(e_core, along(e_core, [(3, 1)]))
    e_peer = ahead(e_own, [1])
    tails = jnp.concatenate([e_core[256 * j + 208 : 256 * j + 256] for j in range(8)], axis=0)
    tails = add(tails, along(tails, [(1, 3)]))
    t_own = along(tails, [(3, 2)])
    t_peer = ahead(t_own, [2])
    pd = jnp.concatenate([pd, along(pd, CORE)], axis=0)
    pd_own = jnp.concatenate([pd, along(pd, CHIP)], axis=0)
    pd_peer = ahead(pd_own, [2, 3])

    ds, dext, dnorm2 = call(
        back_spatial, "back_spatial", [SM, VM, VM, VM, VM, VM],
        [shape((2, 2560, 128), BF), shape((1152, 256), BF), shape((8, 128), F32)],
        [pltpu.VMEM((ROWS, 256), F32)], 2 * 1024 * 2304 * 256, 6 * 2**20,
    )(lax.rem(role, 2), dsec, xh2, inv2, norms, padt)
    s_core = add(ds[0], along(ds[1], CORE))
    s_own = add(s_core, along(s_core, [(2, 0), (3, 1)]))
    s_peer = ahead(s_own, [0, 1])

    dwr, dnorm1 = call(
        back_reduce, "back_reduce", [VM] * 6,
        [shape((2048, 128), BF), shape((8, 128), F32)],
        [
            pltpu.VMEM((1024, 768), BF), pltpu.VMEM((ROWS, 256), F32), pltpu.VMEM((ROWS, 256), BF),
        ],
        2 * ROWS * (2304 + 1024) * 256, 8 * 2**20,
    )(dext, xh1, inv1, norms, rowst, wsp)
    r_core = add(dwr, along(dwr, [(1, 0), (3, 2)]))
    r_own = add(r_core, along(r_core, [(2, 0)]))
    r_peer = ahead(r_own, [0])
    dnorm = jnp.concatenate([dnorm1[0:4], dnorm2[0:4], dnorm3, jnp.zeros((8, 128), F32)], axis=0)
    dnorm = dnorm + along(dnorm, CORE)
    n_own = dnorm + along(dnorm, CHIP)
    n_peer = ahead(n_own, [3])

    return call(
        finish, "finish", [SM, ANY, ANY] + [VM] * 14,
        [shape((1, LROWS * 128), F32)] * 2,
        [
            pltpu.VMEM((5440, 128), F32), pltpu.VMEM((GROWS, 128), F32),
            pltpu.VMEM((GROWS, 128), F32), pltpu.VMEM((1152, 128), F32), dma((2,)),
        ],
        0, 6 * flat, out_specs=[ANY, ANY],
    )(
        role, params, momentum, peer_p, peer_m, r_own, r_peer, s_own, s_peer, e_own, e_peer,
        t_own, t_peer, n_own, n_peer, pd_own, pd_peer,
    )


def body(images, labels, params, momentum, step):
    degrees = lax.axis_size("node").bit_length() - 1
    branches = [functools.partial(whole_step, distance=1 << degree) for degree in range(degrees)]
    return tuple(lax.switch(step[0] % degrees, branches, images, labels, params, momentum))


def solution(mesh):
    in_specs = (
        P(("node", "local"), None, None, None),
        P(("node", "local")),
        P("node", "local"),
        P("node", "local"),
        P(),
    )
    out_specs = (P("node", "local"), P("node", "local"))
    return jax.shard_map(body, mesh=mesh, in_specs=in_specs, out_specs=out_specs, check_vma=False)
```

```python
import functools

import jax
import jax.numpy as jnp
from jax import lax
from jax.experimental import pallas as pl
from jax.experimental.pallas import tpu as pltpu
from jax.sharding import PartitionSpec as P

F32 = jnp.float32
BF = jnp.bfloat16

CLASSES = 1000
EPS = 1e-05
MOMENTUM_RATE = 0.9
LEARN_RATE = 0.1

LROWS = 4182
GROWS = 4192
OFF = 96
PIX = 784.0

ROWS = 896
LINE = 64
VALID = 56
STEPS = 7

WIDE = 9 * 128


PART_A = 2048
PART_B = 2560
SENT = PART_A + PART_B
NORMS = 2000
TAILS = 2000
SPILL = 2000

VMEM_LIMIT = 48 * 1024 * 1024

ANY = pl.BlockSpec(memory_space=pl.ANY)
VM = pl.BlockSpec(memory_space=pltpu.VMEM)
SM = pl.BlockSpec(memory_space=pltpu.SMEM)


def shape(dims, dtype):
    return jax.ShapeDtypeStruct(dims, dtype)


def call(kernel, name, in_specs, out_shape, scratch, out_specs=None):
    extra = {} if out_specs is None else {"out_specs": out_specs}
    return pl.pallas_call(
        kernel,
        name=name,
        in_specs=in_specs,
        out_shape=out_shape,
        scratch_shapes=scratch,
        compiler_params=pltpu.CompilerParams(vmem_limit_bytes=VMEM_LIMIT),
        cost_estimate=pl.CostEstimate(flops=1, bytes_accessed=1, transcendentals=0),
        **extra,
    )


def at(step, size=128):
    return pl.ds(pl.multiple_of(step * size, size), size)


def dot(a, b):
    return jnp.dot(a, b, preferred_element_type=F32)


def dot_nt(a, b):
    return lax.dot_general(a, b, (((1,), (1,)), ((), ())), preferred_element_type=F32)


def fold(values):
    rows, lanes = values.shape
    return jnp.sum(values.reshape(rows // 8, 8, lanes), axis=0)


def total(folded):
    return jnp.sum(folded, axis=0, keepdims=True)


def row_mask(lanes):
    rows = lax.broadcasted_iota(jnp.int32, (128, lanes), 0)
    return jnp.where(lax.rem(rows, LINE) < VALID, 1.0, 0.0).astype(F32)


def line_mask(lanes):
    rows = lax.broadcasted_iota(jnp.int32, (LINE, lanes), 0)
    return jnp.where(rows < VALID, 1.0, 0.0).astype(F32)


def slope(values):
    return jnp.where(values > 0.0, 1.0, jnp.where(values == 0.0, 0.5, 0.0))


def vector(norms, row, count):
    return jnp.concatenate([norms[row + i : row + i + 1, :] for i in range(count)], axis=1)


def window_of(j):
    return lax.div(125 * j, 16), 8 * lax.rem(125 * j, 16)


def loop(count, body, times=1):
    def step(i, carry):
        for k in range(times):
            body(i * times + k)
        return carry

    lax.fori_loop(0, count // times, step, 0)


def summed(count, body, start, times=1):
    def step(i, carry):
        for k in range(times):
            carry = body(i * times + k, carry)
        return carry

    return lax.fori_loop(0, count // times, step, start)


def choose(own, wanted, candidates, start, place, sem):
    for distance in range(4):

        @pl.when(lax.bitwise_xor(own, wanted) == distance)
        def _(source=candidates[distance]):
            pltpu.make_async_copy(source.at[pl.ds(start, place.shape[0])], place, sem).start()


def landed(candidates, start, place, sem):
    pltpu.make_async_copy(candidates[0].at[pl.ds(start, place.shape[0])], place, sem).wait()


def load_flat(flat, buf, sem):
    copy = pltpu.make_async_copy(flat.reshape(LROWS, 128), buf.at[pl.ds(OFF, LROWS)], sem)
    copy.start()
    buf[0:OFF, :] = jnp.zeros((OFF, 128), F32)
    end = OFF + LROWS
    buf[end : buf.shape[0], :] = jnp.zeros((buf.shape[0] - end, 128), F32)
    copy.wait()


def columns(buf, out, place, start, stride, size, chunk):
    def body(i):
        rows = buf[pl.ds(start + i * chunk * stride, chunk, stride=stride), :]
        out[pl.ds(pl.multiple_of(place + i * chunk, 16), chunk), :] = rows.astype(BF)

    loop(size // chunk, body)


def prepare(role, flat, out_a, out_b, buf, sem):
    load_flat(flat, buf, sem)
    own = role[0]

    @pl.when(own == 0)
    def _():
        for t in range(2):
            columns(buf, out_a, 1024 * t, OFF + t, 2, 1024, 256)
            columns(buf, out_b, 1280 * t, OFF + 2048 + t, 2, 1280, 256)

    @pl.when(own == 1)
    def _():
        columns(buf, out_a, 0, 10, 2, 1280, 256)
        columns(buf, out_a, 1280, 11, 2, 768, 256)
        columns(buf, out_b, 0, 11 + 2 * 768, 2, 512, 256)

        def body(j):
            columns(buf, out_b, 512 + 256 * j, OFF + 2474 + j, 8, 256, 256)

        loop(8, body)

    @pl.when(own >= 2)
    def _():
        start = jnp.where(own == 2, 436, 254)

        def body(k):
            for i in range(5):
                r = 5 * k + i
                where = pl.ds(pl.multiple_of(16 * r, 16), 16)
                for half, out in ((0, out_a), (1, out_b)):
                    rows = buf[pl.ds(start + half * 16 * 125 + r, 16, stride=125), :]
                    out[where, :] = rows.astype(BF)

        loop(25, body)
        out_a[2000:2048, :] = jnp.zeros((48, 128), BF)

    @pl.when(own == 2)
    def _():
        def body(j):
            columns(buf, out_b, TAILS + 48 * j, 52 + j, 8, 48, 48)

        loop(8, body)
        out_b[TAILS + 384 : PART_B, :] = jnp.zeros((176, 128), BF)

    @pl.when(own == 3)
    def _():
        out_a[NORMS : NORMS + 32, :] = buf[OFF + 4158 : OFF + 4190, :].astype(BF)
        out_b[SPILL : SPILL + 128, :] = buf[4:132, :].astype(BF)
        out_b[SPILL + 128 : SPILL + 256, :] = buf[129:257, :].astype(BF)
        out_b[SPILL + 256 : PART_B, :] = jnp.zeros((304, 128), BF)


def prepare_gossip(flat_p, flat_m, out, buf_p, buf_m, sems):
    copies = [
        pltpu.make_async_copy(flat_p.reshape(LROWS, 128), buf_p.at[pl.ds(0, LROWS)], sems.at[0]),
        pltpu.make_async_copy(flat_m.reshape(LROWS, 128), buf_m.at[pl.ds(0, LROWS)], sems.at[1]),
    ]
    for copy in copies:
        copy.start()
    for copy in copies:
        copy.wait()
    for buf in (buf_p, buf_m):
        buf[LROWS:GROWS, :] = jnp.zeros((GROWS - LROWS, 128), F32)

    def piece(where, second):
        decayed = MOMENTUM_RATE * buf_m[where, :]
        out[where, :] = (buf_p[where, :] - LEARN_RATE * decayed).astype(BF)
        out[second, :] = decayed.astype(BF)

    def body(i):
        piece(at(i, 32), pl.ds(pl.multiple_of(i * 32 + GROWS, 32), 32))

    loop(131, body)


def turned(source, out):
    def body(c):
        out[:, at(c)] = source[at(c), :].T

    steps = source.shape[0] // 128
    loop(steps, body, steps if source.shape[1] == 256 else 1)


def spread(out, step, values, mask):
    where = pl.ds(pl.multiple_of(step * 128 + LINE, LINE), 128)
    out[where, 0:256] = (pltpu.roll(values, 4, 0) * mask).astype(BF)
    out[where, 256:512] = values.astype(BF)
    out[where, 512:768] = (pltpu.roll(values, 124, 0) * mask).astype(BF)


def edges(out):
    zeros = jnp.zeros((LINE, out.shape[1]), out.dtype)
    out[0:LINE, :] = zeros
    out[LINE + ROWS : 2 * LINE + ROWS, :] = zeros


def spread_of(values, mean):
    lanes = values.shape[1]
    mask = line_mask(lanes)

    def step(c, acc):
        centred = (values[at(c, LINE), :] - mean) * mask
        return acc + fold(centred * centred)

    return total(summed(ROWS // LINE, step, jnp.zeros((8, lanes), F32), 2))


def first_layer(role, rows, x0, x1, x2, x3, xh, inv_out, padded, norms_out, weight, norms, sems):
    cands = (x0, x1, x2, x3)
    choose(role[0], 0, cands, 0, weight, sems.at[0])
    choose(role[0], 3, cands, NORMS, norms, sems.at[1])
    edges(padded)
    mask = row_mask(256)
    landed(cands, NORMS, norms, sems.at[1])
    norms_out[...] = norms[...]
    small = norms[...].astype(F32)
    gain, bias = vector(small, 0, 2), vector(small, 2, 2)
    landed(cands, 0, weight, sems.at[0])

    def one(c, acc):
        w = jnp.concatenate([weight[0:1024, :], weight[1024:2048, :]], axis=1)
        h = dot(rows[at(c), :], w)
        xh[at(c), :] = h
        return acc + fold(h)

    mean = total(lax.fori_loop(0, STEPS, one, jnp.zeros((8, 256), F32))) / PIX
    inv = lax.rsqrt(spread_of(xh, mean) / PIX + EPS)
    inv_out[...] = jnp.broadcast_to(inv, (8, 256))

    def two(c, carry):
        hat = (xh[at(c), :] - mean) * inv * mask
        xh[at(c), :] = hat
        spread(padded, c, jnp.maximum(hat * gain + bias, 0.0) * mask, mask)
        return carry

    lax.fori_loop(0, STEPS, two, 0)


def middle(
    role, labels, rows, padded, norms, a0, a1, a2, a3, b0, b1, b2, b3,
    de, dsec, xh2, inv_out, wsp, small_out, dnorm,
    s0, s1, s2, s3, we, h3, dh3, sec, sect, turn, turn2, wide_buf, sems,
):
    own = role[0]
    part_a, part_b = (a0, a1, a2, a3), (b0, b1, b2, b3)
    plan = [(0, part_b, s0)]
    for wanted, whole in ((1, s1), (2, s2), (3, s3)):
        plan.append((wanted, part_a, whole.at[pl.ds(0, PART_A)]))
        plan.append((wanted, part_b, whole.at[pl.ds(PART_A, PART_B)]))
    for i, (wanted, cands, place) in enumerate(plan):
        choose(own, wanted, cands, 0, place, sems.at[i])
    mask = row_mask(256)
    small = norms[...].astype(F32)
    gain2, bias2 = vector(small, 4, 2), vector(small, 6, 2)
    gain3, bias3 = vector(small, 8, 8), vector(small, 16, 8)

    for i, (wanted, cands, place) in enumerate(plan):
        landed(cands, 0, place, sems.at[i])
    for t in range(2):
        lanes = slice(128 * t, 128 * t + 128)

        def below(i, t=t, lanes=lanes):
            wsp[at(i), lanes] = s0[pl.ds(pl.multiple_of(1280 * t + 128 * i, 128), 128), :]
            where = pl.ds(pl.multiple_of(1280 + 128 * i, 128), 128)
            wsp[where, lanes] = s1[pl.ds(pl.multiple_of(1280 * t + 256 + 128 * i, 128), 128), :]

        loop(8, below, 4)
        wsp[1024:1280, lanes] = (
            s0[1280 * t + 1024 : 1280 * t + 1280, :] + s1[1280 * t : 1280 * t + 256, :]
        )

    def across(j):
        low = 2560 + 256 * j
        we[0:208, at(j)] = s1[pl.ds(pl.multiple_of(low, 256), 208), :]
        we[208:256, at(j)] = (
            s1[pl.ds(pl.multiple_of(low + 208, 16), 48), :]
            + s2[pl.ds(pl.multiple_of(PART_A + TAILS + 48 * j, 16), 48), :]
        )

    loop(8, across, 4)

    def widen(i):
        wide_buf[at(i, 80), :] = s2[pl.ds(pl.multiple_of(2048 + 80 * i, 16), 80), :].astype(F32)

    def narrow(i):
        s2[pl.ds(pl.multiple_of(2048 + 80 * i, 16), 80), :] = wide_buf[at(i, 80), :].astype(BF)

    loop(25, widen, 5)
    for i in range(2):
        spill = s3[PART_A + SPILL + 128 * i : PART_A + SPILL + 128 * i + 128, :].astype(F32)[0:125, :]
        where = pl.ds(14 + i, 125, stride=16)
        wide_buf[where, :] = wide_buf[where, :] + spill
    loop(25, narrow, 5)

    def conv(c, acc):
        h = jnp.zeros((128, 256), F32)
        for dy in range(3):
            where = pl.ds(pl.multiple_of(c * 128 + dy * LINE, LINE), 128)
            h = h + dot(padded[where, :], wsp[768 * dy : 768 * dy + 768, :])
        xh2[at(c), :] = h
        return acc + fold(h)

    mean = total(lax.fori_loop(0, STEPS, conv, jnp.zeros((8, 256), F32))) / PIX
    inv = lax.rsqrt(spread_of(xh2, mean) / PIX + EPS)
    inv_out[...] = jnp.broadcast_to(inv, (8, 256))

    def expand(c, acc):
        hat = (xh2[at(c), :] - mean) * inv * mask
        xh2[at(c), :] = hat
        second = (jnp.maximum(hat * gain2 + bias2, 0.0) * mask).astype(BF)
        sec[at(c), :] = second
        h = dot(second, we[...])
        h3[at(c), :] = h
        return acc + fold(h)

    mean3 = total(lax.fori_loop(0, STEPS, expand, jnp.zeros((8, 1024), F32))) / PIX
    inv3 = lax.rsqrt(spread_of(h3, mean3) / PIX + EPS)

    def pool(c, carry):
        acc, count, weighed = carry
        hat = (h3[at(c, LINE), :] - mean3) * inv3
        h3[at(c, LINE), :] = hat
        out = hat * gain3 + bias3 + rows[at(c, LINE), :].astype(F32)
        on = slope(out) * real3
        return (
            acc + fold(jnp.maximum(out, 0.0) * real3),
            count + fold(on),
            weighed + fold(on * hat),
        )

    zero8 = jnp.zeros((8, 1024), F32)
    real3 = line_mask(1024)
    acc, count, weighed = summed(ROWS // LINE, pool, (zero8, zero8, zero8), 2)
    acc = (acc + pltpu.roll(acc, 4, 0)) / 196.0
    four = lax.broadcasted_iota(jnp.int32, (8, 1024), 0) < 4
    pooled = jnp.where(four, acc, 0.0).astype(BF).astype(F32)

    turn[...] = jnp.concatenate([pooled, jnp.zeros((120, 1024), F32)], axis=0).T

    def regroup(j):
        part = jnp.concatenate([turn[pl.ds(j, 64, stride=16), :], jnp.zeros((64, 128), F32)], axis=0)
        turn2[at(j, 16), :] = part.T[0:16, :]

    loop(16, regroup, 4)

    def window(first):
        tiles = []
        for i in range(9):
            parts = [
                s[pl.ds(pl.multiple_of(start + 16 * (first + i), 16), 16), :]
                for s in (s2, s3)
                for start in (0, 2048)
            ]
            tiles.append(jnp.concatenate(parts, axis=0))
        return jnp.concatenate(tiles, axis=1)

    def score(j, acc):
        first, shift = window_of(j)
        wide = dot(turn2[at(j, 16), 0:64].astype(BF), window(first))
        return acc + pltpu.roll(wide, WIDE - shift, 1)[:, 0:1024]

    logits = summed(16, score, jnp.zeros((16, 1024), F32), 4)
    lane = lax.broadcasted_iota(jnp.int32, (16, 1024), 1)
    image = lax.broadcasted_iota(jnp.int32, (16, 1024), 0)
    real = lane < CLASSES
    logits = jnp.where(real, logits, -1e30)
    top = jnp.max(logits, axis=1, keepdims=True)
    ex = jnp.where(real, jnp.exp(logits - top), 0.0)
    prob = ex / jnp.sum(ex, axis=1, keepdims=True)
    hot = jnp.zeros((16, 1024), jnp.bool_)
    for i in range(4):
        hot = hot | ((image == i) & (lane == labels[i]))
    dl = jnp.where(image < 4, (prob - jnp.where(hot, 1.0, 0.0)) * 0.25, 0.0)
    pair = jnp.concatenate([pooled, dl[0:8, :]], axis=0).astype(BF)
    for t in range(8):
        small_out[384 + 16 * t : 400 + 16 * t, :] = pair[:, 128 * t : 128 * t + 128]
    dl = jnp.concatenate([dl, jnp.zeros((16, 128), F32)], axis=1)

    def unscore(j):
        first, shift = window_of(j)
        moved = pltpu.roll(dl, shift, 1).astype(BF)
        moved = jnp.concatenate([moved, jnp.zeros((112, WIDE), BF)], axis=0)
        turn[pl.ds(j, 64, stride=16), :] = dot_nt(window(first), moved)

    loop(16, unscore, 4)
    dpool = turn[...].T[0:8, :] / 196.0
    dpool = jnp.where(four, dpool, pltpu.roll(dpool, 4, 0))

    dbias3 = total(count * dpool)
    dgain3 = total(weighed * dpool)
    for j in range(8):
        dnorm[j : j + 1, :] = dgain3[:, 128 * j : 128 * j + 128]
        dnorm[8 + j : 9 + j, :] = dbias3[:, 128 * j : 128 * j + 128]
    scale = gain3 * inv3
    level = scale * dbias3 / PIX
    tilt = scale * dgain3 / PIX
    steep = scale * dpool

    def back(c):
        hat = h3[at(c, LINE), :]
        on = slope(hat * gain3 + bias3 + rows[at(c, LINE), :].astype(F32))
        step = (on.reshape(8, 8, 1024) * steep[None]).reshape(LINE, 1024)
        dh3[at(c, LINE), :] = (step - level - hat * tilt).astype(BF)

    loop(ROWS // LINE, back, 2)
    turned(sec, sect)

    def weigh(n):
        right = dh3[:, at(n, 256)]
        piece = dot(sect[...], right).astype(BF)
        for t in range(2):
            half = piece[:, 128 * t : 128 * t + 128]
            de[pl.ds(pl.multiple_of(512 * n + 256 * t, 128), 256), :] = half
            small_out[pl.ds(pl.multiple_of(96 * n + 48 * t, 16), 48), :] = half[208:256, :]

    loop(4, weigh, 2)
    small_out[512:544, :] = jnp.zeros((32, 128), BF)

    def down(c, carry):
        dsec[at(c), :] = dot_nt(dh3[at(c), :], we[...])
        return carry

    lax.fori_loop(0, STEPS, down, 0)


def bn_back(dy, xh, gain, bias, inv, mask):
    def sums(c, carry):
        hat = xh[at(c), :]
        d = dy[at(c), :] * slope(hat * gain + bias) * mask
        dy[at(c), :] = d
        return (carry[0] + fold(d), carry[1] + fold(d * hat))

    zero = jnp.zeros((8, 256), F32)
    a, b = lax.fori_loop(0, STEPS, sums, (zero, zero))
    return total(a), total(b)


def back_spatial(role, dsec, xh2, inv2, norms, padt, ds, dext, dnorm, work, full):
    own = role[0]
    small = norms[...].astype(F32)
    gain, bias = vector(small, 4, 2), vector(small, 6, 2)
    inv = inv2[0:1, :]
    mask = row_mask(256)

    def take(c, carry):
        work[at(c), :] = dsec[at(c), :]
        return carry

    lax.fori_loop(0, STEPS, take, 0)
    dbias, dgain = bn_back(work, xh2, gain, bias, inv, mask)
    for t in range(2):
        dnorm[t : t + 1, :] = dgain[:, 128 * t : 128 * t + 128]
        dnorm[2 + t : 3 + t, :] = dbias[:, 128 * t : 128 * t + 128]
    dnorm[4:8, :] = jnp.zeros((4, 128), F32)
    dext[0:128, :] = jnp.zeros((128, 256), BF)
    dext[1024:1152, :] = jnp.zeros((128, 256), BF)
    scale = gain * inv
    level, tilt = dbias / PIX, dgain / PIX

    def one(c, carry):
        d = scale * (work[at(c), :] - level - xh2[at(c), :] * tilt) * mask
        dext[pl.ds(pl.multiple_of(c * 128 + 128, 128), 128), :] = d.astype(BF)
        return carry

    lax.fori_loop(0, STEPS, one, 0)

    def weigh(dy):
        right = dext[pl.ds(pl.multiple_of(128 - LINE * dy, LINE), 1024), :]
        for m in range(2):
            piece = dot(padt[384 * m : 384 * m + 384, :], right).astype(BF)
            full[pl.ds(pl.multiple_of(768 * dy + 384 * m, 128), 384), :] = piece

    loop(3, weigh)

    def hand_out(i):
        for t in range(2):
            lanes = slice(128 * t, 128 * t + 128)
            where = at(i, 256)
            ds[own, t, where, :] = full[where, lanes]
            shifted = pl.ds(pl.multiple_of(1024 + 256 * i, 256), 256)
            ds[1 - own, t, where, :] = full[shifted, lanes]

    loop(5, hand_out)


def back_reduce(
    dext, xh1, inv1, norms, rowst, wsp, small_in, dnorm2, dnorm3, out, spreads, work, dh1,
):
    small = norms[...].astype(F32)
    gain, bias = vector(small, 0, 2), vector(small, 2, 2)
    inv = inv1[0:1, :]
    mask = row_mask(256)
    edges(spreads)

    def widen(c, carry):
        where = pl.ds(pl.multiple_of(c * 128 + 128, 128), 128)
        spread(spreads, c, dext[where, :].astype(F32), mask)
        return carry

    lax.fori_loop(0, STEPS, widen, 0)

    def conv(c, carry):
        d = jnp.zeros((128, 256), F32)
        for dy in range(3):
            where = pl.ds(pl.multiple_of(c * 128 + (2 - dy) * LINE, LINE), 128)
            for dx in range(3):
                tap = 256 * (3 * dy + dx)
                lanes = 256 * (2 - dx)
                d = d + dot_nt(spreads[where, lanes : lanes + 256], wsp[tap : tap + 256, :])
        work[at(c), :] = d
        return carry

    lax.fori_loop(0, STEPS, conv, 0)
    dbias, dgain = bn_back(work, xh1, gain, bias, inv, mask)
    out[2048:2560, :] = small_in[0:512, :]
    parts = [v[:, 128 * t : 128 * t + 128] for v in (dgain, dbias) for t in range(2)]
    parts = parts + [dnorm2[0:4, :], dnorm3[...], jnp.zeros((8, 128), F32)]
    out[2560:2592, :] = jnp.concatenate(parts, axis=0).astype(BF)
    scale = gain * inv
    level, tilt = dbias / PIX, dgain / PIX

    def one(c, carry):
        d = scale * (work[at(c), :] - level - xh1[at(c), :] * tilt) * mask
        dh1[at(c), :] = d.astype(BF)
        return carry

    lax.fori_loop(0, STEPS, one, 0)

    def weigh(m):
        piece = dot(rowst[at(m, 256), :], dh1[...]).astype(BF)
        for t in range(2):
            start = pl.multiple_of(1024 * t + 256 * m, 256)
            out[pl.ds(start, 256), :] = piece[:, 128 * t : 128 * t + 128]

    loop(4, weigh)


def finish(
    role, flat_p, flat_m, peer, r_own, r_peer, s0_own, s0_peer, s1_own, s1_peer, e_own, e_peer, small_own, small_peer,
    out_p, out_m, grad, buf_p, buf_m, turn, sems,
):
    own = role[0]
    copies = [
        pltpu.make_async_copy(flat_p.reshape(LROWS, 128), buf_p.at[pl.ds(0, LROWS)], sems.at[0]),
        pltpu.make_async_copy(flat_m.reshape(LROWS, 128), buf_m.at[pl.ds(0, LROWS)], sems.at[1]),
    ]
    for copy in copies:
        copy.start()

    def both(a, b, start, size):
        where = pl.ds(pl.multiple_of(start, 16), size)
        return a[where, :].astype(F32) + b[where, :].astype(F32)

    def place(a, b, source, start, stride, size, chunk):
        def body(i):
            where = pl.ds(start + i * chunk * stride, chunk, stride=stride)
            grad[where, :] = both(a, b, source + i * chunk, chunk)

        loop(size // chunk, body)

    @pl.when(own < 2)
    def _():
        for t, (mine, theirs) in enumerate(((s0_own, s0_peer), (s1_own, s1_peer))):
            place(mine, theirs, 0, jnp.where(own == 0, OFF + 2048, 10) + t, 2, 1280, 256)

    @pl.when(own == 0)
    def _():
        for t in range(2):
            place(r_own, r_peer, 1024 * t, OFF + t, 2, 1024, 256)

    @pl.when(own == 1)
    def _():
        def body(j):
            place(e_own, e_peer, 256 * j, OFF + 2474 + j, 8, 256, 256)

        loop(8, body)

    @pl.when(own >= 2)
    def _():
        group, start = jnp.where(own == 2, 0, 30), jnp.where(own == 2, 436, 4)
        parts = []
        for ref in (small_own, small_peer):
            for i in range(4):
                tiles = [
                    ref[416 + 128 * i + 16 * t : 432 + 128 * i + 16 * t, :].astype(F32)
                    for t in range(8)
                ]
                parts.append(jnp.concatenate(tiles, axis=1))

        def pack(start):
            tiles = [part[start : start + 8, :] for part in parts]
            pairs = [tiles[i] + pltpu.roll(tiles[i + 1], 4, 0) for i in range(0, 8, 2)]
            return jnp.concatenate(pairs, axis=0)

        pooled = jnp.concatenate([pack(0), jnp.zeros((96, 1024), F32)], axis=0)
        turn[0:1024, :] = pooled.T
        turn[1024:1152, :] = jnp.zeros((128, 128), F32)
        dl = jnp.concatenate([pack(8), jnp.zeros((32, 128), F32)], axis=1)

        def clear(i):
            grad[at(i, 64), :] = jnp.zeros((64, 128), F32)

        loop(85, clear, 5)

        def product(j):
            first, shift = window_of(j)
            moved = pltpu.roll(dl, shift, 1).astype(BF)
            left = turn[pl.ds(16 * group + j, 40, stride=16), :].astype(BF)
            wide = dot(left[:, 0:32], moved)
            for i in range(9):
                where = pl.ds(start + first + i, 40, stride=125)
                grad[where, :] = grad[where, :] + wide[:, 128 * i : 128 * i + 128]

        loop(16, product, 4)

    @pl.when(own == 2)
    def _():
        def body(j):
            place(small_own, small_peer, 48 * j, 52 + j, 8, 48, 48)

        loop(8, body)

    @pl.when(own == 3)
    def _():
        grad[OFF + 4158 : OFF + 4182, :] = both(small_own, small_peer, 384, 32)[0:24, :]

    for copy in copies:
        copy.wait()

    def piece(where, second, shifted):
        g = grad[shifted, :] * 0.25
        decayed = MOMENTUM_RATE * buf_m[where, :]
        p = 0.5 * ((buf_p[where, :] - LEARN_RATE * decayed) + peer[where, :].astype(F32))
        m = 0.5 * (decayed + peer[second, :].astype(F32))
        buf_p[where, :] = p - (0.5 * LEARN_RATE) * g
        buf_m[where, :] = m + 0.5 * g

    def body(i):
        piece(
            at(i, 32),
            pl.ds(pl.multiple_of(i * 32 + GROWS, 32), 32),
            pl.ds(pl.multiple_of(i * 32 + OFF, 32), 32),
        )

    loop(131, body)
    copies = [
        pltpu.make_async_copy(buf_p.at[pl.ds(0, LROWS)], out_p.reshape(LROWS, 128), sems.at[0]),
        pltpu.make_async_copy(buf_m.at[pl.ds(0, LROWS)], out_m.reshape(LROWS, 128), sems.at[1]),
    ]
    for copy in copies:
        copy.start()
    for copy in copies:
        copy.wait()


def along(value, pairs):
    return lax.ppermute(value, "local", pairs)


CORE = [(l, l ^ 1) for l in range(4)]
CHIP = [(l, l ^ 2) for l in range(4)]


def add(a, b):
    return (a.astype(F32) + b.astype(F32)).astype(BF)


def whole_step(images, labels, params, momentum, distance):
    nodes = lax.axis_size("node")
    index = lax.axis_index("local")
    role = index.astype(jnp.int32).reshape(1)
    dma = pltpu.SemaphoreType.DMA
    on_y = distance in (1, 4)

    def ahead(value, members):
        pairs = [
            (n * 4 + l, ((n + distance) % nodes) * 4 + l) for n in range(nodes) for l in members
        ]
        return lax.ppermute(value, ("node", "local"), pairs)

    sent_a, sent_b = call(
        prepare, "prepare", [SM, ANY], [shape((PART_A, 128), BF), shape((PART_B, 128), BF)],
        [pltpu.VMEM((5008, 128), F32), dma],
    )(role, params)
    across_a, across_b = along(sent_a, CHIP), along(sent_b, CHIP)
    beside_a, beside_b = along(sent_a, CORE), along(sent_b, CORE)

    params_later, _ = lax.optimization_barrier((params, sent_a))
    early = call(
        prepare_gossip, "prepare_gossip", [ANY, ANY], shape((2 * GROWS, 128), BF),
        [pltpu.VMEM((GROWS, 128), F32), pltpu.VMEM((GROWS, 128), F32), dma((2,))],
    )(params_later, momentum)
    rows = jnp.transpose(images, (1, 2, 0, 3))
    rows = jnp.pad(rows, ((0, 0), (0, 2), (0, 0), (0, 0))).reshape(ROWS, 1024)
    rowst = call(turned, "turn_rows", [VM], shape((1024, ROWS), BF), [])(rows)
    across_a, rows, rowst, _ = lax.optimization_barrier((across_a, rows, rowst, early))
    diagonal_a = along(across_a, CORE)

    xh1, inv1, padded, norms = call(
        first_layer, "first_layer", [SM, VM] + [ANY] * 4,
        [
            shape((ROWS, 256), F32), shape((8, 256), F32), shape((1024, 768), BF),
            shape((32, 128), BF),
        ],
        [pltpu.VMEM((2048, 128), BF), pltpu.VMEM((32, 128), BF), dma((2,))],
    )(role, rows, sent_a, beside_a, across_a, diagonal_a)

    padt = call(turned, "turn_padded", [VM], shape((768, 1024), BF), [])(padded)
    across_b, _, _ = lax.optimization_barrier((across_b, padt, xh1))
    diagonal_b = along(across_b, CORE)
    early, _ = lax.optimization_barrier((early, across_b if on_y else across_a))
    peer = ahead(early, range(4))
    whole = pltpu.VMEM((SENT, 128), BF)
    de, dsec, xh2, inv2, wsp, small, dnorm3 = call(
        middle, "middle", [SM, SM, VM, VM, VM] + [ANY] * 8,
        [
            shape((2048, 128), BF), shape((ROWS, 256), F32), shape((ROWS, 256), F32),
            shape((8, 256), F32), shape((2304, 256), BF), shape((544, 128), BF),
            shape((16, 128), F32),
        ],
        [
            pltpu.VMEM((2560, 128), BF), whole, whole, whole,
            pltpu.VMEM((256, 1024), BF), pltpu.VMEM((ROWS, 1024), F32),
            pltpu.VMEM((ROWS, 1024), BF), pltpu.VMEM((ROWS, 256), BF),
            pltpu.VMEM((256, ROWS), BF), pltpu.VMEM((1024, 128), F32),
            pltpu.VMEM((256, 128), F32), pltpu.VMEM((2000, 128), F32), dma((7,)),
        ],
    )(
        role, labels, rows, padded, norms, sent_a, beside_a, across_a, diagonal_a,
        sent_b, beside_b, across_b, diagonal_b,
    )
    e_core = add(de, along(de, [(0, 1), (2, 3)]))
    e_across = along(e_core, [(3, 1)])
    e_own = add(e_core, e_across)
    e_peer = ahead(e_own, [1])

    ds, dext, dnorm2 = call(
        back_spatial, "back_spatial", [SM, VM, VM, VM, VM, VM],
        [shape((2, 2, 1280, 128), BF), shape((1152, 256), BF), shape((8, 128), F32)],
        [pltpu.VMEM((ROWS, 256), F32), pltpu.VMEM((2304, 256), BF)],
    )(lax.rem(role, 2), dsec, xh2, inv2, norms, padt)
    s_beside = along(ds[1], CORE)
    s_own, s_peer, s_across = [], [], []
    for t in range(2):
        core = add(ds[0, t], s_beside[t])
        s_across.append(along(core, [(2, 0), (3, 1)]))
        s_own.append(add(core, s_across[t]))
        s_peer.append(ahead(s_own[t], [0, 1]))

    dext, _ = lax.optimization_barrier((dext, e_core))
    dwr = call(
        back_reduce, "back_reduce", [VM] * 9, shape((2592, 128), BF),
        [
            pltpu.VMEM((1024, 768), BF), pltpu.VMEM((ROWS, 256), F32), pltpu.VMEM((ROWS, 256), BF),
        ],
    )(dext, xh1, inv1, norms, rowst, wsp, small, dnorm2, dnorm3)
    dwr, _ = lax.optimization_barrier((dwr, (e_across, peer)))
    dwr_beside = along(dwr, CORE)
    r_core = add(dwr[0:2048], dwr_beside[0:2048])
    r_core, _ = lax.optimization_barrier((r_core, (e_peer, s_across[1])))
    r_own = add(r_core, along(r_core, [(2, 0)]))
    r_peer = ahead(r_own, [0])

    def tails_norms_pairs(a, b, count):
        start = a.shape[0] - 416 - 128 * count
        middle_a, middle_b = a[start + 384 : start + 384 + 128 * count], b[start + 384 : start + 384 + 128 * count]
        summed = add(
            jnp.concatenate([a[start : start + 384], a[-32:]], axis=0),
            jnp.concatenate([b[start : start + 384], b[-32:]], axis=0),
        )
        return summed, jnp.concatenate([middle_a, middle_b], axis=0)

    summed, pairs = tails_norms_pairs(dwr, dwr_beside, 1)
    small_chip = jnp.concatenate([summed, pairs], axis=0)
    small_across = along(small_chip, CHIP)
    small_own = jnp.concatenate(
        [add(summed, small_across[0:416]), pairs, small_across[416:672]], axis=0
    )
    small_peer = ahead(small_own, [2, 3])

    return call(
        finish, "finish", [SM, ANY, ANY] + [VM] * 11,
        [shape((1, LROWS * 128), F32)] * 2,
        [
            pltpu.VMEM((5440, 128), F32), pltpu.VMEM((GROWS, 128), F32),
            pltpu.VMEM((GROWS, 128), F32), pltpu.VMEM((1152, 128), F32), dma((2,)),
        ],
        out_specs=[ANY, ANY],
    )(
        role, params, momentum, peer, r_own, r_peer, s_own[0], s_peer[0], s_own[1], s_peer[1],
        e_own, e_peer,
        small_own, small_peer,
    )


def body(images, labels, params, momentum, step):
    degrees = lax.axis_size("node").bit_length() - 1
    branches = [functools.partial(whole_step, distance=1 << degree) for degree in range(degrees)]
    return tuple(lax.switch(step[0] % degrees, branches, images, labels, params, momentum))


def solution(mesh):
    in_specs = (
        P(("node", "local"), None, None, None),
        P(("node", "local")),
        P("node", "local"),
        P("node", "local"),
        P(),
    )
    out_specs = (P("node", "local"), P("node", "local"))
    return jax.shard_map(body, mesh=mesh, in_specs=in_specs, out_specs=out_specs, check_vma=False)
```

```python
import functools

import jax
import jax.numpy as jnp
from jax import lax
from jax.experimental import pallas as pl
from jax.experimental.pallas import tpu as pltpu
from jax.sharding import PartitionSpec as P

F32 = jnp.float32
BF = jnp.bfloat16

CLASSES = 1000
EPS = 1e-05
MOMENTUM_RATE = 0.9
LEARN_RATE = 0.1

LROWS = 4182
GROWS = 4192
OFF = 96
PIX = 784.0

ROWS = 896
LINE = 64
VALID = 56
STEPS = 7

WIDE = 9 * 128


PART_A = 2048
PART_B = 2560
SENT = PART_A + PART_B
NORMS = 2000
TAILS = 2000
SPILL = 2000

VMEM_LIMIT = 48 * 1024 * 1024

ANY = pl.BlockSpec(memory_space=pl.ANY)
VM = pl.BlockSpec(memory_space=pltpu.VMEM)
SM = pl.BlockSpec(memory_space=pltpu.SMEM)


def shape(dims, dtype):
    return jax.ShapeDtypeStruct(dims, dtype)


def call(kernel, name, in_specs, out_shape, scratch, out_specs=None):
    extra = {} if out_specs is None else {"out_specs": out_specs}
    return pl.pallas_call(
        kernel,
        name=name,
        in_specs=in_specs,
        out_shape=out_shape,
        scratch_shapes=scratch,
        compiler_params=pltpu.CompilerParams(vmem_limit_bytes=VMEM_LIMIT),
        cost_estimate=pl.CostEstimate(flops=1, bytes_accessed=1, transcendentals=0),
        **extra,
    )


def at(step, size=128):
    return pl.ds(pl.multiple_of(step * size, size), size)


def dot(a, b):
    return jnp.dot(a, b, preferred_element_type=F32)


def dot_nt(a, b):
    return lax.dot_general(a, b, (((1,), (1,)), ((), ())), preferred_element_type=F32)


def fold(values):
    rows, lanes = values.shape
    return jnp.sum(values.reshape(rows // 8, 8, lanes), axis=0)


def total(folded):
    return jnp.sum(folded, axis=0, keepdims=True)


def row_mask(lanes):
    rows = lax.broadcasted_iota(jnp.int32, (128, lanes), 0)
    return jnp.where(lax.rem(rows, LINE) < VALID, 1.0, 0.0).astype(F32)


def line_mask(lanes):
    rows = lax.broadcasted_iota(jnp.int32, (LINE, lanes), 0)
    return jnp.where(rows < VALID, 1.0, 0.0).astype(F32)


def slope(values):
    return jnp.where(values > 0.0, 1.0, jnp.where(values == 0.0, 0.5, 0.0))


def vector(norms, row, count):
    return jnp.concatenate([norms[row + i : row + i + 1, :] for i in range(count)], axis=1)


def window_of(j):
    return lax.div(125 * j, 16), 8 * lax.rem(125 * j, 16)


def loop(count, body, times=1):
    def step(i, carry):
        for k in range(times):
            body(i * times + k)
        return carry

    lax.fori_loop(0, count // times, step, 0)


def summed(count, body, start, times=1):
    def step(i, carry):
        for k in range(times):
            carry = body(i * times + k, carry)
        return carry

    return lax.fori_loop(0, count // times, step, start)


def choose(own, wanted, candidates, start, place, sem):
    for distance in range(4):

        @pl.when(lax.bitwise_xor(own, wanted) == distance)
        def _(source=candidates[distance]):
            pltpu.make_async_copy(source.at[pl.ds(start, place.shape[0])], place, sem).start()


def landed(candidates, start, place, sem):
    pltpu.make_async_copy(candidates[0].at[pl.ds(start, place.shape[0])], place, sem).wait()


def load_flat(flat, buf, sem):
    copy = pltpu.make_async_copy(flat.reshape(LROWS, 128), buf.at[pl.ds(OFF, LROWS)], sem)
    copy.start()
    buf[0:OFF, :] = jnp.zeros((OFF, 128), F32)
    end = OFF + LROWS
    buf[end : buf.shape[0], :] = jnp.zeros((buf.shape[0] - end, 128), F32)
    copy.wait()


def columns(buf, out, place, start, stride, size, chunk):
    def body(i):
        rows = buf[pl.ds(start + i * chunk * stride, chunk, stride=stride), :]
        out[pl.ds(pl.multiple_of(place + i * chunk, 16), chunk), :] = rows.astype(BF)

    loop(size // chunk, body)


def prepare(role, flat, out_a, out_b, buf, sem):
    load_flat(flat, buf, sem)
    own = role[0]

    @pl.when(own == 0)
    def _():
        for t in range(2):
            columns(buf, out_a, 1024 * t, OFF + t, 2, 1024, 256)
            columns(buf, out_b, 1280 * t, OFF + 2048 + t, 2, 1280, 256)

    @pl.when(own == 1)
    def _():
        columns(buf, out_a, 0, 10, 2, 1280, 256)
        columns(buf, out_a, 1280, 11, 2, 768, 256)
        columns(buf, out_b, 0, 11 + 2 * 768, 2, 512, 256)

        def body(j):
            columns(buf, out_b, 512 + 256 * j, OFF + 2474 + j, 8, 256, 256)

        loop(8, body)

    @pl.when(own >= 2)
    def _():
        start = jnp.where(own == 2, 436, 254)

        def body(k):
            for i in range(5):
                r = 5 * k + i
                where = pl.ds(pl.multiple_of(16 * r, 16), 16)
                for half, out in ((0, out_a), (1, out_b)):
                    rows = buf[pl.ds(start + half * 16 * 125 + r, 16, stride=125), :]
                    out[where, :] = rows.astype(BF)

        loop(25, body)
        out_a[2000:2048, :] = jnp.zeros((48, 128), BF)

    @pl.when(own == 2)
    def _():
        def body(j):
            columns(buf, out_b, TAILS + 48 * j, 52 + j, 8, 48, 48)

        loop(8, body)
        out_b[TAILS + 384 : PART_B, :] = jnp.zeros((176, 128), BF)

    @pl.when(own == 3)
    def _():
        out_a[NORMS : NORMS + 32, :] = buf[OFF + 4158 : OFF + 4190, :].astype(BF)
        out_b[SPILL : SPILL + 128, :] = buf[4:132, :].astype(BF)
        out_b[SPILL + 128 : SPILL + 256, :] = buf[129:257, :].astype(BF)
        out_b[SPILL + 256 : PART_B, :] = jnp.zeros((304, 128), BF)


def prepare_gossip(flat_p, flat_m, out_p, out_m, buf_p, buf_m, sems):
    copies = [
        pltpu.make_async_copy(flat_p.reshape(LROWS, 128), buf_p.at[pl.ds(0, LROWS)], sems.at[0]),
        pltpu.make_async_copy(flat_m.reshape(LROWS, 128), buf_m.at[pl.ds(0, LROWS)], sems.at[1]),
    ]
    for copy in copies:
        copy.start()
    for copy in copies:
        copy.wait()
    for buf in (buf_p, buf_m):
        buf[LROWS:GROWS, :] = jnp.zeros((GROWS - LROWS, 128), F32)

    def body(i):
        where = at(i, 32)
        decayed = MOMENTUM_RATE * buf_m[where, :]
        out_p[where, :] = (buf_p[where, :] - LEARN_RATE * decayed).astype(BF)
        out_m[where, :] = decayed.astype(BF)

    loop(131, body)


def turned(source, out):
    def body(c):
        out[:, at(c)] = source[at(c), :].T

    steps = source.shape[0] // 128
    loop(steps, body, steps if source.shape[1] == 256 else 1)


def spread(out, step, values, mask):
    where = pl.ds(pl.multiple_of(step * 128 + LINE, LINE), 128)
    out[where, 0:256] = (pltpu.roll(values, 4, 0) * mask).astype(BF)
    out[where, 256:512] = values.astype(BF)
    out[where, 512:768] = (pltpu.roll(values, 124, 0) * mask).astype(BF)


def edges(out):
    zeros = jnp.zeros((LINE, out.shape[1]), out.dtype)
    out[0:LINE, :] = zeros
    out[LINE + ROWS : 2 * LINE + ROWS, :] = zeros


def spread_of(values, mean):
    lanes = values.shape[1]
    mask = line_mask(lanes)

    def step(c, acc):
        centred = (values[at(c, LINE), :] - mean) * mask
        return acc + fold(centred * centred)

    return total(summed(ROWS // LINE, step, jnp.zeros((8, lanes), F32), 2))


def first_layer(role, rows, x0, x1, x2, x3, xh, inv_out, padded, norms_out, weight, norms, sems):
    cands = (x0, x1, x2, x3)
    choose(role[0], 0, cands, 0, weight, sems.at[0])
    choose(role[0], 3, cands, NORMS, norms, sems.at[1])
    edges(padded)
    mask = row_mask(256)
    landed(cands, NORMS, norms, sems.at[1])
    norms_out[...] = norms[...]
    small = norms[...].astype(F32)
    gain, bias = vector(small, 0, 2), vector(small, 2, 2)
    landed(cands, 0, weight, sems.at[0])

    def one(c, acc):
        w = jnp.concatenate([weight[0:1024, :], weight[1024:2048, :]], axis=1)
        h = dot(rows[at(c), :], w)
        xh[at(c), :] = h
        return acc + fold(h)

    mean = total(lax.fori_loop(0, STEPS, one, jnp.zeros((8, 256), F32))) / PIX
    inv = lax.rsqrt(spread_of(xh, mean) / PIX + EPS)
    inv_out[...] = jnp.broadcast_to(inv, (8, 256))

    def two(c, carry):
        hat = (xh[at(c), :] - mean) * inv * mask
        xh[at(c), :] = hat
        spread(padded, c, jnp.maximum(hat * gain + bias, 0.0) * mask, mask)
        return carry

    lax.fori_loop(0, STEPS, two, 0)


def middle(
    role, labels, rows, padded, norms, a0, a1, a2, a3, b0, b1, b2, b3,
    de, dsec, xh2, inv_out, wsp, small_out, dnorm,
    s0, s1, s2, s3, we, h3, dh3, sec, sect, turn, turn2, wide_buf, sems,
):
    own = role[0]
    part_a, part_b = (a0, a1, a2, a3), (b0, b1, b2, b3)
    plan = [(0, part_b, s0)]
    for wanted, whole in ((1, s1), (2, s2), (3, s3)):
        plan.append((wanted, part_a, whole.at[pl.ds(0, PART_A)]))
        plan.append((wanted, part_b, whole.at[pl.ds(PART_A, PART_B)]))
    for i, (wanted, cands, place) in enumerate(plan):
        choose(own, wanted, cands, 0, place, sems.at[i])
    mask = row_mask(256)
    small = norms[...].astype(F32)
    gain2, bias2 = vector(small, 4, 2), vector(small, 6, 2)
    gain3, bias3 = vector(small, 8, 8), vector(small, 16, 8)

    for i, (wanted, cands, place) in enumerate(plan):
        landed(cands, 0, place, sems.at[i])
    for t in range(2):
        lanes = slice(128 * t, 128 * t + 128)

        def below(i, t=t, lanes=lanes):
            wsp[at(i), lanes] = s0[pl.ds(pl.multiple_of(1280 * t + 128 * i, 128), 128), :]
            where = pl.ds(pl.multiple_of(1280 + 128 * i, 128), 128)
            wsp[where, lanes] = s1[pl.ds(pl.multiple_of(1280 * t + 256 + 128 * i, 128), 128), :]

        loop(8, below, 4)
        wsp[1024:1280, lanes] = (
            s0[1280 * t + 1024 : 1280 * t + 1280, :] + s1[1280 * t : 1280 * t + 256, :]
        )

    def across(j):
        low = 2560 + 256 * j
        we[0:208, at(j)] = s1[pl.ds(pl.multiple_of(low, 256), 208), :]
        we[208:256, at(j)] = (
            s1[pl.ds(pl.multiple_of(low + 208, 16), 48), :]
            + s2[pl.ds(pl.multiple_of(PART_A + TAILS + 48 * j, 16), 48), :]
        )

    loop(8, across, 4)

    def widen(i):
        wide_buf[at(i, 80), :] = s2[pl.ds(pl.multiple_of(2048 + 80 * i, 16), 80), :].astype(F32)

    def narrow(i):
        s2[pl.ds(pl.multiple_of(2048 + 80 * i, 16), 80), :] = wide_buf[at(i, 80), :].astype(BF)

    loop(25, widen, 5)
    for i in range(2):
        spill = s3[PART_A + SPILL + 128 * i : PART_A + SPILL + 128 * i + 128, :].astype(F32)[0:125, :]
        where = pl.ds(14 + i, 125, stride=16)
        wide_buf[where, :] = wide_buf[where, :] + spill
    loop(25, narrow, 5)

    def conv(c, acc):
        h = jnp.zeros((128, 256), F32)
        for dy in range(3):
            where = pl.ds(pl.multiple_of(c * 128 + dy * LINE, LINE), 128)
            h = h + dot(padded[where, :], wsp[768 * dy : 768 * dy + 768, :])
        xh2[at(c), :] = h
        return acc + fold(h)

    mean = total(lax.fori_loop(0, STEPS, conv, jnp.zeros((8, 256), F32))) / PIX
    inv = lax.rsqrt(spread_of(xh2, mean) / PIX + EPS)
    inv_out[...] = jnp.broadcast_to(inv, (8, 256))

    def expand(c, acc):
        hat = (xh2[at(c), :] - mean) * inv * mask
        xh2[at(c), :] = hat
        second = (jnp.maximum(hat * gain2 + bias2, 0.0) * mask).astype(BF)
        sec[at(c), :] = second
        h = dot(second, we[...])
        h3[at(c), :] = h
        return acc + fold(h)

    mean3 = total(lax.fori_loop(0, STEPS, expand, jnp.zeros((8, 1024), F32))) / PIX
    inv3 = lax.rsqrt(spread_of(h3, mean3) / PIX + EPS)

    def pool(c, carry):
        acc, count, weighed = carry
        hat = (h3[at(c, LINE), :] - mean3) * inv3
        h3[at(c, LINE), :] = hat
        out = hat * gain3 + bias3 + rows[at(c, LINE), :].astype(F32)
        on = slope(out) * real3
        return (
            acc + fold(jnp.maximum(out, 0.0) * real3),
            count + fold(on),
            weighed + fold(on * hat),
        )

    zero8 = jnp.zeros((8, 1024), F32)
    real3 = line_mask(1024)
    acc, count, weighed = summed(ROWS // LINE, pool, (zero8, zero8, zero8), 2)
    acc = (acc + pltpu.roll(acc, 4, 0)) / 196.0
    four = lax.broadcasted_iota(jnp.int32, (8, 1024), 0) < 4
    pooled = jnp.where(four, acc, 0.0).astype(BF).astype(F32)

    turn[...] = jnp.concatenate([pooled, jnp.zeros((120, 1024), F32)], axis=0).T

    def regroup(j):
        part = jnp.concatenate([turn[pl.ds(j, 64, stride=16), :], jnp.zeros((64, 128), F32)], axis=0)
        turn2[at(j, 16), :] = part.T[0:16, :]

    loop(16, regroup, 4)

    def window(first):
        tiles = []
        for i in range(9):
            parts = [
                s[pl.ds(pl.multiple_of(start + 16 * (first + i), 16), 16), :]
                for s in (s2, s3)
                for start in (0, 2048)
            ]
            tiles.append(jnp.concatenate(parts, axis=0))
        return jnp.concatenate(tiles, axis=1)

    def score(j, acc):
        first, shift = window_of(j)
        wide = dot(turn2[at(j, 16), 0:64].astype(BF), window(first))
        return acc + pltpu.roll(wide, WIDE - shift, 1)[:, 0:1024]

    logits = summed(16, score, jnp.zeros((16, 1024), F32), 4)
    lane = lax.broadcasted_iota(jnp.int32, (16, 1024), 1)
    image = lax.broadcasted_iota(jnp.int32, (16, 1024), 0)
    real = lane < CLASSES
    logits = jnp.where(real, logits, -1e30)
    top = jnp.max(logits, axis=1, keepdims=True)
    ex = jnp.where(real, jnp.exp(logits - top), 0.0)
    prob = ex / jnp.sum(ex, axis=1, keepdims=True)
    hot = jnp.zeros((16, 1024), jnp.bool_)
    for i in range(4):
        hot = hot | ((image == i) & (lane == labels[i]))
    dl = jnp.where(image < 4, (prob - jnp.where(hot, 1.0, 0.0)) * 0.25, 0.0)
    pair = jnp.concatenate([pooled, dl[0:8, :]], axis=0).astype(BF)
    for t in range(8):
        small_out[384 + 16 * t : 400 + 16 * t, :] = pair[:, 128 * t : 128 * t + 128]
    dl = jnp.concatenate([dl, jnp.zeros((16, 128), F32)], axis=1)

    def unscore(j):
        first, shift = window_of(j)
        moved = pltpu.roll(dl, shift, 1).astype(BF)
        moved = jnp.concatenate([moved, jnp.zeros((112, WIDE), BF)], axis=0)
        turn[pl.ds(j, 64, stride=16), :] = dot_nt(window(first), moved)

    loop(16, unscore, 4)
    dpool = turn[...].T[0:8, :] / 196.0
    dpool = jnp.where(four, dpool, pltpu.roll(dpool, 4, 0))

    dbias3 = total(count * dpool)
    dgain3 = total(weighed * dpool)
    for j in range(8):
        dnorm[j : j + 1, :] = dgain3[:, 128 * j : 128 * j + 128]
        dnorm[8 + j : 9 + j, :] = dbias3[:, 128 * j : 128 * j + 128]
    scale = gain3 * inv3
    level = scale * dbias3 / PIX
    tilt = scale * dgain3 / PIX
    steep = scale * dpool

    def back(c):
        hat = h3[at(c, LINE), :]
        on = slope(hat * gain3 + bias3 + rows[at(c, LINE), :].astype(F32))
        step = (on.reshape(8, 8, 1024) * steep[None]).reshape(LINE, 1024)
        dh3[at(c, LINE), :] = (step - level - hat * tilt).astype(BF)

    loop(ROWS // LINE, back, 2)
    turned(sec, sect)

    def weigh(n):
        right = dh3[:, at(n, 256)]
        piece = dot(sect[...], right).astype(BF)
        for t in range(2):
            half = piece[:, 128 * t : 128 * t + 128]
            de[pl.ds(pl.multiple_of(512 * n + 256 * t, 128), 256), :] = half
            small_out[pl.ds(pl.multiple_of(96 * n + 48 * t, 16), 48), :] = half[208:256, :]

    loop(4, weigh, 2)
    small_out[512:544, :] = jnp.zeros((32, 128), BF)

    def down(c, carry):
        dsec[at(c), :] = dot_nt(dh3[at(c), :], we[...])
        return carry

    lax.fori_loop(0, STEPS, down, 0)


def bn_back(dy, xh, gain, bias, inv, mask):
    def sums(c, carry):
        hat = xh[at(c), :]
        d = dy[at(c), :] * slope(hat * gain + bias) * mask
        dy[at(c), :] = d
        return (carry[0] + fold(d), carry[1] + fold(d * hat))

    zero = jnp.zeros((8, 256), F32)
    a, b = lax.fori_loop(0, STEPS, sums, (zero, zero))
    return total(a), total(b)


def back_spatial(role, dsec, xh2, inv2, norms, padt, ds, dext, dnorm, work, full):
    own = role[0]
    small = norms[...].astype(F32)
    gain, bias = vector(small, 4, 2), vector(small, 6, 2)
    inv = inv2[0:1, :]
    mask = row_mask(256)

    def take(c, carry):
        work[at(c), :] = dsec[at(c), :]
        return carry

    lax.fori_loop(0, STEPS, take, 0)
    dbias, dgain = bn_back(work, xh2, gain, bias, inv, mask)
    for t in range(2):
        dnorm[t : t + 1, :] = dgain[:, 128 * t : 128 * t + 128]
        dnorm[2 + t : 3 + t, :] = dbias[:, 128 * t : 128 * t + 128]
    dnorm[4:8, :] = jnp.zeros((4, 128), F32)
    dext[0:128, :] = jnp.zeros((128, 256), BF)
    dext[1024:1152, :] = jnp.zeros((128, 256), BF)
    scale = gain * inv
    level, tilt = dbias / PIX, dgain / PIX

    def one(c, carry):
        d = scale * (work[at(c), :] - level - xh2[at(c), :] * tilt) * mask
        dext[pl.ds(pl.multiple_of(c * 128 + 128, 128), 128), :] = d.astype(BF)
        return carry

    lax.fori_loop(0, STEPS, one, 0)

    def weigh(dy):
        right = dext[pl.ds(pl.multiple_of(128 - LINE * dy, LINE), 1024), :]
        for m in range(2):
            piece = dot(padt[384 * m : 384 * m + 384, :], right).astype(BF)
            full[pl.ds(pl.multiple_of(768 * dy + 384 * m, 128), 384), :] = piece

    loop(3, weigh)

    def hand_out(i):
        for t in range(2):
            lanes = slice(128 * t, 128 * t + 128)
            where = at(i, 256)
            place = pl.ds(pl.multiple_of(1280 * t + 256 * i, 256), 256)
            ds[own, place, :] = full[where, lanes]
            shifted = pl.ds(pl.multiple_of(1024 + 256 * i, 256), 256)
            ds[1 - own, place, :] = full[shifted, lanes]

    loop(5, hand_out)


def back_reduce(
    dext, xh1, inv1, norms, rowst, wsp, small_in, dnorm2, dnorm3, out, spreads, work, dh1,
):
    small = norms[...].astype(F32)
    gain, bias = vector(small, 0, 2), vector(small, 2, 2)
    inv = inv1[0:1, :]
    mask = row_mask(256)
    edges(spreads)

    def widen(c, carry):
        where = pl.ds(pl.multiple_of(c * 128 + 128, 128), 128)
        spread(spreads, c, dext[where, :].astype(F32), mask)
        return carry

    lax.fori_loop(0, STEPS, widen, 0)

    def conv(c, carry):
        d = jnp.zeros((128, 256), F32)
        for dy in range(3):
            where = pl.ds(pl.multiple_of(c * 128 + (2 - dy) * LINE, LINE), 128)
            for dx in range(3):
                tap = 256 * (3 * dy + dx)
                lanes = 256 * (2 - dx)
                d = d + dot_nt(spreads[where, lanes : lanes + 256], wsp[tap : tap + 256, :])
        work[at(c), :] = d
        return carry

    lax.fori_loop(0, STEPS, conv, 0)
    dbias, dgain = bn_back(work, xh1, gain, bias, inv, mask)
    out[2048:2560, :] = small_in[0:512, :]
    parts = [v[:, 128 * t : 128 * t + 128] for v in (dgain, dbias) for t in range(2)]
    parts = parts + [dnorm2[0:4, :], dnorm3[...], jnp.zeros((8, 128), F32)]
    out[2560:2592, :] = jnp.concatenate(parts, axis=0).astype(BF)
    scale = gain * inv
    level, tilt = dbias / PIX, dgain / PIX

    def one(c, carry):
        d = scale * (work[at(c), :] - level - xh1[at(c), :] * tilt) * mask
        dh1[at(c), :] = d.astype(BF)
        return carry

    lax.fori_loop(0, STEPS, one, 0)

    def weigh(m):
        piece = dot(rowst[at(m, 256), :], dh1[...]).astype(BF)
        for t in range(2):
            start = pl.multiple_of(1024 * t + 256 * m, 256)
            out[pl.ds(start, 256), :] = piece[:, 128 * t : 128 * t + 128]

    loop(4, weigh)


def finish(
    role, flat_p, flat_m, peer_p, peer_m, r_own, r_peer, s_own, s_peer, e_own, e_peer, small_own, small_peer,
    out_p, out_m, grad, buf_p, buf_m, turn, sems,
):
    own = role[0]
    copies = [
        pltpu.make_async_copy(flat_p.reshape(LROWS, 128), buf_p.at[pl.ds(0, LROWS)], sems.at[0]),
        pltpu.make_async_copy(flat_m.reshape(LROWS, 128), buf_m.at[pl.ds(0, LROWS)], sems.at[1]),
    ]
    for copy in copies:
        copy.start()

    def both(a, b, start, size):
        where = pl.ds(pl.multiple_of(start, 16), size)
        return a[where, :].astype(F32) + b[where, :].astype(F32)

    def place(a, b, source, start, stride, size, chunk):
        def body(i):
            where = pl.ds(start + i * chunk * stride, chunk, stride=stride)
            grad[where, :] = both(a, b, source + i * chunk, chunk)

        loop(size // chunk, body)

    @pl.when(own < 2)
    def _():
        for t in range(2):
            place(s_own, s_peer, 1280 * t, jnp.where(own == 0, OFF + 2048, 10) + t, 2, 1280, 256)

    @pl.when(own == 0)
    def _():
        for t in range(2):
            place(r_own, r_peer, 1024 * t, OFF + t, 2, 1024, 256)

    @pl.when(own == 1)
    def _():
        def body(j):
            place(e_own, e_peer, 256 * j, OFF + 2474 + j, 8, 256, 256)

        loop(8, body)

    @pl.when(own >= 2)
    def _():
        group, start = jnp.where(own == 2, 0, 30), jnp.where(own == 2, 436, 4)
        parts = []
        for ref in (small_own, small_peer):
            for i in range(4):
                tiles = [
                    ref[416 + 128 * i + 16 * t : 432 + 128 * i + 16 * t, :].astype(F32)
                    for t in range(8)
                ]
                parts.append(jnp.concatenate(tiles, axis=1))

        def pack(start):
            tiles = [part[start : start + 8, :] for part in parts]
            pairs = [tiles[i] + pltpu.roll(tiles[i + 1], 4, 0) for i in range(0, 8, 2)]
            return jnp.concatenate(pairs, axis=0)

        pooled = jnp.concatenate([pack(0), jnp.zeros((96, 1024), F32)], axis=0)
        turn[0:1024, :] = pooled.T
        turn[1024:1152, :] = jnp.zeros((128, 128), F32)
        dl = jnp.concatenate([pack(8), jnp.zeros((32, 128), F32)], axis=1)

        def clear(i):
            grad[at(i, 64), :] = jnp.zeros((64, 128), F32)

        loop(85, clear, 5)

        def product(j):
            first, shift = window_of(j)
            moved = pltpu.roll(dl, shift, 1).astype(BF)
            left = turn[pl.ds(16 * group + j, 40, stride=16), :].astype(BF)
            wide = dot(left[:, 0:32], moved)
            for i in range(9):
                where = pl.ds(start + first + i, 40, stride=125)
                grad[where, :] = grad[where, :] + wide[:, 128 * i : 128 * i + 128]

        loop(16, product, 4)

    @pl.when(own == 2)
    def _():
        def body(j):
            place(small_own, small_peer, 48 * j, 52 + j, 8, 48, 48)

        loop(8, body)

    @pl.when(own == 3)
    def _():
        grad[OFF + 4158 : OFF + 4182, :] = both(small_own, small_peer, 384, 32)[0:24, :]

    for copy in copies:
        copy.wait()

    def piece(where, shifted):
        g = grad[shifted, :] * 0.25
        decayed = MOMENTUM_RATE * buf_m[where, :]
        p = 0.5 * ((buf_p[where, :] - LEARN_RATE * decayed) + peer_p[where, :].astype(F32))
        m = 0.5 * (decayed + peer_m[where, :].astype(F32))
        buf_p[where, :] = p - (0.5 * LEARN_RATE) * g
        buf_m[where, :] = m + 0.5 * g

    def body(i):
        piece(
            at(i, 32),
            pl.ds(pl.multiple_of(i * 32 + OFF, 32), 32),
        )

    loop(131, body)
    copies = [
        pltpu.make_async_copy(buf_p.at[pl.ds(0, LROWS)], out_p.reshape(LROWS, 128), sems.at[0]),
        pltpu.make_async_copy(buf_m.at[pl.ds(0, LROWS)], out_m.reshape(LROWS, 128), sems.at[1]),
    ]
    for copy in copies:
        copy.start()
    for copy in copies:
        copy.wait()


def along(value, pairs):
    return lax.ppermute(value, "local", pairs)


CORE = [(l, l ^ 1) for l in range(4)]
CHIP = [(l, l ^ 2) for l in range(4)]


def add(a, b):
    return (a.astype(F32) + b.astype(F32)).astype(BF)


def whole_step(images, labels, params, momentum, distance):
    nodes = lax.axis_size("node")
    index = lax.axis_index("local")
    role = index.astype(jnp.int32).reshape(1)
    dma = pltpu.SemaphoreType.DMA
    on_y = distance in (1, 4)

    def ahead(value, members):
        pairs = [
            (n * 4 + l, ((n + distance) % nodes) * 4 + l) for n in range(nodes) for l in members
        ]
        return lax.ppermute(value, ("node", "local"), pairs)

    sent_a, sent_b = call(
        prepare, "prepare", [SM, ANY], [shape((PART_A, 128), BF), shape((PART_B, 128), BF)],
        [pltpu.VMEM((5008, 128), F32), dma],
    )(role, params)
    across_a, across_b = along(sent_a, CHIP), along(sent_b, CHIP)
    beside_a, beside_b = along(sent_a, CORE), along(sent_b, CORE)

    params_later, _ = lax.optimization_barrier((params, sent_a))
    early_p, early_m = call(
        prepare_gossip, "prepare_gossip", [ANY, ANY], [shape((GROWS, 128), BF)] * 2,
        [pltpu.VMEM((GROWS, 128), F32), pltpu.VMEM((GROWS, 128), F32), dma((2,))],
    )(params_later, momentum)
    rows = jnp.transpose(images, (1, 2, 0, 3))
    rows = jnp.pad(rows, ((0, 0), (0, 2), (0, 0), (0, 0))).reshape(ROWS, 1024)
    rowst = call(turned, "turn_rows", [VM], shape((1024, ROWS), BF), [])(rows)
    across_a, rows, rowst, _ = lax.optimization_barrier((across_a, rows, rowst, early_p))
    diagonal_a = along(across_a, CORE)

    xh1, inv1, padded, norms = call(
        first_layer, "first_layer", [SM, VM] + [ANY] * 4,
        [
            shape((ROWS, 256), F32), shape((8, 256), F32), shape((1024, 768), BF),
            shape((32, 128), BF),
        ],
        [pltpu.VMEM((2048, 128), BF), pltpu.VMEM((32, 128), BF), dma((2,))],
    )(role, rows, sent_a, beside_a, across_a, diagonal_a)

    padt = call(turned, "turn_padded", [VM], shape((768, 1024), BF), [])(padded)
    across_b, _, _ = lax.optimization_barrier((across_b, padt, xh1))
    diagonal_b = along(across_b, CORE)
    gathered = across_b if on_y else across_a
    early_p, early_m, _ = lax.optimization_barrier((early_p, early_m, gathered))
    peer_p = ahead(early_p, range(4))
    if on_y:
        early_m, _ = lax.optimization_barrier((early_m, peer_p))
    peer_m = ahead(early_m, range(4))
    whole = pltpu.VMEM((SENT, 128), BF)
    de, dsec, xh2, inv2, wsp, small, dnorm3 = call(
        middle, "middle", [SM, SM, VM, VM, VM] + [ANY] * 8,
        [
            shape((2048, 128), BF), shape((ROWS, 256), F32), shape((ROWS, 256), F32),
            shape((8, 256), F32), shape((2304, 256), BF), shape((544, 128), BF),
            shape((16, 128), F32),
        ],
        [
            pltpu.VMEM((2560, 128), BF), whole, whole, whole,
            pltpu.VMEM((256, 1024), BF), pltpu.VMEM((ROWS, 1024), F32),
            pltpu.VMEM((ROWS, 1024), BF), pltpu.VMEM((ROWS, 256), BF),
            pltpu.VMEM((256, ROWS), BF), pltpu.VMEM((1024, 128), F32),
            pltpu.VMEM((256, 128), F32), pltpu.VMEM((2000, 128), F32), dma((7,)),
        ],
    )(
        role, labels, rows, padded, norms, sent_a, beside_a, across_a, diagonal_a,
        sent_b, beside_b, across_b, diagonal_b,
    )
    e_core = add(de, along(de, [(0, 1), (2, 3)]))
    e_across = along(e_core, [(3, 1)])
    e_own = add(e_core, e_across)
    e_peer = ahead(e_own, [1])

    ds, dext, dnorm2 = call(
        back_spatial, "back_spatial", [SM, VM, VM, VM, VM, VM],
        [shape((2, 2560, 128), BF), shape((1152, 256), BF), shape((8, 128), F32)],
        [pltpu.VMEM((ROWS, 256), F32), pltpu.VMEM((2304, 256), BF)],
    )(lax.rem(role, 2), dsec, xh2, inv2, norms, padt)
    s_core = add(ds[0], along(ds[1], CORE))
    s_across = along(s_core, [(2, 0), (3, 1)])
    s_own = add(s_core, s_across)
    s_peer = ahead(s_own, [0, 1])

    dext, _ = lax.optimization_barrier((dext, (e_core, peer_p) if on_y else e_core))
    dwr = call(
        back_reduce, "back_reduce", [VM] * 9, shape((2592, 128), BF),
        [
            pltpu.VMEM((1024, 768), BF), pltpu.VMEM((ROWS, 256), F32), pltpu.VMEM((ROWS, 256), BF),
        ],
    )(dext, xh1, inv1, norms, rowst, wsp, small, dnorm2, dnorm3)
    dwr, _ = lax.optimization_barrier((dwr, e_across if on_y else (e_across, peer_p, peer_m)))
    dwr_beside = along(dwr, CORE)
    r_core = add(dwr[0:2048], dwr_beside[0:2048])
    r_core, _ = lax.optimization_barrier((r_core, (e_peer, s_across, peer_m) if on_y else (e_peer, s_across)))
    r_own = add(r_core, along(r_core, [(2, 0)]))
    r_peer = ahead(r_own, [0])

    def tails_norms_pairs(a, b, count):
        start = a.shape[0] - 416 - 128 * count
        middle_a, middle_b = a[start + 384 : start + 384 + 128 * count], b[start + 384 : start + 384 + 128 * count]
        summed = add(
            jnp.concatenate([a[start : start + 384], a[-32:]], axis=0),
            jnp.concatenate([b[start : start + 384], b[-32:]], axis=0),
        )
        return summed, jnp.concatenate([middle_a, middle_b], axis=0)

    summed, pairs = tails_norms_pairs(dwr, dwr_beside, 1)
    small_chip = jnp.concatenate([summed, pairs], axis=0)
    small_across = along(small_chip, CHIP)
    small_own = jnp.concatenate(
        [add(summed, small_across[0:416]), pairs, small_across[416:672]], axis=0
    )
    small_peer = ahead(small_own, [2, 3])

    return call(
        finish, "finish", [SM, ANY, ANY] + [VM] * 10,
        [shape((1, LROWS * 128), F32)] * 2,
        [
            pltpu.VMEM((5440, 128), F32), pltpu.VMEM((GROWS, 128), F32),
            pltpu.VMEM((GROWS, 128), F32), pltpu.VMEM((1152, 128), F32), dma((2,)),
        ],
        out_specs=[ANY, ANY],
    )(
        role, params, momentum, peer_p, peer_m, r_own, r_peer, s_own, s_peer, e_own, e_peer,
        small_own, small_peer,
    )


def body(images, labels, params, momentum, step):
    degrees = lax.axis_size("node").bit_length() - 1
    branches = [functools.partial(whole_step, distance=1 << degree) for degree in range(degrees)]
    return tuple(lax.switch(step[0] % degrees, branches, images, labels, params, momentum))


def solution(mesh):
    in_specs = (
        P(("node", "local"), None, None, None),
        P(("node", "local")),
        P("node", "local"),
        P("node", "local"),
        P(),
    )
    out_specs = (P("node", "local"), P("node", "local"))
    return jax.shard_map(body, mesh=mesh, in_specs=in_specs, out_specs=out_specs, check_vma=False)
```

```python
import functools

import jax
import jax.numpy as jnp
from jax import lax
from jax.experimental import pallas as pl
from jax.experimental.pallas import tpu as pltpu
from jax.sharding import PartitionSpec as P

F32 = jnp.float32
BF = jnp.bfloat16

CLASSES = 1000
EPS = 1e-05
MOMENTUM_RATE = 0.9
LEARN_RATE = 0.1

LROWS = 4182
GROWS = 4192
OFF = 96
PIX = 784.0

ROWS = 896
LINE = 64
VALID = 56
STEPS = 7

WIDE = 9 * 128


PART_A = 2048
PART_B = 2560
SENT = PART_A + PART_B
NORMS = 2000
TAILS = 2000
SPILL = 2000

VMEM_LIMIT = 48 * 1024 * 1024

ANY = pl.BlockSpec(memory_space=pl.ANY)
VM = pl.BlockSpec(memory_space=pltpu.VMEM)
SM = pl.BlockSpec(memory_space=pltpu.SMEM)


def shape(dims, dtype):
    return jax.ShapeDtypeStruct(dims, dtype)


def call(kernel, name, in_specs, out_shape, scratch, out_specs=None):
    extra = {} if out_specs is None else {"out_specs": out_specs}
    return pl.pallas_call(
        kernel,
        name=name,
        in_specs=in_specs,
        out_shape=out_shape,
        scratch_shapes=scratch,
        compiler_params=pltpu.CompilerParams(vmem_limit_bytes=VMEM_LIMIT),
        cost_estimate=pl.CostEstimate(flops=1, bytes_accessed=1, transcendentals=0),
        **extra,
    )


def at(step, size=128):
    return pl.ds(pl.multiple_of(step * size, size), size)


def dot(a, b):
    return jnp.dot(a, b, preferred_element_type=F32)


def dot_nt(a, b):
    return lax.dot_general(a, b, (((1,), (1,)), ((), ())), preferred_element_type=F32)


def fold(values):
    rows, lanes = values.shape
    return jnp.sum(values.reshape(rows // 8, 8, lanes), axis=0)


def total(folded):
    return jnp.sum(folded, axis=0, keepdims=True)


def row_mask(lanes):
    rows = lax.broadcasted_iota(jnp.int32, (128, lanes), 0)
    return jnp.where(lax.rem(rows, LINE) < VALID, 1.0, 0.0).astype(F32)


def line_mask(lanes):
    rows = lax.broadcasted_iota(jnp.int32, (LINE, lanes), 0)
    return jnp.where(rows < VALID, 1.0, 0.0).astype(F32)


def slope(values):
    return jnp.where(values > 0.0, 1.0, jnp.where(values == 0.0, 0.5, 0.0))


def vector(norms, row, count):
    return jnp.concatenate([norms[row + i : row + i + 1, :] for i in range(count)], axis=1)


def window_of(j):
    return lax.div(125 * j, 16), 8 * lax.rem(125 * j, 16)


def loop(count, body, times=1):
    def step(i, carry):
        for k in range(times):
            body(i * times + k)
        return carry

    lax.fori_loop(0, count // times, step, 0)


def summed(count, body, start, times=1):
    def step(i, carry):
        for k in range(times):
            carry = body(i * times + k, carry)
        return carry

    return lax.fori_loop(0, count // times, step, start)


def choose(own, wanted, candidates, start, place, sem):
    for distance in range(4):

        @pl.when(lax.bitwise_xor(own, wanted) == distance)
        def _(source=candidates[distance]):
            pltpu.make_async_copy(source.at[pl.ds(start, place.shape[0])], place, sem).start()


def landed(candidates, start, place, sem):
    pltpu.make_async_copy(candidates[0].at[pl.ds(start, place.shape[0])], place, sem).wait()


def load_flat(flat, buf, sem):
    copy = pltpu.make_async_copy(flat.reshape(LROWS, 128), buf.at[pl.ds(OFF, LROWS)], sem)
    copy.start()
    buf[0:OFF, :] = jnp.zeros((OFF, 128), F32)
    end = OFF + LROWS
    buf[end : buf.shape[0], :] = jnp.zeros((buf.shape[0] - end, 128), F32)
    copy.wait()


def columns(buf, out, place, start, stride, size, chunk):
    def body(i):
        rows = buf[pl.ds(start + i * chunk * stride, chunk, stride=stride), :]
        out[pl.ds(pl.multiple_of(place + i * chunk, 16), chunk), :] = rows.astype(BF)

    loop(size // chunk, body)


def prepare(role, flat, out_a, out_b, buf, sem):
    load_flat(flat, buf, sem)
    own = role[0]

    @pl.when(own == 0)
    def _():
        for t in range(2):
            columns(buf, out_a, 1024 * t, OFF + t, 2, 1024, 256)
            columns(buf, out_b, 1280 * t, OFF + 2048 + t, 2, 1280, 256)

    @pl.when(own == 1)
    def _():
        columns(buf, out_a, 0, 10, 2, 1280, 256)
        columns(buf, out_a, 1280, 11, 2, 768, 256)
        columns(buf, out_b, 0, 11 + 2 * 768, 2, 512, 256)

        def body(j):
            columns(buf, out_b, 512 + 256 * j, OFF + 2474 + j, 8, 256, 256)

        loop(8, body)

    @pl.when(own >= 2)
    def _():
        start = jnp.where(own == 2, 436, 254)

        def body(k):
            for i in range(5):
                r = 5 * k + i
                where = pl.ds(pl.multiple_of(16 * r, 16), 16)
                for half, out in ((0, out_a), (1, out_b)):
                    rows = buf[pl.ds(start + half * 16 * 125 + r, 16, stride=125), :]
                    out[where, :] = rows.astype(BF)

        loop(25, body)
        out_a[2000:2048, :] = jnp.zeros((48, 128), BF)

    @pl.when(own == 2)
    def _():
        def body(j):
            columns(buf, out_b, TAILS + 48 * j, 52 + j, 8, 48, 48)

        loop(8, body)
        out_b[TAILS + 384 : PART_B, :] = jnp.zeros((176, 128), BF)

    @pl.when(own == 3)
    def _():
        out_a[NORMS : NORMS + 32, :] = buf[OFF + 4158 : OFF + 4190, :].astype(BF)
        out_b[SPILL : SPILL + 128, :] = buf[4:132, :].astype(BF)
        out_b[SPILL + 128 : SPILL + 256, :] = buf[129:257, :].astype(BF)
        out_b[SPILL + 256 : PART_B, :] = jnp.zeros((304, 128), BF)


def prepare_gossip(flat_p, flat_m, out_p, out_m, buf_p, buf_m, sems):
    copies = [
        pltpu.make_async_copy(flat_p.reshape(LROWS, 128), buf_p.at[pl.ds(0, LROWS)], sems.at[0]),
        pltpu.make_async_copy(flat_m.reshape(LROWS, 128), buf_m.at[pl.ds(0, LROWS)], sems.at[1]),
    ]
    for copy in copies:
        copy.start()
    for copy in copies:
        copy.wait()
    for buf in (buf_p, buf_m):
        buf[LROWS:GROWS, :] = jnp.zeros((GROWS - LROWS, 128), F32)

    def body(i):
        where = at(i, 32)
        decayed = MOMENTUM_RATE * buf_m[where, :]
        out_p[where, :] = (buf_p[where, :] - LEARN_RATE * decayed).astype(BF)
        out_m[where, :] = decayed.astype(BF)

    loop(131, body)


def turned(source, out):
    def body(c):
        out[:, at(c)] = source[at(c), :].T

    steps = source.shape[0] // 128
    loop(steps, body, steps if source.shape[1] == 256 else 1)


def spread(out, step, values, mask):
    where = pl.ds(pl.multiple_of(step * 128 + LINE, LINE), 128)
    out[where, 0:256] = (pltpu.roll(values, 4, 0) * mask).astype(BF)
    out[where, 256:512] = values.astype(BF)
    out[where, 512:768] = (pltpu.roll(values, 124, 0) * mask).astype(BF)


def edges(out):
    zeros = jnp.zeros((LINE, out.shape[1]), out.dtype)
    out[0:LINE, :] = zeros
    out[LINE + ROWS : 2 * LINE + ROWS, :] = zeros


def spread_of(values, mean):
    lanes = values.shape[1]
    mask = line_mask(lanes)

    def step(c, acc):
        centred = (values[at(c, LINE), :] - mean) * mask
        return acc + fold(centred * centred)

    return total(summed(ROWS // LINE, step, jnp.zeros((8, lanes), F32), 2))


def first_layer(role, rows, x0, x1, x2, x3, xh, inv_out, padded, norms_out, weight, norms, sems):
    cands = (x0, x1, x2, x3)
    choose(role[0], 0, cands, 0, weight, sems.at[0])
    choose(role[0], 3, cands, NORMS, norms, sems.at[1])
    edges(padded)
    mask = row_mask(256)
    landed(cands, NORMS, norms, sems.at[1])
    norms_out[...] = norms[...]
    small = norms[...].astype(F32)
    gain, bias = vector(small, 0, 2), vector(small, 2, 2)
    landed(cands, 0, weight, sems.at[0])

    def one(c, acc):
        w = jnp.concatenate([weight[0:1024, :], weight[1024:2048, :]], axis=1)
        h = dot(rows[at(c), :], w)
        xh[at(c), :] = h
        return acc + fold(h)

    mean = total(lax.fori_loop(0, STEPS, one, jnp.zeros((8, 256), F32))) / PIX
    inv = lax.rsqrt(spread_of(xh, mean) / PIX + EPS)
    inv_out[...] = jnp.broadcast_to(inv, (8, 256))

    def two(c, carry):
        hat = (xh[at(c), :] - mean) * inv * mask
        xh[at(c), :] = hat
        spread(padded, c, jnp.maximum(hat * gain + bias, 0.0) * mask, mask)
        return carry

    lax.fori_loop(0, STEPS, two, 0)


def middle(
    role, labels, rows, padded, norms, a0, a1, a2, a3, b0, b1, b2, b3,
    de, dsec, xh2, inv_out, wsp, small_out, dnorm,
    s0, s1, s2, s3, we, h3, dh3, sec, sect, turn, turn2, wide_buf, sems,
):
    own = role[0]
    part_a, part_b = (a0, a1, a2, a3), (b0, b1, b2, b3)
    plan = [(0, part_b, s0)]
    for wanted, whole in ((1, s1), (2, s2), (3, s3)):
        plan.append((wanted, part_a, whole.at[pl.ds(0, PART_A)]))
        plan.append((wanted, part_b, whole.at[pl.ds(PART_A, PART_B)]))
    for i, (wanted, cands, place) in enumerate(plan):
        choose(own, wanted, cands, 0, place, sems.at[i])
    mask = row_mask(256)
    small = norms[...].astype(F32)
    gain2, bias2 = vector(small, 4, 2), vector(small, 6, 2)
    gain3, bias3 = vector(small, 8, 8), vector(small, 16, 8)

    for i, (wanted, cands, place) in enumerate(plan):
        landed(cands, 0, place, sems.at[i])
    for t in range(2):
        lanes = slice(128 * t, 128 * t + 128)

        def below(i, t=t, lanes=lanes):
            wsp[at(i), lanes] = s0[pl.ds(pl.multiple_of(1280 * t + 128 * i, 128), 128), :]
            where = pl.ds(pl.multiple_of(1280 + 128 * i, 128), 128)
            wsp[where, lanes] = s1[pl.ds(pl.multiple_of(1280 * t + 256 + 128 * i, 128), 128), :]

        loop(8, below, 4)
        wsp[1024:1280, lanes] = (
            s0[1280 * t + 1024 : 1280 * t + 1280, :] + s1[1280 * t : 1280 * t + 256, :]
        )

    def across(j):
        low = 2560 + 256 * j
        we[0:208, at(j)] = s1[pl.ds(pl.multiple_of(low, 256), 208), :]
        we[208:256, at(j)] = (
            s1[pl.ds(pl.multiple_of(low + 208, 16), 48), :]
            + s2[pl.ds(pl.multiple_of(PART_A + TAILS + 48 * j, 16), 48), :]
        )

    loop(8, across, 4)

    def widen(i):
        wide_buf[at(i, 80), :] = s2[pl.ds(pl.multiple_of(2048 + 80 * i, 16), 80), :].astype(F32)

    def narrow(i):
        s2[pl.ds(pl.multiple_of(2048 + 80 * i, 16), 80), :] = wide_buf[at(i, 80), :].astype(BF)

    loop(25, widen, 5)
    for i in range(2):
        spill = s3[PART_A + SPILL + 128 * i : PART_A + SPILL + 128 * i + 128, :].astype(F32)[0:125, :]
        where = pl.ds(14 + i, 125, stride=16)
        wide_buf[where, :] = wide_buf[where, :] + spill
    loop(25, narrow, 5)

    def conv(c, acc):
        h = jnp.zeros((128, 256), F32)
        for dy in range(3):
            where = pl.ds(pl.multiple_of(c * 128 + dy * LINE, LINE), 128)
            h = h + dot(padded[where, :], wsp[768 * dy : 768 * dy + 768, :])
        xh2[at(c), :] = h
        return acc + fold(h)

    mean = total(lax.fori_loop(0, STEPS, conv, jnp.zeros((8, 256), F32))) / PIX
    inv = lax.rsqrt(spread_of(xh2, mean) / PIX + EPS)
    inv_out[...] = jnp.broadcast_to(inv, (8, 256))

    def expand(c, acc):
        hat = (xh2[at(c), :] - mean) * inv * mask
        xh2[at(c), :] = hat
        second = (jnp.maximum(hat * gain2 + bias2, 0.0) * mask).astype(BF)
        sec[at(c), :] = second
        h = dot(second, we[...])
        h3[at(c), :] = h
        return acc + fold(h)

    mean3 = total(lax.fori_loop(0, STEPS, expand, jnp.zeros((8, 1024), F32))) / PIX
    inv3 = lax.rsqrt(spread_of(h3, mean3) / PIX + EPS)

    def pool(c, carry):
        acc, count, weighed = carry
        hat = (h3[at(c, LINE), :] - mean3) * inv3
        h3[at(c, LINE), :] = hat
        out = hat * gain3 + bias3 + rows[at(c, LINE), :].astype(F32)
        on = slope(out) * real3
        return (
            acc + fold(jnp.maximum(out, 0.0) * real3),
            count + fold(on),
            weighed + fold(on * hat),
        )

    zero8 = jnp.zeros((8, 1024), F32)
    real3 = line_mask(1024)
    acc, count, weighed = summed(ROWS // LINE, pool, (zero8, zero8, zero8), 2)
    acc = (acc + pltpu.roll(acc, 4, 0)) / 196.0
    four = lax.broadcasted_iota(jnp.int32, (8, 1024), 0) < 4
    pooled = jnp.where(four, acc, 0.0).astype(BF).astype(F32)

    turn[...] = jnp.concatenate([pooled, jnp.zeros((120, 1024), F32)], axis=0).T

    def regroup(j):
        part = jnp.concatenate([turn[pl.ds(j, 64, stride=16), :], jnp.zeros((64, 128), F32)], axis=0)
        turn2[at(j, 16), :] = part.T[0:16, :]

    loop(16, regroup, 4)

    def window(first):
        tiles = []
        for i in range(9):
            parts = [
                s[pl.ds(pl.multiple_of(start + 16 * (first + i), 16), 16), :]
                for s in (s2, s3)
                for start in (0, 2048)
            ]
            tiles.append(jnp.concatenate(parts, axis=0))
        return jnp.concatenate(tiles, axis=1)

    def score(j, acc):
        first, shift = window_of(j)
        wide = dot(turn2[at(j, 16), 0:64].astype(BF), window(first))
        return acc + pltpu.roll(wide, WIDE - shift, 1)[:, 0:1024]

    logits = summed(16, score, jnp.zeros((16, 1024), F32), 4)
    lane = lax.broadcasted_iota(jnp.int32, (16, 1024), 1)
    image = lax.broadcasted_iota(jnp.int32, (16, 1024), 0)
    real = lane < CLASSES
    logits = jnp.where(real, logits, -1e30)
    top = jnp.max(logits, axis=1, keepdims=True)
    ex = jnp.where(real, jnp.exp(logits - top), 0.0)
    prob = ex / jnp.sum(ex, axis=1, keepdims=True)
    hot = jnp.zeros((16, 1024), jnp.bool_)
    for i in range(4):
        hot = hot | ((image == i) & (lane == labels[i]))
    dl = jnp.where(image < 4, (prob - jnp.where(hot, 1.0, 0.0)) * 0.25, 0.0)
    pair = jnp.concatenate([pooled, dl[0:8, :]], axis=0).astype(BF)
    for t in range(8):
        small_out[384 + 16 * t : 400 + 16 * t, :] = pair[:, 128 * t : 128 * t + 128]
    dl = jnp.concatenate([dl, jnp.zeros((16, 128), F32)], axis=1)

    def unscore(j):
        first, shift = window_of(j)
        moved = pltpu.roll(dl, shift, 1).astype(BF)
        moved = jnp.concatenate([moved, jnp.zeros((112, WIDE), BF)], axis=0)
        turn[pl.ds(j, 64, stride=16), :] = dot_nt(window(first), moved)

    loop(16, unscore, 4)
    dpool = turn[...].T[0:8, :] / 196.0
    dpool = jnp.where(four, dpool, pltpu.roll(dpool, 4, 0))

    dbias3 = total(count * dpool)
    dgain3 = total(weighed * dpool)
    for j in range(8):
        dnorm[j : j + 1, :] = dgain3[:, 128 * j : 128 * j + 128]
        dnorm[8 + j : 9 + j, :] = dbias3[:, 128 * j : 128 * j + 128]
    scale = gain3 * inv3
    level = scale * dbias3 / PIX
    tilt = scale * dgain3 / PIX
    steep = scale * dpool

    def back(c):
        hat = h3[at(c, LINE), :]
        on = slope(hat * gain3 + bias3 + rows[at(c, LINE), :].astype(F32))
        step = (on.reshape(8, 8, 1024) * steep[None]).reshape(LINE, 1024)
        dh3[at(c, LINE), :] = (step - level - hat * tilt).astype(BF)

    loop(ROWS // LINE, back, 2)
    turned(sec, sect)

    def weigh(n):
        right = dh3[:, at(n, 256)]
        piece = dot(sect[...], right).astype(BF)
        for t in range(2):
            half = piece[:, 128 * t : 128 * t + 128]
            de[pl.ds(pl.multiple_of(512 * n + 256 * t, 128), 256), :] = half
            small_out[pl.ds(pl.multiple_of(96 * n + 48 * t, 16), 48), :] = half[208:256, :]

    loop(4, weigh, 2)
    small_out[512:544, :] = jnp.zeros((32, 128), BF)

    def down(c, carry):
        dsec[at(c), :] = dot_nt(dh3[at(c), :], we[...])
        return carry

    lax.fori_loop(0, STEPS, down, 0)


def bn_back(dy, xh, gain, bias, inv, mask):
    def sums(c, carry):
        hat = xh[at(c), :]
        d = dy[at(c), :] * slope(hat * gain + bias) * mask
        dy[at(c), :] = d
        return (carry[0] + fold(d), carry[1] + fold(d * hat))

    zero = jnp.zeros((8, 256), F32)
    a, b = lax.fori_loop(0, STEPS, sums, (zero, zero))
    return total(a), total(b)


def back_spatial(role, dsec, xh2, inv2, norms, padt, ds, dext, dnorm, work, full):
    own = role[0]
    small = norms[...].astype(F32)
    gain, bias = vector(small, 4, 2), vector(small, 6, 2)
    inv = inv2[0:1, :]
    mask = row_mask(256)

    def take(c, carry):
        work[at(c), :] = dsec[at(c), :]
        return carry

    lax.fori_loop(0, STEPS, take, 0)
    dbias, dgain = bn_back(work, xh2, gain, bias, inv, mask)
    for t in range(2):
        dnorm[t : t + 1, :] = dgain[:, 128 * t : 128 * t + 128]
        dnorm[2 + t : 3 + t, :] = dbias[:, 128 * t : 128 * t + 128]
    dnorm[4:8, :] = jnp.zeros((4, 128), F32)
    dext[0:128, :] = jnp.zeros((128, 256), BF)
    dext[1024:1152, :] = jnp.zeros((128, 256), BF)
    scale = gain * inv
    level, tilt = dbias / PIX, dgain / PIX

    def one(c, carry):
        d = scale * (work[at(c), :] - level - xh2[at(c), :] * tilt) * mask
        dext[pl.ds(pl.multiple_of(c * 128 + 128, 128), 128), :] = d.astype(BF)
        return carry

    lax.fori_loop(0, STEPS, one, 0)

    def weigh(dy):
        right = dext[pl.ds(pl.multiple_of(128 - LINE * dy, LINE), 1024), :]
        for m in range(2):
            piece = dot(padt[384 * m : 384 * m + 384, :], right).astype(BF)
            full[pl.ds(pl.multiple_of(768 * dy + 384 * m, 128), 384), :] = piece

    loop(3, weigh)

    def hand_out(i):
        for t in range(2):
            lanes = slice(128 * t, 128 * t + 128)
            where = at(i, 256)
            place = pl.ds(pl.multiple_of(1280 * t + 256 * i, 256), 256)
            ds[own, place, :] = full[where, lanes]
            shifted = pl.ds(pl.multiple_of(1024 + 256 * i, 256), 256)
            ds[1 - own, place, :] = full[shifted, lanes]

    loop(5, hand_out)


def back_reduce(
    dext, xh1, inv1, norms, rowst, wsp, small_in, dnorm2, dnorm3, out, spreads, work, dh1,
):
    small = norms[...].astype(F32)
    gain, bias = vector(small, 0, 2), vector(small, 2, 2)
    inv = inv1[0:1, :]
    mask = row_mask(256)
    edges(spreads)

    def widen(c, carry):
        where = pl.ds(pl.multiple_of(c * 128 + 128, 128), 128)
        spread(spreads, c, dext[where, :].astype(F32), mask)
        return carry

    lax.fori_loop(0, STEPS, widen, 0)

    def conv(c, carry):
        d = jnp.zeros((128, 256), F32)
        for dy in range(3):
            where = pl.ds(pl.multiple_of(c * 128 + (2 - dy) * LINE, LINE), 128)
            for dx in range(3):
                tap = 256 * (3 * dy + dx)
                lanes = 256 * (2 - dx)
                d = d + dot_nt(spreads[where, lanes : lanes + 256], wsp[tap : tap + 256, :])
        work[at(c), :] = d
        return carry

    lax.fori_loop(0, STEPS, conv, 0)
    dbias, dgain = bn_back(work, xh1, gain, bias, inv, mask)
    out[2048:2560, :] = small_in[0:512, :]
    parts = [v[:, 128 * t : 128 * t + 128] for v in (dgain, dbias) for t in range(2)]
    parts = parts + [dnorm2[0:4, :], dnorm3[...], jnp.zeros((8, 128), F32)]
    out[2560:2592, :] = jnp.concatenate(parts, axis=0).astype(BF)
    scale = gain * inv
    level, tilt = dbias / PIX, dgain / PIX

    def one(c, carry):
        d = scale * (work[at(c), :] - level - xh1[at(c), :] * tilt) * mask
        dh1[at(c), :] = d.astype(BF)
        return carry

    lax.fori_loop(0, STEPS, one, 0)

    def weigh(m):
        piece = dot(rowst[at(m, 256), :], dh1[...]).astype(BF)
        for t in range(2):
            start = pl.multiple_of(1024 * t + 256 * m, 256)
            out[pl.ds(start, 256), :] = piece[:, 128 * t : 128 * t + 128]

    loop(4, weigh)


def finish(
    role, flat_p, flat_m, peer_p, peer_m, r_own, r_peer, s_own, s_peer, e_own, e_peer, small_own, small_peer,
    out_p, out_m, grad, buf_p, buf_m, turn, sems,
):
    own = role[0]
    copies = [
        pltpu.make_async_copy(flat_p.reshape(LROWS, 128), buf_p.at[pl.ds(0, LROWS)], sems.at[0]),
        pltpu.make_async_copy(flat_m.reshape(LROWS, 128), buf_m.at[pl.ds(0, LROWS)], sems.at[1]),
    ]
    for copy in copies:
        copy.start()

    def both(a, b, start, size):
        where = pl.ds(pl.multiple_of(start, 16), size)
        return a[where, :].astype(F32) + b[where, :].astype(F32)

    def place(a, b, source, start, stride, size, chunk):
        def body(i):
            where = pl.ds(start + i * chunk * stride, chunk, stride=stride)
            grad[where, :] = both(a, b, source + i * chunk, chunk)

        loop(size // chunk, body)

    @pl.when(own < 2)
    def _():
        for t in range(2):
            place(s_own, s_peer, 1280 * t, jnp.where(own == 0, OFF + 2048, 10) + t, 2, 1280, 256)

    @pl.when(own == 0)
    def _():
        for t in range(2):
            place(r_own, r_peer, 1024 * t, OFF + t, 2, 1024, 256)

    @pl.when(own == 1)
    def _():
        def body(j):
            place(e_own, e_peer, 256 * j, OFF + 2474 + j, 8, 256, 256)

        loop(8, body)

    @pl.when(own >= 2)
    def _():
        group, start = jnp.where(own == 2, 0, 30), jnp.where(own == 2, 436, 4)
        parts = []
        for ref in (small_own, small_peer):
            for i in range(4):
                tiles = [
                    ref[416 + 128 * i + 16 * t : 432 + 128 * i + 16 * t, :].astype(F32)
                    for t in range(8)
                ]
                parts.append(jnp.concatenate(tiles, axis=1))

        def pack(start):
            tiles = [part[start : start + 8, :] for part in parts]
            pairs = [tiles[i] + pltpu.roll(tiles[i + 1], 4, 0) for i in range(0, 8, 2)]
            return jnp.concatenate(pairs, axis=0)

        pooled = jnp.concatenate([pack(0), jnp.zeros((96, 1024), F32)], axis=0)
        turn[0:1024, :] = pooled.T
        turn[1024:1152, :] = jnp.zeros((128, 128), F32)
        dl = jnp.concatenate([pack(8), jnp.zeros((32, 128), F32)], axis=1)

        def clear(i):
            grad[at(i, 64), :] = jnp.zeros((64, 128), F32)

        loop(85, clear, 5)

        def product(j):
            first, shift = window_of(j)
            moved = pltpu.roll(dl, shift, 1).astype(BF)
            left = turn[pl.ds(16 * group + j, 40, stride=16), :].astype(BF)
            wide = dot(left[:, 0:32], moved)
            for i in range(9):
                where = pl.ds(start + first + i, 40, stride=125)
                grad[where, :] = grad[where, :] + wide[:, 128 * i : 128 * i + 128]

        loop(16, product, 4)

    @pl.when(own == 2)
    def _():
        def body(j):
            place(small_own, small_peer, 48 * j, 52 + j, 8, 48, 48)

        loop(8, body)

    @pl.when(own == 3)
    def _():
        grad[OFF + 4158 : OFF + 4182, :] = both(small_own, small_peer, 384, 32)[0:24, :]

    for copy in copies:
        copy.wait()

    def piece(where, shifted):
        g = grad[shifted, :] * 0.25
        decayed = MOMENTUM_RATE * buf_m[where, :]
        p = 0.5 * ((buf_p[where, :] - LEARN_RATE * decayed) + peer_p[where, :].astype(F32))
        m = 0.5 * (decayed + peer_m[where, :].astype(F32))
        buf_p[where, :] = p - (0.5 * LEARN_RATE) * g
        buf_m[where, :] = m + 0.5 * g

    def body(i):
        piece(
            at(i, 32),
            pl.ds(pl.multiple_of(i * 32 + OFF, 32), 32),
        )

    loop(131, body)
    copies = [
        pltpu.make_async_copy(buf_p.at[pl.ds(0, LROWS)], out_p.reshape(LROWS, 128), sems.at[0]),
        pltpu.make_async_copy(buf_m.at[pl.ds(0, LROWS)], out_m.reshape(LROWS, 128), sems.at[1]),
    ]
    for copy in copies:
        copy.start()
    for copy in copies:
        copy.wait()


def along(value, pairs):
    return lax.ppermute(value, "local", pairs)


CORE = [(l, l ^ 1) for l in range(4)]
CHIP = [(l, l ^ 2) for l in range(4)]


def add(a, b):
    return (a.astype(F32) + b.astype(F32)).astype(BF)


def whole_step(images, labels, params, momentum, distance):
    nodes = lax.axis_size("node")
    index = lax.axis_index("local")
    role = index.astype(jnp.int32).reshape(1)
    dma = pltpu.SemaphoreType.DMA
    on_y = distance in (1, 4)

    def ahead(value, members):
        pairs = [
            (n * 4 + l, ((n + distance) % nodes) * 4 + l) for n in range(nodes) for l in members
        ]
        return lax.ppermute(value, ("node", "local"), pairs)

    sent_a, sent_b = call(
        prepare, "prepare", [SM, ANY], [shape((PART_A, 128), BF), shape((PART_B, 128), BF)],
        [pltpu.VMEM((5008, 128), F32), dma],
    )(role, params)
    across_a, across_b = along(sent_a, CHIP), along(sent_b, CHIP)
    beside_a, beside_b = along(sent_a, CORE), along(sent_b, CORE)

    params_later, _ = lax.optimization_barrier((params, sent_a))
    early_p, early_m = call(
        prepare_gossip, "prepare_gossip", [ANY, ANY], [shape((GROWS, 128), BF)] * 2,
        [pltpu.VMEM((GROWS, 128), F32), pltpu.VMEM((GROWS, 128), F32), dma((2,))],
    )(params_later, momentum)
    rows = jnp.transpose(images, (1, 2, 0, 3))
    rows = jnp.pad(rows, ((0, 0), (0, 2), (0, 0), (0, 0))).reshape(ROWS, 1024)
    rowst = call(turned, "turn_rows", [VM], shape((1024, ROWS), BF), [])(rows)
    across_a, rows, rowst, _ = lax.optimization_barrier((across_a, rows, rowst, early_p))
    diagonal_a = along(across_a, CORE)

    xh1, inv1, padded, norms = call(
        first_layer, "first_layer", [SM, VM] + [ANY] * 4,
        [
            shape((ROWS, 256), F32), shape((8, 256), F32), shape((1024, 768), BF),
            shape((32, 128), BF),
        ],
        [pltpu.VMEM((2048, 128), BF), pltpu.VMEM((32, 128), BF), dma((2,))],
    )(role, rows, sent_a, beside_a, across_a, diagonal_a)

    padt = call(turned, "turn_padded", [VM], shape((768, 1024), BF), [])(padded)
    across_b, _, _ = lax.optimization_barrier((across_b, padt, xh1))
    diagonal_b = along(across_b, CORE)
    gathered = across_b if on_y else across_a
    early_p, early_m, _ = lax.optimization_barrier((early_p, early_m, gathered))
    peer_p = ahead(early_p, range(4))
    if not on_y:
        early_m, _ = lax.optimization_barrier((early_m, peer_p))
    peer_m = ahead(early_m, range(4))
    whole = pltpu.VMEM((SENT, 128), BF)
    de, dsec, xh2, inv2, wsp, small, dnorm3 = call(
        middle, "middle", [SM, SM, VM, VM, VM] + [ANY] * 8,
        [
            shape((2048, 128), BF), shape((ROWS, 256), F32), shape((ROWS, 256), F32),
            shape((8, 256), F32), shape((2304, 256), BF), shape((544, 128), BF),
            shape((16, 128), F32),
        ],
        [
            pltpu.VMEM((2560, 128), BF), whole, whole, whole,
            pltpu.VMEM((256, 1024), BF), pltpu.VMEM((ROWS, 1024), F32),
            pltpu.VMEM((ROWS, 1024), BF), pltpu.VMEM((ROWS, 256), BF),
            pltpu.VMEM((256, ROWS), BF), pltpu.VMEM((1024, 128), F32),
            pltpu.VMEM((256, 128), F32), pltpu.VMEM((2000, 128), F32), dma((7,)),
        ],
    )(
        role, labels, rows, padded, norms, sent_a, beside_a, across_a, diagonal_a,
        sent_b, beside_b, across_b, diagonal_b,
    )
    e_core = add(de, along(de, [(0, 1), (2, 3)]))
    e_across = along(e_core, [(3, 1)])
    e_own = add(e_core, e_across)
    e_peer = ahead(e_own, [1])

    ds, dext, dnorm2 = call(
        back_spatial, "back_spatial", [SM, VM, VM, VM, VM, VM],
        [shape((2, 2560, 128), BF), shape((1152, 256), BF), shape((8, 128), F32)],
        [pltpu.VMEM((ROWS, 256), F32), pltpu.VMEM((2304, 256), BF)],
    )(lax.rem(role, 2), dsec, xh2, inv2, norms, padt)
    s_core = add(ds[0], along(ds[1], CORE))
    s_across = along(s_core, [(2, 0), (3, 1)])
    s_own = add(s_core, s_across)
    s_peer = ahead(s_own, [0, 1])

    dext, _ = lax.optimization_barrier((dext, e_core if on_y else (e_core, peer_p)))
    dwr = call(
        back_reduce, "back_reduce", [VM] * 9, shape((2592, 128), BF),
        [
            pltpu.VMEM((1024, 768), BF), pltpu.VMEM((ROWS, 256), F32), pltpu.VMEM((ROWS, 256), BF),
        ],
    )(dext, xh1, inv1, norms, rowst, wsp, small, dnorm2, dnorm3)
    dwr, _ = lax.optimization_barrier((dwr, (e_across, peer_p, peer_m) if on_y else e_across))
    dwr_beside = along(dwr, CORE)
    r_core = add(dwr[0:2048], dwr_beside[0:2048])
    r_core, _ = lax.optimization_barrier((r_core, (e_peer, s_across) if on_y else (e_peer, s_across, peer_m)))
    r_own = add(r_core, along(r_core, [(2, 0)]))
    r_peer = ahead(r_own, [0])

    def tails_norms_pairs(a, b, count):
        start = a.shape[0] - 416 - 128 * count
        middle_a, middle_b = a[start + 384 : start + 384 + 128 * count], b[start + 384 : start + 384 + 128 * count]
        summed = add(
            jnp.concatenate([a[start : start + 384], a[-32:]], axis=0),
            jnp.concatenate([b[start : start + 384], b[-32:]], axis=0),
        )
        return summed, jnp.concatenate([middle_a, middle_b], axis=0)

    summed, pairs = tails_norms_pairs(dwr, dwr_beside, 1)
    small_chip = jnp.concatenate([summed, pairs], axis=0)
    small_across = along(small_chip, CHIP)
    small_own = jnp.concatenate(
        [add(summed, small_across[0:416]), pairs, small_across[416:672]], axis=0
    )
    small_peer = ahead(small_own, [2, 3])

    return call(
        finish, "finish", [SM, ANY, ANY] + [VM] * 10,
        [shape((1, LROWS * 128), F32)] * 2,
        [
            pltpu.VMEM((5440, 128), F32), pltpu.VMEM((GROWS, 128), F32),
            pltpu.VMEM((GROWS, 128), F32), pltpu.VMEM((1152, 128), F32), dma((2,)),
        ],
        out_specs=[ANY, ANY],
    )(
        role, params, momentum, peer_p, peer_m, r_own, r_peer, s_own, s_peer, e_own, e_peer,
        small_own, small_peer,
    )


def body(images, labels, params, momentum, step):
    degrees = lax.axis_size("node").bit_length() - 1
    branches = [functools.partial(whole_step, distance=1 << degree) for degree in range(degrees)]
    return tuple(lax.switch(step[0] % degrees, branches, images, labels, params, momentum))


def solution(mesh):
    in_specs = (
        P(("node", "local"), None, None, None),
        P(("node", "local")),
        P("node", "local"),
        P("node", "local"),
        P(),
    )
    out_specs = (P("node", "local"), P("node", "local"))
    return jax.shard_map(body, mesh=mesh, in_specs=in_specs, out_specs=out_specs, check_vma=False)
```

```python
import functools

import jax
import jax.numpy as jnp
from jax import lax
from jax.experimental import pallas as pl
from jax.experimental.pallas import tpu as pltpu
from jax.sharding import PartitionSpec as P

F32 = jnp.float32
BF = jnp.bfloat16

CLASSES = 1000
EPS = 1e-05
MOMENTUM_RATE = 0.9
LEARN_RATE = 0.1

LROWS = 4182
GROWS = 4192
OFF = 96
PIX = 784.0

ROWS = 896
LINE = 64
VALID = 56
STEPS = 7

WIDE = 9 * 128


PART_A = 2048
PART_B = 2560
SENT = PART_A + PART_B
NORMS = 2000
TAILS = 2000
SPILL = 2000

VMEM_LIMIT = 48 * 1024 * 1024

ANY = pl.BlockSpec(memory_space=pl.ANY)
VM = pl.BlockSpec(memory_space=pltpu.VMEM)
SM = pl.BlockSpec(memory_space=pltpu.SMEM)


def shape(dims, dtype):
    return jax.ShapeDtypeStruct(dims, dtype)


def call(kernel, name, in_specs, out_shape, scratch, out_specs=None):
    extra = {} if out_specs is None else {"out_specs": out_specs}
    return pl.pallas_call(
        kernel,
        name=name,
        in_specs=in_specs,
        out_shape=out_shape,
        scratch_shapes=scratch,
        compiler_params=pltpu.CompilerParams(vmem_limit_bytes=VMEM_LIMIT),
        cost_estimate=pl.CostEstimate(flops=1, bytes_accessed=1, transcendentals=0),
        **extra,
    )


def at(step, size=128):
    return pl.ds(pl.multiple_of(step * size, size), size)


def dot(a, b):
    return jnp.dot(a, b, preferred_element_type=F32)


def dot_nt(a, b):
    return lax.dot_general(a, b, (((1,), (1,)), ((), ())), preferred_element_type=F32)


def fold(values):
    rows, lanes = values.shape
    return jnp.sum(values.reshape(rows // 8, 8, lanes), axis=0)


def total(folded):
    return jnp.sum(folded, axis=0, keepdims=True)


def row_mask(lanes):
    rows = lax.broadcasted_iota(jnp.int32, (128, lanes), 0)
    return jnp.where(lax.rem(rows, LINE) < VALID, 1.0, 0.0).astype(F32)


def line_mask(lanes):
    rows = lax.broadcasted_iota(jnp.int32, (LINE, lanes), 0)
    return jnp.where(rows < VALID, 1.0, 0.0).astype(F32)


def slope(values):
    return jnp.where(values > 0.0, 1.0, jnp.where(values == 0.0, 0.5, 0.0))


def vector(norms, row, count):
    return jnp.concatenate([norms[row + i : row + i + 1, :] for i in range(count)], axis=1)


def window_of(j):
    return lax.div(125 * j, 16), 8 * lax.rem(125 * j, 16)


def loop(count, body, times=1):
    def step(i, carry):
        for k in range(times):
            body(i * times + k)
        return carry

    lax.fori_loop(0, count // times, step, 0)


def summed(count, body, start, times=1):
    def step(i, carry):
        for k in range(times):
            carry = body(i * times + k, carry)
        return carry

    return lax.fori_loop(0, count // times, step, start)


def choose(own, wanted, candidates, start, place, sem):
    for distance in range(4):

        @pl.when(lax.bitwise_xor(own, wanted) == distance)
        def _(source=candidates[distance]):
            pltpu.make_async_copy(source.at[pl.ds(start, place.shape[0])], place, sem).start()


def landed(candidates, start, place, sem):
    pltpu.make_async_copy(candidates[0].at[pl.ds(start, place.shape[0])], place, sem).wait()


def load_flat(flat, buf, sem):
    copy = pltpu.make_async_copy(flat.reshape(LROWS, 128), buf.at[pl.ds(OFF, LROWS)], sem)
    copy.start()
    buf[0:OFF, :] = jnp.zeros((OFF, 128), F32)
    end = OFF + LROWS
    buf[end : buf.shape[0], :] = jnp.zeros((buf.shape[0] - end, 128), F32)
    copy.wait()


def columns(buf, out, place, start, stride, size, chunk):
    def body(i):
        rows = buf[pl.ds(start + i * chunk * stride, chunk, stride=stride), :]
        out[pl.ds(pl.multiple_of(place + i * chunk, 16), chunk), :] = rows.astype(BF)

    loop(size // chunk, body)


def prepare(role, flat, out_a, out_b, buf, sem):
    load_flat(flat, buf, sem)
    own = role[0]

    @pl.when(own == 0)
    def _():
        for t in range(2):
            columns(buf, out_a, 1024 * t, OFF + t, 2, 1024, 256)
            columns(buf, out_b, 1280 * t, OFF + 2048 + t, 2, 1280, 256)

    @pl.when(own == 1)
    def _():
        columns(buf, out_a, 0, 10, 2, 1280, 256)
        columns(buf, out_a, 1280, 11, 2, 768, 256)
        columns(buf, out_b, 0, 11 + 2 * 768, 2, 512, 256)

        def body(j):
            columns(buf, out_b, 512 + 256 * j, OFF + 2474 + j, 8, 256, 256)

        loop(8, body)

    @pl.when(own >= 2)
    def _():
        start = jnp.where(own == 2, 436, 254)

        def body(k):
            for i in range(5):
                r = 5 * k + i
                where = pl.ds(pl.multiple_of(16 * r, 16), 16)
                for half, out in ((0, out_a), (1, out_b)):
                    rows = buf[pl.ds(start + half * 16 * 125 + r, 16, stride=125), :]
                    out[where, :] = rows.astype(BF)

        loop(25, body)
        out_a[2000:2048, :] = jnp.zeros((48, 128), BF)

    @pl.when(own == 2)
    def _():
        def body(j):
            columns(buf, out_b, TAILS + 48 * j, 52 + j, 8, 48, 48)

        loop(8, body)
        out_b[TAILS + 384 : PART_B, :] = jnp.zeros((176, 128), BF)

    @pl.when(own == 3)
    def _():
        out_a[NORMS : NORMS + 32, :] = buf[OFF + 4158 : OFF + 4190, :].astype(BF)
        out_b[SPILL : SPILL + 128, :] = buf[4:132, :].astype(BF)
        out_b[SPILL + 128 : SPILL + 256, :] = buf[129:257, :].astype(BF)
        out_b[SPILL + 256 : PART_B, :] = jnp.zeros((304, 128), BF)


def prepare_gossip(flat_p, flat_m, out_p, out_m, buf_p, buf_m, sems):
    copies = [
        pltpu.make_async_copy(flat_p.reshape(LROWS, 128), buf_p.at[pl.ds(0, LROWS)], sems.at[0]),
        pltpu.make_async_copy(flat_m.reshape(LROWS, 128), buf_m.at[pl.ds(0, LROWS)], sems.at[1]),
    ]
    for copy in copies:
        copy.start()
    for copy in copies:
        copy.wait()
    for buf in (buf_p, buf_m):
        buf[LROWS:GROWS, :] = jnp.zeros((GROWS - LROWS, 128), F32)

    def body(i):
        where = at(i, 32)
        decayed = MOMENTUM_RATE * buf_m[where, :]
        out_p[where, :] = (buf_p[where, :] - LEARN_RATE * decayed).astype(BF)
        out_m[where, :] = decayed.astype(BF)

    loop(131, body)


def turned(source, out):
    def body(c):
        out[:, at(c)] = source[at(c), :].T

    steps = source.shape[0] // 128
    loop(steps, body, steps if source.shape[1] == 256 else 1)


def spread(out, step, values, mask):
    where = pl.ds(pl.multiple_of(step * 128 + LINE, LINE), 128)
    out[where, 0:256] = (pltpu.roll(values, 4, 0) * mask).astype(BF)
    out[where, 256:512] = values.astype(BF)
    out[where, 512:768] = (pltpu.roll(values, 124, 0) * mask).astype(BF)


def edges(out):
    zeros = jnp.zeros((LINE, out.shape[1]), out.dtype)
    out[0:LINE, :] = zeros
    out[LINE + ROWS : 2 * LINE + ROWS, :] = zeros


def spread_of(values, mean):
    lanes = values.shape[1]
    mask = line_mask(lanes)

    def step(c, acc):
        centred = (values[at(c, LINE), :] - mean) * mask
        return acc + fold(centred * centred)

    return total(summed(ROWS // LINE, step, jnp.zeros((8, lanes), F32), 2))


def first_layer(role, rows, x0, x1, x2, x3, xh, inv_out, padded, norms_out, weight, norms, sems):
    cands = (x0, x1, x2, x3)
    choose(role[0], 0, cands, 0, weight, sems.at[0])
    choose(role[0], 3, cands, NORMS, norms, sems.at[1])
    edges(padded)
    mask = row_mask(256)
    landed(cands, NORMS, norms, sems.at[1])
    norms_out[...] = norms[...]
    small = norms[...].astype(F32)
    gain, bias = vector(small, 0, 2), vector(small, 2, 2)
    landed(cands, 0, weight, sems.at[0])

    def one(c, acc):
        w = jnp.concatenate([weight[0:1024, :], weight[1024:2048, :]], axis=1)
        h = dot(rows[at(c), :], w)
        xh[at(c), :] = h
        return acc + fold(h)

    mean = total(lax.fori_loop(0, STEPS, one, jnp.zeros((8, 256), F32))) / PIX
    inv = lax.rsqrt(spread_of(xh, mean) / PIX + EPS)
    inv_out[...] = jnp.broadcast_to(inv, (8, 256))

    def two(c, carry):
        hat = (xh[at(c), :] - mean) * inv * mask
        xh[at(c), :] = hat
        spread(padded, c, jnp.maximum(hat * gain + bias, 0.0) * mask, mask)
        return carry

    lax.fori_loop(0, STEPS, two, 0)


def middle(
    role, labels, rows, padded, norms, a0, a1, a2, a3, b0, b1, b2, b3,
    de, dsec, xh2, inv_out, wsp, small_out, dnorm,
    s0, s1, s2, s3, we, h3, dh3, sec, sect, turn, turn2, wide_buf, sems,
):
    own = role[0]
    part_a, part_b = (a0, a1, a2, a3), (b0, b1, b2, b3)
    plan = [(0, part_b, s0)]
    for wanted, whole in ((1, s1), (2, s2), (3, s3)):
        plan.append((wanted, part_a, whole.at[pl.ds(0, PART_A)]))
        plan.append((wanted, part_b, whole.at[pl.ds(PART_A, PART_B)]))
    for i, (wanted, cands, place) in enumerate(plan):
        choose(own, wanted, cands, 0, place, sems.at[i])
    mask = row_mask(256)
    small = norms[...].astype(F32)
    gain2, bias2 = vector(small, 4, 2), vector(small, 6, 2)
    gain3, bias3 = vector(small, 8, 8), vector(small, 16, 8)

    for i, (wanted, cands, place) in enumerate(plan):
        landed(cands, 0, place, sems.at[i])
    for t in range(2):
        lanes = slice(128 * t, 128 * t + 128)

        def below(i, t=t, lanes=lanes):
            wsp[at(i), lanes] = s0[pl.ds(pl.multiple_of(1280 * t + 128 * i, 128), 128), :]
            where = pl.ds(pl.multiple_of(1280 + 128 * i, 128), 128)
            wsp[where, lanes] = s1[pl.ds(pl.multiple_of(1280 * t + 256 + 128 * i, 128), 128), :]

        loop(8, below, 4)
        wsp[1024:1280, lanes] = (
            s0[1280 * t + 1024 : 1280 * t + 1280, :] + s1[1280 * t : 1280 * t + 256, :]
        )

    def across(j):
        low = 2560 + 256 * j
        we[0:208, at(j)] = s1[pl.ds(pl.multiple_of(low, 256), 208), :]
        we[208:256, at(j)] = (
            s1[pl.ds(pl.multiple_of(low + 208, 16), 48), :]
            + s2[pl.ds(pl.multiple_of(PART_A + TAILS + 48 * j, 16), 48), :]
        )

    loop(8, across, 4)

    def widen(i):
        wide_buf[at(i, 80), :] = s2[pl.ds(pl.multiple_of(2048 + 80 * i, 16), 80), :].astype(F32)

    def narrow(i):
        s2[pl.ds(pl.multiple_of(2048 + 80 * i, 16), 80), :] = wide_buf[at(i, 80), :].astype(BF)

    loop(25, widen, 5)
    for i in range(2):
        spill = s3[PART_A + SPILL + 128 * i : PART_A + SPILL + 128 * i + 128, :].astype(F32)[0:125, :]
        where = pl.ds(14 + i, 125, stride=16)
        wide_buf[where, :] = wide_buf[where, :] + spill
    loop(25, narrow, 5)

    def conv(c, acc):
        h = jnp.zeros((128, 256), F32)
        for dy in range(3):
            where = pl.ds(pl.multiple_of(c * 128 + dy * LINE, LINE), 128)
            h = h + dot(padded[where, :], wsp[768 * dy : 768 * dy + 768, :])
        xh2[at(c), :] = h
        return acc + fold(h)

    mean = total(lax.fori_loop(0, STEPS, conv, jnp.zeros((8, 256), F32))) / PIX
    inv = lax.rsqrt(spread_of(xh2, mean) / PIX + EPS)
    inv_out[...] = jnp.broadcast_to(inv, (8, 256))

    def expand(c, acc):
        hat = (xh2[at(c), :] - mean) * inv * mask
        xh2[at(c), :] = hat
        second = (jnp.maximum(hat * gain2 + bias2, 0.0) * mask).astype(BF)
        sec[at(c), :] = second
        h = dot(second, we[...])
        h3[at(c), :] = h
        return acc + fold(h)

    mean3 = total(lax.fori_loop(0, STEPS, expand, jnp.zeros((8, 1024), F32))) / PIX
    inv3 = lax.rsqrt(spread_of(h3, mean3) / PIX + EPS)

    def pool(c, carry):
        acc, count, weighed = carry
        hat = (h3[at(c, LINE), :] - mean3) * inv3
        h3[at(c, LINE), :] = hat
        out = hat * gain3 + bias3 + rows[at(c, LINE), :].astype(F32)
        on = slope(out) * real3
        return (
            acc + fold(jnp.maximum(out, 0.0) * real3),
            count + fold(on),
            weighed + fold(on * hat),
        )

    zero8 = jnp.zeros((8, 1024), F32)
    real3 = line_mask(1024)
    acc, count, weighed = summed(ROWS // LINE, pool, (zero8, zero8, zero8), 2)
    acc = (acc + pltpu.roll(acc, 4, 0)) / 196.0
    four = lax.broadcasted_iota(jnp.int32, (8, 1024), 0) < 4
    pooled = jnp.where(four, acc, 0.0).astype(BF).astype(F32)

    turn[...] = jnp.concatenate([pooled, jnp.zeros((120, 1024), F32)], axis=0).T

    def regroup(j):
        part = jnp.concatenate([turn[pl.ds(j, 64, stride=16), :], jnp.zeros((64, 128), F32)], axis=0)
        turn2[at(j, 16), :] = part.T[0:16, :]

    loop(16, regroup, 4)

    def window(first):
        tiles = []
        for i in range(9):
            parts = [
                s[pl.ds(pl.multiple_of(start + 16 * (first + i), 16), 16), :]
                for s in (s2, s3)
                for start in (0, 2048)
            ]
            tiles.append(jnp.concatenate(parts, axis=0))
        return jnp.concatenate(tiles, axis=1)

    def score(j, acc):
        first, shift = window_of(j)
        wide = dot(turn2[at(j, 16), 0:64].astype(BF), window(first))
        return acc + pltpu.roll(wide, WIDE - shift, 1)[:, 0:1024]

    logits = summed(16, score, jnp.zeros((16, 1024), F32), 4)
    lane = lax.broadcasted_iota(jnp.int32, (16, 1024), 1)
    image = lax.broadcasted_iota(jnp.int32, (16, 1024), 0)
    real = lane < CLASSES
    logits = jnp.where(real, logits, -1e30)
    top = jnp.max(logits, axis=1, keepdims=True)
    ex = jnp.where(real, jnp.exp(logits - top), 0.0)
    prob = ex / jnp.sum(ex, axis=1, keepdims=True)
    hot = jnp.zeros((16, 1024), jnp.bool_)
    for i in range(4):
        hot = hot | ((image == i) & (lane == labels[i]))
    dl = jnp.where(image < 4, (prob - jnp.where(hot, 1.0, 0.0)) * 0.25, 0.0)
    pair = jnp.concatenate([pooled, dl[0:8, :]], axis=0).astype(BF)
    for t in range(8):
        small_out[384 + 16 * t : 400 + 16 * t, :] = pair[:, 128 * t : 128 * t + 128]
    dl = jnp.concatenate([dl, jnp.zeros((16, 128), F32)], axis=1)

    def unscore(j):
        first, shift = window_of(j)
        moved = pltpu.roll(dl, shift, 1).astype(BF)
        moved = jnp.concatenate([moved, jnp.zeros((112, WIDE), BF)], axis=0)
        turn[pl.ds(j, 64, stride=16), :] = dot_nt(window(first), moved)

    loop(16, unscore, 4)
    dpool = turn[...].T[0:8, :] / 196.0
    dpool = jnp.where(four, dpool, pltpu.roll(dpool, 4, 0))

    dbias3 = total(count * dpool)
    dgain3 = total(weighed * dpool)
    for j in range(8):
        dnorm[j : j + 1, :] = dgain3[:, 128 * j : 128 * j + 128]
        dnorm[8 + j : 9 + j, :] = dbias3[:, 128 * j : 128 * j + 128]
    scale = gain3 * inv3
    level = scale * dbias3 / PIX
    tilt = scale * dgain3 / PIX
    steep = scale * dpool

    def back(c):
        hat = h3[at(c, LINE), :]
        on = slope(hat * gain3 + bias3 + rows[at(c, LINE), :].astype(F32))
        step = (on.reshape(8, 8, 1024) * steep[None]).reshape(LINE, 1024)
        dh3[at(c, LINE), :] = (step - level - hat * tilt).astype(BF)

    loop(ROWS // LINE, back, 2)
    turned(sec, sect)

    def weigh(n):
        right = dh3[:, at(n, 256)]
        piece = dot(sect[...], right).astype(BF)
        for t in range(2):
            half = piece[:, 128 * t : 128 * t + 128]
            de[pl.ds(pl.multiple_of(512 * n + 256 * t, 128), 256), :] = half
            small_out[pl.ds(pl.multiple_of(96 * n + 48 * t, 16), 48), :] = half[208:256, :]

    loop(4, weigh, 2)
    small_out[512:544, :] = jnp.zeros((32, 128), BF)

    def down(c, carry):
        dsec[at(c), :] = dot_nt(dh3[at(c), :], we[...])
        return carry

    lax.fori_loop(0, STEPS, down, 0)


def bn_back(dy, xh, gain, bias, inv, mask):
    def sums(c, carry):
        hat = xh[at(c), :]
        d = dy[at(c), :] * slope(hat * gain + bias) * mask
        dy[at(c), :] = d
        return (carry[0] + fold(d), carry[1] + fold(d * hat))

    zero = jnp.zeros((8, 256), F32)
    a, b = lax.fori_loop(0, STEPS, sums, (zero, zero))
    return total(a), total(b)


def back_spatial(role, dsec, xh2, inv2, norms, padt, ds, dext, dnorm, work, full):
    own = role[0]
    small = norms[...].astype(F32)
    gain, bias = vector(small, 4, 2), vector(small, 6, 2)
    inv = inv2[0:1, :]
    mask = row_mask(256)

    def take(c, carry):
        work[at(c), :] = dsec[at(c), :]
        return carry

    lax.fori_loop(0, STEPS, take, 0)
    dbias, dgain = bn_back(work, xh2, gain, bias, inv, mask)
    for t in range(2):
        dnorm[t : t + 1, :] = dgain[:, 128 * t : 128 * t + 128]
        dnorm[2 + t : 3 + t, :] = dbias[:, 128 * t : 128 * t + 128]
    dnorm[4:8, :] = jnp.zeros((4, 128), F32)
    dext[0:128, :] = jnp.zeros((128, 256), BF)
    dext[1024:1152, :] = jnp.zeros((128, 256), BF)
    scale = gain * inv
    level, tilt = dbias / PIX, dgain / PIX

    def one(c, carry):
        d = scale * (work[at(c), :] - level - xh2[at(c), :] * tilt) * mask
        dext[pl.ds(pl.multiple_of(c * 128 + 128, 128), 128), :] = d.astype(BF)
        return carry

    lax.fori_loop(0, STEPS, one, 0)

    def weigh(dy):
        right = dext[pl.ds(pl.multiple_of(128 - LINE * dy, LINE), 1024), :]
        for m in range(2):
            piece = dot(padt[384 * m : 384 * m + 384, :], right).astype(BF)
            full[pl.ds(pl.multiple_of(768 * dy + 384 * m, 128), 384), :] = piece

    loop(3, weigh)

    def hand_out(i):
        for t in range(2):
            lanes = slice(128 * t, 128 * t + 128)
            where = at(i, 256)
            place = pl.ds(pl.multiple_of(1280 * t + 256 * i, 256), 256)
            ds[own, place, :] = full[where, lanes]
            shifted = pl.ds(pl.multiple_of(1024 + 256 * i, 256), 256)
            ds[1 - own, place, :] = full[shifted, lanes]

    loop(5, hand_out)


def back_reduce(
    dext, xh1, inv1, norms, rowst, wsp, small_in, dnorm2, dnorm3, out, spreads, work, dh1,
):
    small = norms[...].astype(F32)
    gain, bias = vector(small, 0, 2), vector(small, 2, 2)
    inv = inv1[0:1, :]
    mask = row_mask(256)
    edges(spreads)

    def widen(c, carry):
        where = pl.ds(pl.multiple_of(c * 128 + 128, 128), 128)
        spread(spreads, c, dext[where, :].astype(F32), mask)
        return carry

    lax.fori_loop(0, STEPS, widen, 0)

    def conv(c, carry):
        d = jnp.zeros((128, 256), F32)
        for dy in range(3):
            where = pl.ds(pl.multiple_of(c * 128 + (2 - dy) * LINE, LINE), 128)
            for dx in range(3):
                tap = 256 * (3 * dy + dx)
                lanes = 256 * (2 - dx)
                d = d + dot_nt(spreads[where, lanes : lanes + 256], wsp[tap : tap + 256, :])
        work[at(c), :] = d
        return carry

    lax.fori_loop(0, STEPS, conv, 0)
    dbias, dgain = bn_back(work, xh1, gain, bias, inv, mask)
    out[2048:2560, :] = small_in[0:512, :]
    parts = [v[:, 128 * t : 128 * t + 128] for v in (dgain, dbias) for t in range(2)]
    parts = parts + [dnorm2[0:4, :], dnorm3[...], jnp.zeros((8, 128), F32)]
    out[2560:2592, :] = jnp.concatenate(parts, axis=0).astype(BF)
    scale = gain * inv
    level, tilt = dbias / PIX, dgain / PIX

    def one(c, carry):
        d = scale * (work[at(c), :] - level - xh1[at(c), :] * tilt) * mask
        dh1[at(c), :] = d.astype(BF)
        return carry

    lax.fori_loop(0, STEPS, one, 0)

    def weigh(m):
        piece = dot(rowst[at(m, 256), :], dh1[...]).astype(BF)
        for t in range(2):
            start = pl.multiple_of(1024 * t + 256 * m, 256)
            out[pl.ds(start, 256), :] = piece[:, 128 * t : 128 * t + 128]

    loop(4, weigh)


def finish(
    role, flat_p, flat_m, peer_p, peer_m, r_own, r_peer, s_own, s_peer, e_own, e_peer, small_own, small_peer,
    out_p, out_m, grad, buf_p, buf_m, turn, sems,
):
    own = role[0]
    copies = [
        pltpu.make_async_copy(flat_p.reshape(LROWS, 128), buf_p.at[pl.ds(0, LROWS)], sems.at[0]),
        pltpu.make_async_copy(flat_m.reshape(LROWS, 128), buf_m.at[pl.ds(0, LROWS)], sems.at[1]),
    ]
    for copy in copies:
        copy.start()

    def both(a, b, start, size):
        where = pl.ds(pl.multiple_of(start, 16), size)
        return a[where, :].astype(F32) + b[where, :].astype(F32)

    def place(a, b, source, start, stride, size, chunk):
        def body(i):
            where = pl.ds(start + i * chunk * stride, chunk, stride=stride)
            grad[where, :] = both(a, b, source + i * chunk, chunk)

        loop(size // chunk, body)

    @pl.when(own < 2)
    def _():
        for t in range(2):
            place(s_own, s_peer, 1280 * t, jnp.where(own == 0, OFF + 2048, 10) + t, 2, 1280, 256)

    @pl.when(own == 0)
    def _():
        for t in range(2):
            place(r_own, r_peer, 1024 * t, OFF + t, 2, 1024, 256)

    @pl.when(own == 1)
    def _():
        def body(j):
            place(e_own, e_peer, 256 * j, OFF + 2474 + j, 8, 256, 256)

        loop(8, body)

    @pl.when(own >= 2)
    def _():
        group, start = jnp.where(own == 2, 0, 30), jnp.where(own == 2, 436, 4)
        parts = []
        for ref in (small_own, small_peer):
            for i in range(4):
                tiles = [
                    ref[416 + 128 * i + 16 * t : 432 + 128 * i + 16 * t, :].astype(F32)
                    for t in range(8)
                ]
                parts.append(jnp.concatenate(tiles, axis=1))

        def pack(start):
            tiles = [part[start : start + 8, :] for part in parts]
            pairs = [tiles[i] + pltpu.roll(tiles[i + 1], 4, 0) for i in range(0, 8, 2)]
            return jnp.concatenate(pairs, axis=0)

        pooled = jnp.concatenate([pack(0), jnp.zeros((96, 1024), F32)], axis=0)
        turn[0:1024, :] = pooled.T
        turn[1024:1152, :] = jnp.zeros((128, 128), F32)
        dl = jnp.concatenate([pack(8), jnp.zeros((32, 128), F32)], axis=1)

        def clear(i):
            grad[at(i, 64), :] = jnp.zeros((64, 128), F32)

        loop(85, clear, 5)

        def product(j):
            first, shift = window_of(j)
            moved = pltpu.roll(dl, shift, 1).astype(BF)
            left = turn[pl.ds(16 * group + j, 40, stride=16), :].astype(BF)
            wide = dot(left[:, 0:32], moved)
            for i in range(9):
                where = pl.ds(start + first + i, 40, stride=125)
                grad[where, :] = grad[where, :] + wide[:, 128 * i : 128 * i + 128]

        loop(16, product, 4)

    @pl.when(own == 2)
    def _():
        def body(j):
            place(small_own, small_peer, 48 * j, 52 + j, 8, 48, 48)

        loop(8, body)

    @pl.when(own == 3)
    def _():
        grad[OFF + 4158 : OFF + 4182, :] = both(small_own, small_peer, 384, 32)[0:24, :]

    for copy in copies:
        copy.wait()

    def piece(where, shifted):
        g = grad[shifted, :] * 0.25
        decayed = MOMENTUM_RATE * buf_m[where, :]
        p = 0.5 * ((buf_p[where, :] - LEARN_RATE * decayed) + peer_p[where, :].astype(F32))
        m = 0.5 * (decayed + peer_m[where, :].astype(F32))
        buf_p[where, :] = p - (0.5 * LEARN_RATE) * g
        buf_m[where, :] = m + 0.5 * g

    def body(i):
        piece(
            at(i, 32),
            pl.ds(pl.multiple_of(i * 32 + OFF, 32), 32),
        )

    loop(131, body)
    copies = [
        pltpu.make_async_copy(buf_p.at[pl.ds(0, LROWS)], out_p.reshape(LROWS, 128), sems.at[0]),
        pltpu.make_async_copy(buf_m.at[pl.ds(0, LROWS)], out_m.reshape(LROWS, 128), sems.at[1]),
    ]
    for copy in copies:
        copy.start()
    for copy in copies:
        copy.wait()


def along(value, pairs):
    return lax.ppermute(value, "local", pairs)


CORE = [(l, l ^ 1) for l in range(4)]
CHIP = [(l, l ^ 2) for l in range(4)]


def add(a, b):
    return (a.astype(F32) + b.astype(F32)).astype(BF)


def whole_step(images, labels, params, momentum, distance):
    nodes = lax.axis_size("node")
    index = lax.axis_index("local")
    role = index.astype(jnp.int32).reshape(1)
    dma = pltpu.SemaphoreType.DMA
    on_y = distance in (1, 4)

    def ahead(value, members):
        pairs = [
            (n * 4 + l, ((n + distance) % nodes) * 4 + l) for n in range(nodes) for l in members
        ]
        return lax.ppermute(value, ("node", "local"), pairs)

    sent_a, sent_b = call(
        prepare, "prepare", [SM, ANY], [shape((PART_A, 128), BF), shape((PART_B, 128), BF)],
        [pltpu.VMEM((5008, 128), F32), dma],
    )(role, params)
    across_a, across_b = along(sent_a, CHIP), along(sent_b, CHIP)
    beside_a, beside_b = along(sent_a, CORE), along(sent_b, CORE)

    params_later, _ = lax.optimization_barrier((params, sent_a))
    early_p, early_m = call(
        prepare_gossip, "prepare_gossip", [ANY, ANY], [shape((GROWS, 128), BF)] * 2,
        [pltpu.VMEM((GROWS, 128), F32), pltpu.VMEM((GROWS, 128), F32), dma((2,))],
    )(params_later, momentum)
    rows = jnp.transpose(images, (1, 2, 0, 3))
    rows = jnp.pad(rows, ((0, 0), (0, 2), (0, 0), (0, 0))).reshape(ROWS, 1024)
    rowst = call(turned, "turn_rows", [VM], shape((1024, ROWS), BF), [])(rows)
    across_a, rows, rowst, _ = lax.optimization_barrier((across_a, rows, rowst, early_p))
    diagonal_a = along(across_a, CORE)

    xh1, inv1, padded, norms = call(
        first_layer, "first_layer", [SM, VM] + [ANY] * 4,
        [
            shape((ROWS, 256), F32), shape((8, 256), F32), shape((1024, 768), BF),
            shape((32, 128), BF),
        ],
        [pltpu.VMEM((2048, 128), BF), pltpu.VMEM((32, 128), BF), dma((2,))],
    )(role, rows, sent_a, beside_a, across_a, diagonal_a)

    padt = call(turned, "turn_padded", [VM], shape((768, 1024), BF), [])(padded)
    across_b, _, _ = lax.optimization_barrier((across_b, padt, xh1))
    diagonal_b = along(across_b, CORE)
    gathered = across_b if on_y else across_a
    early_p, early_m, _ = lax.optimization_barrier((early_p, early_m, gathered))
    peer_p = ahead(early_p, range(4))
    if not on_y:
        early_m, _ = lax.optimization_barrier((early_m, peer_p))
    peer_m = ahead(early_m, range(4))
    whole = pltpu.VMEM((SENT, 128), BF)
    de, dsec, xh2, inv2, wsp, small, dnorm3 = call(
        middle, "middle", [SM, SM, VM, VM, VM] + [ANY] * 8,
        [
            shape((2048, 128), BF), shape((ROWS, 256), F32), shape((ROWS, 256), F32),
            shape((8, 256), F32), shape((2304, 256), BF), shape((544, 128), BF),
            shape((16, 128), F32),
        ],
        [
            pltpu.VMEM((2560, 128), BF), whole, whole, whole,
            pltpu.VMEM((256, 1024), BF), pltpu.VMEM((ROWS, 1024), F32),
            pltpu.VMEM((ROWS, 1024), BF), pltpu.VMEM((ROWS, 256), BF),
            pltpu.VMEM((256, ROWS), BF), pltpu.VMEM((1024, 128), F32),
            pltpu.VMEM((256, 128), F32), pltpu.VMEM((2000, 128), F32), dma((7,)),
        ],
    )(
        role, labels, rows, padded, norms, sent_a, beside_a, across_a, diagonal_a,
        sent_b, beside_b, across_b, diagonal_b,
    )
    e_core = add(de, along(de, [(0, 1), (2, 3)]))
    e_across = along(e_core, [(3, 1)])
    e_own = add(e_core, e_across)
    e_peer = ahead(e_own, [1])

    ds, dext, dnorm2 = call(
        back_spatial, "back_spatial", [SM, VM, VM, VM, VM, VM],
        [shape((2, 2560, 128), BF), shape((1152, 256), BF), shape((8, 128), F32)],
        [pltpu.VMEM((ROWS, 256), F32), pltpu.VMEM((2304, 256), BF)],
    )(lax.rem(role, 2), dsec, xh2, inv2, norms, padt)
    s_core = add(ds[0], along(ds[1], CORE))
    s_across = along(s_core, [(2, 0), (3, 1)])
    s_own = add(s_core, s_across)
    s_peer = ahead(s_own, [0, 1])

    dext, _ = lax.optimization_barrier((dext, e_core if on_y else (e_core, peer_p)))
    dwr = call(
        back_reduce, "back_reduce", [VM] * 9, shape((2592, 128), BF),
        [
            pltpu.VMEM((1024, 768), BF), pltpu.VMEM((ROWS, 256), F32), pltpu.VMEM((ROWS, 256), BF),
        ],
    )(dext, xh1, inv1, norms, rowst, wsp, small, dnorm2, dnorm3)
    dwr, _ = lax.optimization_barrier((dwr, (s_across, peer_p, peer_m) if on_y else (e_across, s_across)))
    dwr_beside = along(dwr, CORE)
    r_core = add(dwr[0:2048], dwr_beside[0:2048])
    r_core, _ = lax.optimization_barrier((r_core, (e_peer, s_across) if on_y else (e_peer, s_across, peer_m)))
    r_own = add(r_core, along(r_core, [(2, 0)]))
    r_peer = ahead(r_own, [0])

    def tails_norms_pairs(a, b, count):
        start = a.shape[0] - 416 - 128 * count
        middle_a, middle_b = a[start + 384 : start + 384 + 128 * count], b[start + 384 : start + 384 + 128 * count]
        summed = add(
            jnp.concatenate([a[start : start + 384], a[-32:]], axis=0),
            jnp.concatenate([b[start : start + 384], b[-32:]], axis=0),
        )
        return summed, jnp.concatenate([middle_a, middle_b], axis=0)

    summed, pairs = tails_norms_pairs(dwr, dwr_beside, 1)
    small_chip = jnp.concatenate([summed, pairs], axis=0)
    small_across = along(small_chip, CHIP)
    small_own = jnp.concatenate(
        [add(summed, small_across[0:416]), pairs, small_across[416:672]], axis=0
    )
    small_peer = ahead(small_own, [2, 3])

    return call(
        finish, "finish", [SM, ANY, ANY] + [VM] * 10,
        [shape((1, LROWS * 128), F32)] * 2,
        [
            pltpu.VMEM((5440, 128), F32), pltpu.VMEM((GROWS, 128), F32),
            pltpu.VMEM((GROWS, 128), F32), pltpu.VMEM((1152, 128), F32), dma((2,)),
        ],
        out_specs=[ANY, ANY],
    )(
        role, params, momentum, peer_p, peer_m, r_own, r_peer, s_own, s_peer, e_own, e_peer,
        small_own, small_peer,
    )


def body(images, labels, params, momentum, step):
    degrees = lax.axis_size("node").bit_length() - 1
    branches = [functools.partial(whole_step, distance=1 << degree) for degree in range(degrees)]
    return tuple(lax.switch(step[0] % degrees, branches, images, labels, params, momentum))


def solution(mesh):
    in_specs = (
        P(("node", "local"), None, None, None),
        P(("node", "local")),
        P("node", "local"),
        P("node", "local"),
        P(),
    )
    out_specs = (P("node", "local"), P("node", "local"))
    return jax.shard_map(body, mesh=mesh, in_specs=in_specs, out_specs=out_specs, check_vma=False)
```

```python
import functools

import jax
import jax.numpy as jnp
from jax import lax
from jax.experimental import pallas as pl
from jax.experimental.pallas import tpu as pltpu
from jax.sharding import PartitionSpec as P

F32 = jnp.float32
BF = jnp.bfloat16

CLASSES = 1000
EPS = 1e-05
MOMENTUM_RATE = 0.9
LEARN_RATE = 0.1

LROWS = 4182
GROWS = 4192
OFF = 96
PIX = 784.0

ROWS = 896
LINE = 64
VALID = 56
STEPS = 7

WIDE = 9 * 128


PART_A = 2048
PART_B = 2560
SENT = PART_A + PART_B
NORMS = 2000
TAILS = 2000
SPILL = 2000

VMEM_LIMIT = 48 * 1024 * 1024

ANY = pl.BlockSpec(memory_space=pl.ANY)
VM = pl.BlockSpec(memory_space=pltpu.VMEM)
SM = pl.BlockSpec(memory_space=pltpu.SMEM)


def shape(dims, dtype):
    return jax.ShapeDtypeStruct(dims, dtype)


def call(kernel, name, in_specs, out_shape, scratch, out_specs=None):
    extra = {} if out_specs is None else {"out_specs": out_specs}
    return pl.pallas_call(
        kernel,
        name=name,
        in_specs=in_specs,
        out_shape=out_shape,
        scratch_shapes=scratch,
        compiler_params=pltpu.CompilerParams(vmem_limit_bytes=VMEM_LIMIT),
        cost_estimate=pl.CostEstimate(flops=1, bytes_accessed=1, transcendentals=0),
        **extra,
    )


def at(step, size=128):
    return pl.ds(pl.multiple_of(step * size, size), size)


def dot(a, b):
    return jnp.dot(a, b, preferred_element_type=F32)


def dot_nt(a, b):
    return lax.dot_general(a, b, (((1,), (1,)), ((), ())), preferred_element_type=F32)


def fold(values):
    rows, lanes = values.shape
    return jnp.sum(values.reshape(rows // 8, 8, lanes), axis=0)


def total(folded):
    return jnp.sum(folded, axis=0, keepdims=True)


def row_mask(lanes):
    rows = lax.broadcasted_iota(jnp.int32, (128, lanes), 0)
    return jnp.where(lax.rem(rows, LINE) < VALID, 1.0, 0.0).astype(F32)


def line_mask(lanes):
    rows = lax.broadcasted_iota(jnp.int32, (LINE, lanes), 0)
    return jnp.where(rows < VALID, 1.0, 0.0).astype(F32)


def slope(values):
    return jnp.where(values > 0.0, 1.0, jnp.where(values == 0.0, 0.5, 0.0))


def vector(norms, row, count):
    return jnp.concatenate([norms[row + i : row + i + 1, :] for i in range(count)], axis=1)


def window_of(j):
    return lax.div(125 * j, 16), 8 * lax.rem(125 * j, 16)


def loop(count, body, times=1):
    def step(i, carry):
        for k in range(times):
            body(i * times + k)
        return carry

    lax.fori_loop(0, count // times, step, 0)


def summed(count, body, start, times=1):
    def step(i, carry):
        for k in range(times):
            carry = body(i * times + k, carry)
        return carry

    return lax.fori_loop(0, count // times, step, start)


def choose(own, wanted, candidates, start, place, sem):
    for distance in range(4):

        @pl.when(lax.bitwise_xor(own, wanted) == distance)
        def _(source=candidates[distance]):
            pltpu.make_async_copy(source.at[pl.ds(start, place.shape[0])], place, sem).start()


def landed(candidates, start, place, sem):
    pltpu.make_async_copy(candidates[0].at[pl.ds(start, place.shape[0])], place, sem).wait()


def load_flat(flat, buf, sem):
    copy = pltpu.make_async_copy(flat.reshape(LROWS, 128), buf.at[pl.ds(OFF, LROWS)], sem)
    copy.start()
    buf[0:OFF, :] = jnp.zeros((OFF, 128), F32)
    end = OFF + LROWS
    buf[end : buf.shape[0], :] = jnp.zeros((buf.shape[0] - end, 128), F32)
    copy.wait()


def columns(buf, out, place, start, stride, size, chunk):
    def body(i):
        rows = buf[pl.ds(start + i * chunk * stride, chunk, stride=stride), :]
        out[pl.ds(pl.multiple_of(place + i * chunk, 16), chunk), :] = rows.astype(BF)

    loop(size // chunk, body)


def prepare(role, flat, out_a, out_b, buf, sem):
    load_flat(flat, buf, sem)
    own = role[0]

    @pl.when(own == 0)
    def _():
        for t in range(2):
            columns(buf, out_a, 1024 * t, OFF + t, 2, 1024, 256)
            columns(buf, out_b, 1280 * t, OFF + 2048 + t, 2, 1280, 256)

    @pl.when(own == 1)
    def _():
        columns(buf, out_a, 0, 10, 2, 1280, 256)
        columns(buf, out_a, 1280, 11, 2, 768, 256)
        columns(buf, out_b, 0, 11 + 2 * 768, 2, 512, 256)

        def body(j):
            columns(buf, out_b, 512 + 256 * j, OFF + 2474 + j, 8, 256, 256)

        loop(8, body)

    @pl.when(own >= 2)
    def _():
        start = jnp.where(own == 2, 436, 254)

        def body(k):
            for i in range(5):
                r = 5 * k + i
                where = pl.ds(pl.multiple_of(16 * r, 16), 16)
                for half, out in ((0, out_a), (1, out_b)):
                    rows = buf[pl.ds(start + half * 16 * 125 + r, 16, stride=125), :]
                    out[where, :] = rows.astype(BF)

        loop(25, body)
        out_a[2000:2048, :] = jnp.zeros((48, 128), BF)

    @pl.when(own == 2)
    def _():
        def body(j):
            columns(buf, out_b, TAILS + 48 * j, 52 + j, 8, 48, 48)

        loop(8, body)
        out_b[TAILS + 384 : PART_B, :] = jnp.zeros((176, 128), BF)

    @pl.when(own == 3)
    def _():
        out_a[NORMS : NORMS + 32, :] = buf[OFF + 4158 : OFF + 4190, :].astype(BF)
        out_b[SPILL : SPILL + 128, :] = buf[4:132, :].astype(BF)
        out_b[SPILL + 128 : SPILL + 256, :] = buf[129:257, :].astype(BF)
        out_b[SPILL + 256 : PART_B, :] = jnp.zeros((304, 128), BF)


def prepare_gossip(flat_p, flat_m, out_p, out_m, buf_p, buf_m, sems):
    copies = [
        pltpu.make_async_copy(flat_p.reshape(LROWS, 128), buf_p.at[pl.ds(0, LROWS)], sems.at[0]),
        pltpu.make_async_copy(flat_m.reshape(LROWS, 128), buf_m.at[pl.ds(0, LROWS)], sems.at[1]),
    ]
    for copy in copies:
        copy.start()
    for copy in copies:
        copy.wait()
    for buf in (buf_p, buf_m):
        buf[LROWS:GROWS, :] = jnp.zeros((GROWS - LROWS, 128), F32)

    def body(i):
        where = at(i, 32)
        decayed = MOMENTUM_RATE * buf_m[where, :]
        out_p[where, :] = (buf_p[where, :] - LEARN_RATE * decayed).astype(BF)
        out_m[where, :] = decayed.astype(BF)

    loop(131, body)


def turned(source, out):
    def body(c):
        out[:, at(c)] = source[at(c), :].T

    steps = source.shape[0] // 128
    loop(steps, body, steps if source.shape[1] == 256 else 1)


def spread(out, step, values, mask):
    where = pl.ds(pl.multiple_of(step * 128 + LINE, LINE), 128)
    out[where, 0:256] = (pltpu.roll(values, 4, 0) * mask).astype(BF)
    out[where, 256:512] = values.astype(BF)
    out[where, 512:768] = (pltpu.roll(values, 124, 0) * mask).astype(BF)


def edges(out):
    zeros = jnp.zeros((LINE, out.shape[1]), out.dtype)
    out[0:LINE, :] = zeros
    out[LINE + ROWS : 2 * LINE + ROWS, :] = zeros


def spread_of(values, mean):
    lanes = values.shape[1]
    mask = line_mask(lanes)

    def step(c, acc):
        centred = (values[at(c, LINE), :] - mean) * mask
        return acc + fold(centred * centred)

    return total(summed(ROWS // LINE, step, jnp.zeros((8, lanes), F32), 2))


def first_layer(role, rows, x0, x1, x2, x3, xh, inv_out, padded, norms_out, weight, norms, sems):
    cands = (x0, x1, x2, x3)
    choose(role[0], 0, cands, 0, weight, sems.at[0])
    choose(role[0], 3, cands, NORMS, norms, sems.at[1])
    edges(padded)
    mask = row_mask(256)
    landed(cands, NORMS, norms, sems.at[1])
    norms_out[...] = norms[...]
    small = norms[...].astype(F32)
    gain, bias = vector(small, 0, 2), vector(small, 2, 2)
    landed(cands, 0, weight, sems.at[0])

    def one(c, acc):
        w = jnp.concatenate([weight[0:1024, :], weight[1024:2048, :]], axis=1)
        h = dot(rows[at(c), :], w)
        xh[at(c), :] = h
        return acc + fold(h)

    mean = total(lax.fori_loop(0, STEPS, one, jnp.zeros((8, 256), F32))) / PIX
    inv = lax.rsqrt(spread_of(xh, mean) / PIX + EPS)
    inv_out[...] = jnp.broadcast_to(inv, (8, 256))

    def two(c, carry):
        hat = (xh[at(c), :] - mean) * inv * mask
        xh[at(c), :] = hat
        spread(padded, c, jnp.maximum(hat * gain + bias, 0.0) * mask, mask)
        return carry

    lax.fori_loop(0, STEPS, two, 0)


def middle(
    role, labels, rows, padded, norms, a0, a1, a2, a3, b0, b1, b2, b3,
    de, dsec, xh2, inv_out, wsp, small_out, dnorm,
    s0, s1, s2, s3, we, h3, dh3, sec, sect, turn, turn2, wide_buf, sems,
):
    own = role[0]
    part_a, part_b = (a0, a1, a2, a3), (b0, b1, b2, b3)
    plan = [(0, part_b, s0)]
    for wanted, whole in ((1, s1), (2, s2), (3, s3)):
        plan.append((wanted, part_a, whole.at[pl.ds(0, PART_A)]))
        plan.append((wanted, part_b, whole.at[pl.ds(PART_A, PART_B)]))
    for i, (wanted, cands, place) in enumerate(plan):
        choose(own, wanted, cands, 0, place, sems.at[i])
    mask = row_mask(256)
    small = norms[...].astype(F32)
    gain2, bias2 = vector(small, 4, 2), vector(small, 6, 2)
    gain3, bias3 = vector(small, 8, 8), vector(small, 16, 8)

    for i, (wanted, cands, place) in enumerate(plan):
        landed(cands, 0, place, sems.at[i])
    for t in range(2):
        lanes = slice(128 * t, 128 * t + 128)

        def below(i, t=t, lanes=lanes):
            wsp[at(i), lanes] = s0[pl.ds(pl.multiple_of(1280 * t + 128 * i, 128), 128), :]
            where = pl.ds(pl.multiple_of(1280 + 128 * i, 128), 128)
            wsp[where, lanes] = s1[pl.ds(pl.multiple_of(1280 * t + 256 + 128 * i, 128), 128), :]

        loop(8, below, 4)
        wsp[1024:1280, lanes] = (
            s0[1280 * t + 1024 : 1280 * t + 1280, :] + s1[1280 * t : 1280 * t + 256, :]
        )

    def across(j):
        low = 2560 + 256 * j
        we[0:208, at(j)] = s1[pl.ds(pl.multiple_of(low, 256), 208), :]
        we[208:256, at(j)] = (
            s1[pl.ds(pl.multiple_of(low + 208, 16), 48), :]
            + s2[pl.ds(pl.multiple_of(PART_A + TAILS + 48 * j, 16), 48), :]
        )

    loop(8, across, 4)

    def widen(i):
        wide_buf[at(i, 80), :] = s2[pl.ds(pl.multiple_of(2048 + 80 * i, 16), 80), :].astype(F32)

    def narrow(i):
        s2[pl.ds(pl.multiple_of(2048 + 80 * i, 16), 80), :] = wide_buf[at(i, 80), :].astype(BF)

    loop(25, widen, 5)
    for i in range(2):
        spill = s3[PART_A + SPILL + 128 * i : PART_A + SPILL + 128 * i + 128, :].astype(F32)[0:125, :]
        where = pl.ds(14 + i, 125, stride=16)
        wide_buf[where, :] = wide_buf[where, :] + spill
    loop(25, narrow, 5)

    def conv(c, acc):
        h = jnp.zeros((128, 256), F32)
        for dy in range(3):
            where = pl.ds(pl.multiple_of(c * 128 + dy * LINE, LINE), 128)
            h = h + dot(padded[where, :], wsp[768 * dy : 768 * dy + 768, :])
        xh2[at(c), :] = h
        return acc + fold(h)

    mean = total(lax.fori_loop(0, STEPS, conv, jnp.zeros((8, 256), F32))) / PIX
    inv = lax.rsqrt(spread_of(xh2, mean) / PIX + EPS)
    inv_out[...] = jnp.broadcast_to(inv, (8, 256))

    def expand(c, acc):
        hat = (xh2[at(c), :] - mean) * inv * mask
        xh2[at(c), :] = hat
        second = (jnp.maximum(hat * gain2 + bias2, 0.0) * mask).astype(BF)
        sec[at(c), :] = second
        h = dot(second, we[...])
        h3[at(c), :] = h
        return acc + fold(h)

    mean3 = total(lax.fori_loop(0, STEPS, expand, jnp.zeros((8, 1024), F32))) / PIX
    inv3 = lax.rsqrt(spread_of(h3, mean3) / PIX + EPS)

    def pool(c, carry):
        acc, count, weighed = carry
        hat = (h3[at(c, LINE), :] - mean3) * inv3
        h3[at(c, LINE), :] = hat
        out = hat * gain3 + bias3 + rows[at(c, LINE), :].astype(F32)
        on = slope(out) * real3
        return (
            acc + fold(jnp.maximum(out, 0.0) * real3),
            count + fold(on),
            weighed + fold(on * hat),
        )

    zero8 = jnp.zeros((8, 1024), F32)
    real3 = line_mask(1024)
    acc, count, weighed = summed(ROWS // LINE, pool, (zero8, zero8, zero8), 2)
    acc = (acc + pltpu.roll(acc, 4, 0)) / 196.0
    four = lax.broadcasted_iota(jnp.int32, (8, 1024), 0) < 4
    pooled = jnp.where(four, acc, 0.0).astype(BF).astype(F32)

    turn[...] = jnp.concatenate([pooled, jnp.zeros((120, 1024), F32)], axis=0).T

    def regroup(j):
        part = jnp.concatenate([turn[pl.ds(j, 64, stride=16), :], jnp.zeros((64, 128), F32)], axis=0)
        turn2[at(j, 16), :] = part.T[0:16, :]

    loop(16, regroup, 4)

    def window(first):
        tiles = []
        for i in range(9):
            parts = [
                s[pl.ds(pl.multiple_of(start + 16 * (first + i), 16), 16), :]
                for s in (s2, s3)
                for start in (0, 2048)
            ]
            tiles.append(jnp.concatenate(parts, axis=0))
        return jnp.concatenate(tiles, axis=1)

    def score(j, acc):
        first, shift = window_of(j)
        wide = dot(turn2[at(j, 16), 0:64].astype(BF), window(first))
        return acc + pltpu.roll(wide, WIDE - shift, 1)[:, 0:1024]

    logits = summed(16, score, jnp.zeros((16, 1024), F32), 4)
    lane = lax.broadcasted_iota(jnp.int32, (16, 1024), 1)
    image = lax.broadcasted_iota(jnp.int32, (16, 1024), 0)
    real = lane < CLASSES
    logits = jnp.where(real, logits, -1e30)
    top = jnp.max(logits, axis=1, keepdims=True)
    ex = jnp.where(real, jnp.exp(logits - top), 0.0)
    prob = ex / jnp.sum(ex, axis=1, keepdims=True)
    hot = jnp.zeros((16, 1024), jnp.bool_)
    for i in range(4):
        hot = hot | ((image == i) & (lane == labels[i]))
    dl = jnp.where(image < 4, (prob - jnp.where(hot, 1.0, 0.0)) * 0.25, 0.0)
    pair = jnp.concatenate([pooled, dl[0:8, :]], axis=0).astype(BF)
    for t in range(8):
        small_out[384 + 16 * t : 400 + 16 * t, :] = pair[:, 128 * t : 128 * t + 128]
    dl = jnp.concatenate([dl, jnp.zeros((16, 128), F32)], axis=1)

    def unscore(j):
        first, shift = window_of(j)
        moved = pltpu.roll(dl, shift, 1).astype(BF)
        moved = jnp.concatenate([moved, jnp.zeros((112, WIDE), BF)], axis=0)
        turn[pl.ds(j, 64, stride=16), :] = dot_nt(window(first), moved)

    loop(16, unscore, 4)
    dpool = turn[...].T[0:8, :] / 196.0
    dpool = jnp.where(four, dpool, pltpu.roll(dpool, 4, 0))

    dbias3 = total(count * dpool)
    dgain3 = total(weighed * dpool)
    for j in range(8):
        dnorm[j : j + 1, :] = dgain3[:, 128 * j : 128 * j + 128]
        dnorm[8 + j : 9 + j, :] = dbias3[:, 128 * j : 128 * j + 128]
    scale = gain3 * inv3
    level = scale * dbias3 / PIX
    tilt = scale * dgain3 / PIX
    steep = scale * dpool

    def back(c):
        hat = h3[at(c, LINE), :]
        on = slope(hat * gain3 + bias3 + rows[at(c, LINE), :].astype(F32))
        step = (on.reshape(8, 8, 1024) * steep[None]).reshape(LINE, 1024)
        dh3[at(c, LINE), :] = (step - level - hat * tilt).astype(BF)

    loop(ROWS // LINE, back, 2)
    turned(sec, sect)

    def weigh(n):
        right = dh3[:, at(n, 256)]
        piece = dot(sect[...], right).astype(BF)
        for t in range(2):
            half = piece[:, 128 * t : 128 * t + 128]
            de[pl.ds(pl.multiple_of(512 * n + 256 * t, 128), 256), :] = half
            small_out[pl.ds(pl.multiple_of(96 * n + 48 * t, 16), 48), :] = half[208:256, :]

    loop(4, weigh, 2)
    small_out[512:544, :] = jnp.zeros((32, 128), BF)

    def down(c, carry):
        dsec[at(c), :] = dot_nt(dh3[at(c), :], we[...])
        return carry

    lax.fori_loop(0, STEPS, down, 0)


def bn_back(dy, xh, gain, bias, inv, mask):
    def sums(c, carry):
        hat = xh[at(c), :]
        d = dy[at(c), :] * slope(hat * gain + bias) * mask
        dy[at(c), :] = d
        return (carry[0] + fold(d), carry[1] + fold(d * hat))

    zero = jnp.zeros((8, 256), F32)
    a, b = lax.fori_loop(0, STEPS, sums, (zero, zero))
    return total(a), total(b)


def back_spatial(role, dsec, xh2, inv2, norms, padt, ds, dext, dnorm, work, full):
    own = role[0]
    small = norms[...].astype(F32)
    gain, bias = vector(small, 4, 2), vector(small, 6, 2)
    inv = inv2[0:1, :]
    mask = row_mask(256)

    def take(c, carry):
        work[at(c), :] = dsec[at(c), :]
        return carry

    lax.fori_loop(0, STEPS, take, 0)
    dbias, dgain = bn_back(work, xh2, gain, bias, inv, mask)
    for t in range(2):
        dnorm[t : t + 1, :] = dgain[:, 128 * t : 128 * t + 128]
        dnorm[2 + t : 3 + t, :] = dbias[:, 128 * t : 128 * t + 128]
    dnorm[4:8, :] = jnp.zeros((4, 128), F32)
    dext[0:128, :] = jnp.zeros((128, 256), BF)
    dext[1024:1152, :] = jnp.zeros((128, 256), BF)
    scale = gain * inv
    level, tilt = dbias / PIX, dgain / PIX

    def one(c, carry):
        d = scale * (work[at(c), :] - level - xh2[at(c), :] * tilt) * mask
        dext[pl.ds(pl.multiple_of(c * 128 + 128, 128), 128), :] = d.astype(BF)
        return carry

    lax.fori_loop(0, STEPS, one, 0)

    def weigh(dy):
        right = dext[pl.ds(pl.multiple_of(128 - LINE * dy, LINE), 1024), :]
        for m in range(2):
            piece = dot(padt[384 * m : 384 * m + 384, :], right).astype(BF)
            full[pl.ds(pl.multiple_of(768 * dy + 384 * m, 128), 384), :] = piece

    loop(3, weigh)

    def hand_out(i):
        for t in range(2):
            lanes = slice(128 * t, 128 * t + 128)
            where = at(i, 256)
            place = pl.ds(pl.multiple_of(1280 * t + 256 * i, 256), 256)
            ds[own, place, :] = full[where, lanes]
            shifted = pl.ds(pl.multiple_of(1024 + 256 * i, 256), 256)
            ds[1 - own, place, :] = full[shifted, lanes]

    loop(5, hand_out)


def back_reduce(
    dext, xh1, inv1, norms, rowst, wsp, small_in, dnorm2, dnorm3, out, spreads, work, dh1,
):
    small = norms[...].astype(F32)
    gain, bias = vector(small, 0, 2), vector(small, 2, 2)
    inv = inv1[0:1, :]
    mask = row_mask(256)
    edges(spreads)

    def widen(c, carry):
        where = pl.ds(pl.multiple_of(c * 128 + 128, 128), 128)
        spread(spreads, c, dext[where, :].astype(F32), mask)
        return carry

    lax.fori_loop(0, STEPS, widen, 0)

    def conv(c, carry):
        d = jnp.zeros((128, 256), F32)
        for dy in range(3):
            where = pl.ds(pl.multiple_of(c * 128 + (2 - dy) * LINE, LINE), 128)
            for dx in range(3):
                tap = 256 * (3 * dy + dx)
                lanes = 256 * (2 - dx)
                d = d + dot_nt(spreads[where, lanes : lanes + 256], wsp[tap : tap + 256, :])
        work[at(c), :] = d
        return carry

    lax.fori_loop(0, STEPS, conv, 0)
    dbias, dgain = bn_back(work, xh1, gain, bias, inv, mask)
    out[2048:2560, :] = small_in[0:512, :]
    parts = [v[:, 128 * t : 128 * t + 128] for v in (dgain, dbias) for t in range(2)]
    parts = parts + [dnorm2[0:4, :], dnorm3[...], jnp.zeros((8, 128), F32)]
    out[2560:2592, :] = jnp.concatenate(parts, axis=0).astype(BF)
    scale = gain * inv
    level, tilt = dbias / PIX, dgain / PIX

    def one(c, carry):
        d = scale * (work[at(c), :] - level - xh1[at(c), :] * tilt) * mask
        dh1[at(c), :] = d.astype(BF)
        return carry

    lax.fori_loop(0, STEPS, one, 0)

    def weigh(m):
        piece = dot(rowst[at(m, 256), :], dh1[...]).astype(BF)
        for t in range(2):
            start = pl.multiple_of(1024 * t + 256 * m, 256)
            out[pl.ds(start, 256), :] = piece[:, 128 * t : 128 * t + 128]

    loop(4, weigh)


def finish(
    role, flat_p, flat_m, peer_p, peer_m, r_own, r_peer, s_own, s_peer, e_own, e_peer, small_own, small_peer,
    out_p, out_m, grad, buf_p, buf_m, turn, sems,
):
    own = role[0]
    copies = [
        pltpu.make_async_copy(flat_p.reshape(LROWS, 128), buf_p.at[pl.ds(0, LROWS)], sems.at[0]),
        pltpu.make_async_copy(flat_m.reshape(LROWS, 128), buf_m.at[pl.ds(0, LROWS)], sems.at[1]),
    ]
    for copy in copies:
        copy.start()

    def both(a, b, start, size):
        where = pl.ds(pl.multiple_of(start, 16), size)
        return a[where, :].astype(F32) + b[where, :].astype(F32)

    def place(a, b, source, start, stride, size, chunk):
        def body(i):
            where = pl.ds(start + i * chunk * stride, chunk, stride=stride)
            grad[where, :] = both(a, b, source + i * chunk, chunk)

        loop(size // chunk, body)

    @pl.when(own < 2)
    def _():
        for t in range(2):
            place(s_own, s_peer, 1280 * t, jnp.where(own == 0, OFF + 2048, 10) + t, 2, 1280, 256)

    @pl.when(own == 0)
    def _():
        for t in range(2):
            place(r_own, r_peer, 1024 * t, OFF + t, 2, 1024, 256)

    @pl.when(own == 1)
    def _():
        def body(j):
            place(e_own, e_peer, 256 * j, OFF + 2474 + j, 8, 256, 256)

        loop(8, body)

    @pl.when(own >= 2)
    def _():
        group, start = jnp.where(own == 2, 0, 30), jnp.where(own == 2, 436, 4)
        parts = []
        for ref in (small_own, small_peer):
            for i in range(4):
                tiles = [
                    ref[416 + 128 * i + 16 * t : 432 + 128 * i + 16 * t, :].astype(F32)
                    for t in range(8)
                ]
                parts.append(jnp.concatenate(tiles, axis=1))

        def pack(start):
            tiles = [part[start : start + 8, :] for part in parts]
            pairs = [tiles[i] + pltpu.roll(tiles[i + 1], 4, 0) for i in range(0, 8, 2)]
            return jnp.concatenate(pairs, axis=0)

        pooled = jnp.concatenate([pack(0), jnp.zeros((96, 1024), F32)], axis=0)
        turn[0:1024, :] = pooled.T
        turn[1024:1152, :] = jnp.zeros((128, 128), F32)
        dl = jnp.concatenate([pack(8), jnp.zeros((32, 128), F32)], axis=1)

        def clear(i):
            grad[at(i, 64), :] = jnp.zeros((64, 128), F32)

        loop(85, clear, 5)

        def product(j):
            first, shift = window_of(j)
            moved = pltpu.roll(dl, shift, 1).astype(BF)
            left = turn[pl.ds(16 * group + j, 40, stride=16), :].astype(BF)
            wide = dot(left[:, 0:32], moved)
            for i in range(9):
                where = pl.ds(start + first + i, 40, stride=125)
                grad[where, :] = grad[where, :] + wide[:, 128 * i : 128 * i + 128]

        loop(16, product, 4)

    @pl.when(own == 2)
    def _():
        def body(j):
            place(small_own, small_peer, 48 * j, 52 + j, 8, 48, 48)

        loop(8, body)

    @pl.when(own == 3)
    def _():
        grad[OFF + 4158 : OFF + 4182, :] = both(small_own, small_peer, 384, 32)[0:24, :]

    for copy in copies:
        copy.wait()

    def piece(where, shifted):
        g = grad[shifted, :] * 0.25
        decayed = MOMENTUM_RATE * buf_m[where, :]
        p = 0.5 * ((buf_p[where, :] - LEARN_RATE * decayed) + peer_p[where, :].astype(F32))
        m = 0.5 * (decayed + peer_m[where, :].astype(F32))
        buf_p[where, :] = p - (0.5 * LEARN_RATE) * g
        buf_m[where, :] = m + 0.5 * g

    def body(i):
        piece(
            at(i, 32),
            pl.ds(pl.multiple_of(i * 32 + OFF, 32), 32),
        )

    loop(131, body)
    copies = [
        pltpu.make_async_copy(buf_p.at[pl.ds(0, LROWS)], out_p.reshape(LROWS, 128), sems.at[0]),
        pltpu.make_async_copy(buf_m.at[pl.ds(0, LROWS)], out_m.reshape(LROWS, 128), sems.at[1]),
    ]
    for copy in copies:
        copy.start()
    for copy in copies:
        copy.wait()


def along(value, pairs):
    return lax.ppermute(value, "local", pairs)


CORE = [(l, l ^ 1) for l in range(4)]
CHIP = [(l, l ^ 2) for l in range(4)]


def add(a, b):
    return (a.astype(F32) + b.astype(F32)).astype(BF)


def whole_step(images, labels, params, momentum, distance):
    nodes = lax.axis_size("node")
    index = lax.axis_index("local")
    role = index.astype(jnp.int32).reshape(1)
    dma = pltpu.SemaphoreType.DMA
    on_y = distance in (1, 4)

    def ahead(value, members):
        pairs = [
            (n * 4 + l, ((n + distance) % nodes) * 4 + l) for n in range(nodes) for l in members
        ]
        return lax.ppermute(value, ("node", "local"), pairs)

    sent_a, sent_b = call(
        prepare, "prepare", [SM, ANY], [shape((PART_A, 128), BF), shape((PART_B, 128), BF)],
        [pltpu.VMEM((5008, 128), F32), dma],
    )(role, params)
    across_a, across_b = along(sent_a, CHIP), along(sent_b, CHIP)
    beside_a, beside_b = along(sent_a, CORE), along(sent_b, CORE)

    params_later, _ = lax.optimization_barrier((params, sent_a))
    early_p, early_m = call(
        prepare_gossip, "prepare_gossip", [ANY, ANY], [shape((GROWS, 128), BF)] * 2,
        [pltpu.VMEM((GROWS, 128), F32), pltpu.VMEM((GROWS, 128), F32), dma((2,))],
    )(params_later, momentum)
    rows = jnp.transpose(images, (1, 2, 0, 3))
    rows = jnp.pad(rows, ((0, 0), (0, 2), (0, 0), (0, 0))).reshape(ROWS, 1024)
    rowst = call(turned, "turn_rows", [VM], shape((1024, ROWS), BF), [])(rows)
    across_a, rows, rowst, _ = lax.optimization_barrier((across_a, rows, rowst, early_p))
    diagonal_a = along(across_a, CORE)

    xh1, inv1, padded, norms = call(
        first_layer, "first_layer", [SM, VM] + [ANY] * 4,
        [
            shape((ROWS, 256), F32), shape((8, 256), F32), shape((1024, 768), BF),
            shape((32, 128), BF),
        ],
        [pltpu.VMEM((2048, 128), BF), pltpu.VMEM((32, 128), BF), dma((2,))],
    )(role, rows, sent_a, beside_a, across_a, diagonal_a)

    padt = call(turned, "turn_padded", [VM], shape((768, 1024), BF), [])(padded)
    across_b, _, _ = lax.optimization_barrier((across_b, padt, xh1))
    diagonal_b = along(across_b, CORE)
    gathered = across_b if on_y else across_a
    early_p, early_m, _ = lax.optimization_barrier((early_p, early_m, gathered))
    peer_p = ahead(early_p, range(4))
    if not on_y:
        early_m, _ = lax.optimization_barrier((early_m, peer_p))
    peer_m = ahead(early_m, range(4))
    whole = pltpu.VMEM((SENT, 128), BF)
    de, dsec, xh2, inv2, wsp, small, dnorm3 = call(
        middle, "middle", [SM, SM, VM, VM, VM] + [ANY] * 8,
        [
            shape((2048, 128), BF), shape((ROWS, 256), F32), shape((ROWS, 256), F32),
            shape((8, 256), F32), shape((2304, 256), BF), shape((544, 128), BF),
            shape((16, 128), F32),
        ],
        [
            pltpu.VMEM((2560, 128), BF), whole, whole, whole,
            pltpu.VMEM((256, 1024), BF), pltpu.VMEM((ROWS, 1024), F32),
            pltpu.VMEM((ROWS, 1024), BF), pltpu.VMEM((ROWS, 256), BF),
            pltpu.VMEM((256, ROWS), BF), pltpu.VMEM((1024, 128), F32),
            pltpu.VMEM((256, 128), F32), pltpu.VMEM((2000, 128), F32), dma((7,)),
        ],
    )(
        role, labels, rows, padded, norms, sent_a, beside_a, across_a, diagonal_a,
        sent_b, beside_b, across_b, diagonal_b,
    )
    e_core = add(de, along(de, [(0, 1), (2, 3)]))
    e_across = along(e_core, [(3, 1)])
    e_own = add(e_core, e_across)
    e_peer = ahead(e_own, [1])

    if not on_y:
        dsec, _ = lax.optimization_barrier((dsec, peer_p))
    ds, dext, dnorm2 = call(
        back_spatial, "back_spatial", [SM, VM, VM, VM, VM, VM],
        [shape((2, 2560, 128), BF), shape((1152, 256), BF), shape((8, 128), F32)],
        [pltpu.VMEM((ROWS, 256), F32), pltpu.VMEM((2304, 256), BF)],
    )(lax.rem(role, 2), dsec, xh2, inv2, norms, padt)
    s_core = add(ds[0], along(ds[1], CORE))
    s_across = along(s_core, [(2, 0), (3, 1)])
    s_own = add(s_core, s_across)
    s_peer = ahead(s_own, [0, 1])

    dext, _ = lax.optimization_barrier((dext, e_core))
    dwr = call(
        back_reduce, "back_reduce", [VM] * 9, shape((2592, 128), BF),
        [
            pltpu.VMEM((1024, 768), BF), pltpu.VMEM((ROWS, 256), F32), pltpu.VMEM((ROWS, 256), BF),
        ],
    )(dext, xh1, inv1, norms, rowst, wsp, small, dnorm2, dnorm3)
    dwr, _ = lax.optimization_barrier((dwr, (e_across, peer_p, peer_m) if on_y else (e_across, s_across, peer_m)))
    dwr_beside = along(dwr, CORE)
    r_core = add(dwr[0:2048], dwr_beside[0:2048])
    r_core, _ = lax.optimization_barrier((r_core, (e_peer, s_across)))
    r_own = add(r_core, along(r_core, [(2, 0)]))
    r_peer = ahead(r_own, [0])

    def tails_norms_pairs(a, b, count):
        start = a.shape[0] - 416 - 128 * count
        middle_a, middle_b = a[start + 384 : start + 384 + 128 * count], b[start + 384 : start + 384 + 128 * count]
        summed = add(
            jnp.concatenate([a[start : start + 384], a[-32:]], axis=0),
            jnp.concatenate([b[start : start + 384], b[-32:]], axis=0),
        )
        return summed, jnp.concatenate([middle_a, middle_b], axis=0)

    summed, pairs = tails_norms_pairs(dwr, dwr_beside, 1)
    small_chip = jnp.concatenate([summed, pairs], axis=0)
    small_across = along(small_chip, CHIP)
    small_own = jnp.concatenate(
        [add(summed, small_across[0:416]), pairs, small_across[416:672]], axis=0
    )
    small_peer = ahead(small_own, [2, 3])

    return call(
        finish, "finish", [SM, ANY, ANY] + [VM] * 10,
        [shape((1, LROWS * 128), F32)] * 2,
        [
            pltpu.VMEM((5440, 128), F32), pltpu.VMEM((GROWS, 128), F32),
            pltpu.VMEM((GROWS, 128), F32), pltpu.VMEM((1152, 128), F32), dma((2,)),
        ],
        out_specs=[ANY, ANY],
    )(
        role, params, momentum, peer_p, peer_m, r_own, r_peer, s_own, s_peer, e_own, e_peer,
        small_own, small_peer,
    )


def body(images, labels, params, momentum, step):
    degrees = lax.axis_size("node").bit_length() - 1
    branches = [functools.partial(whole_step, distance=1 << degree) for degree in range(degrees)]
    return tuple(lax.switch(step[0] % degrees, branches, images, labels, params, momentum))


def solution(mesh):
    in_specs = (
        P(("node", "local"), None, None, None),
        P(("node", "local")),
        P("node", "local"),
        P("node", "local"),
        P(),
    )
    out_specs = (P("node", "local"), P("node", "local"))
    return jax.shard_map(body, mesh=mesh, in_specs=in_specs, out_specs=out_specs, check_vma=False)
```
